32 devices in a mesh: dp: 2 (over core), ctx: 4 (over y, x), shard: 4 (over z).
Axes of the slice: x: 2, y: 2, z: 4, core: 2. Of those that a mesh axis runs over, the one named last changes fastest.
Arguments:
- tokens: bfloat16 [8, 512, 1536], P(('dp', 'shard'), 'ctx'), may hold values from -6 to 6
- cotangent: bfloat16 [8, 512, 1536], P(('dp', 'shard'), 'ctx'), may hold values from -6 to 6
- positions: int32 [8, 512], P(('dp', 'shard'), 'ctx'), may hold values from 0 to 511, as said below
- w_qkv: float32 [2, 1536, 3072], P(None, ('ctx', 'shard')), may hold values from -0.15625 to 0.15625
- w_out: float32 [2, 1536, 1536], P(None, ('ctx', 'shard')), may hold values from -2.5 to 2.5
- w_gate_up: float32 [2, 1536, 8192], P(None, ('ctx', 'shard')), may hold values from -0.15625 to 0.15625
- w_down: float32 [2, 4096, 1536], P(None, ('ctx', 'shard')), may hold values from -0.09375 to 0.09375
- norm_gains: float32 [2, 2, 1536], P(None, None, ('ctx', 'shard')), may hold values from 0.5 to 1.5
- first_qkv: float32 [2, 1536, 3072], P(None, ('ctx', 'shard')), as said below
- first_out: float32 [2, 1536, 1536], P(None, ('ctx', 'shard')), as said below
- first_gate_up: float32 [2, 1536, 8192], P(None, ('ctx', 'shard')), as said below
- first_down: float32 [2, 4096, 1536], P(None, ('ctx', 'shard')), as said below
- first_gains: float32 [2, 2, 1536], P(None, None, ('ctx', 'shard')), as said below
- second_qkv: float32 [2, 1536, 3072], P(None, ('ctx', 'shard')), as said below
- second_out: float32 [2, 1536, 1536], P(None, ('ctx', 'shard')), as said below
- second_gate_up: float32 [2, 1536, 8192], P(None, ('ctx', 'shard')), as said below
- second_down: float32 [2, 4096, 1536], P(None, ('ctx', 'shard')), as said below
- second_gains: float32 [2, 2, 1536], P(None, None, ('ctx', 'shard')), as said below
Outputs:
- output: bfloat16 [8, 512, 1536], P(('dp', 'shard'), 'ctx')
- input_grad: float32 [8, 512, 1536], P(('dp', 'shard'), 'ctx')
- new_qkv: float32 [2, 1536, 3072], P(None, ('ctx', 'shard'))
- new_out: float32 [2, 1536, 1536], P(None, ('ctx', 'shard'))
- new_gate_up: float32 [2, 1536, 8192], P(None, ('ctx', 'shard'))
- new_down: float32 [2, 4096, 1536], P(None, ('ctx', 'shard'))
- new_gains: float32 [2, 2, 1536], P(None, None, ('ctx', 'shard'))
- moment_qkv: float32 [2, 1536, 3072], P(None, ('ctx', 'shard'))
- moment_out: float32 [2, 1536, 1536], P(None, ('ctx', 'shard'))
- moment_gate_up: float32 [2, 1536, 8192], P(None, ('ctx', 'shard'))
- moment_down: float32 [2, 4096, 1536], P(None, ('ctx', 'shard'))
- moment_gains: float32 [2, 2, 1536], P(None, None, ('ctx', 'shard'))
- square_qkv: float32 [2, 1536, 3072], P(None, ('ctx', 'shard'))
- square_out: float32 [2, 1536, 1536], P(None, ('ctx', 'shard'))
- square_gate_up: float32 [2, 1536, 8192], P(None, ('ctx', 'shard'))
- square_down: float32 [2, 4096, 1536], P(None, ('ctx', 'shard'))
- square_gains: float32 [2, 2, 1536], P(None, None, ('ctx', 'shard'))
The draws below stay inside these ranges and needn't reach their ends.
Inputs may be any that keep to these rules, and one draw needn't show every extreme that they name: Within each sequence the positions are a permutation of all 512; cut into 8 runs of 64 stored tokens, each run holds 64 consecutive positions starting at a multiple of 64, and runs 2 i and 2 i + 1 hold blocks b and 7 - b in either order. `first_qkv`: entries of both signs. `first_out`: entries of both signs. `first_gate_up`: entries of both signs. `first_down`: entries of both signs. `first_gains`: entries of both signs. `second_qkv`: entries positive. `second_out`: entries positive. `second_gate_up`: entries positive. `second_down`: entries positive. `second_gains`: entries positive.
All inputs are finite; a program needn't handle non-finite values.
Results may differ from the reference program's by a relative error of at most 0.025.
Values may be sent and summed in bfloat16 or wider, within the bound.
A program may use at most 640 MiB of HBM per device.

```python
import jax
import jax.numpy as jnp
from jax import lax

D = 1536
HEADS = 16
KV_HEADS = 8
HEAD_DIM = 96
FF = 4096
LAYERS = 2
STEP = 10
BLOCK_TOK = 64
SEQ_LEN = 512
SEQS = 8
TOKENS = 4096
QKV = 3072
N_CTX = 4


def grad_size(factor):
    return factor * jnp.sqrt(jnp.float32(TOKENS))


def first_moment(key, shape, size):
    return 0.1 / 0.9 * size * jax.random.normal(key, shape, jnp.float32)


def second_moment(key, shape, size):
    spread = jnp.exp(jax.random.uniform(key, shape, jnp.float32, jnp.log(0.5), jnp.log(2.0)))
    return 2.0 * (0.05 / 0.95) * size * size * spread


def out_size():
    return jnp.sqrt(jnp.float32(2.0 * TOKENS / SEQ_LEN))


def draw_positions(key, part):
    key = jax.random.fold_in(key, 11)

    def one_sequence(seq_key):
        order_key, flip_key = jax.random.split(seq_key)
        pair_order = jax.random.permutation(order_key, N_CTX).astype(jnp.int32)
        flip_bits = jax.random.randint(flip_key, (N_CTX,), 0, 2)
        high_block = 2 * N_CTX - 1 - pair_order
        first_block = jnp.where(flip_bits == 1, high_block, pair_order)
        second_block = jnp.where(flip_bits == 1, pair_order, high_block)
        blocks = jnp.stack([first_block, second_block], axis=1).reshape(2 * N_CTX)
        offsets = jnp.arange(BLOCK_TOK, dtype=jnp.int32)
        return (blocks[:, None] * BLOCK_TOK + offsets[None, :]).reshape(SEQ_LEN)
    return jax.vmap(one_sequence)(jax.random.split(key, SEQS)).astype(jnp.int32)


def draw_first_qkv(key, part):
    key = jax.random.fold_in(key, 21)
    return first_moment(key, (LAYERS, D, QKV), grad_size(2.0))


def draw_first_out(key, part):
    key = jax.random.fold_in(key, 22)
    return first_moment(key, (LAYERS, D, D), out_size())


def draw_first_gate_up(key, part):
    key = jax.random.fold_in(key, 23)
    return first_moment(key, (LAYERS, D, 2 * FF), grad_size(0.6))


def draw_first_down(key, part):
    key = jax.random.fold_in(key, 24)
    return first_moment(key, (LAYERS, FF, D), grad_size(0.6))


def draw_first_gains(key, part):
    key = jax.random.fold_in(key, 25)
    return first_moment(key, (LAYERS, 2, D), grad_size(1.0))


def draw_second_qkv(key, part):
    key = jax.random.fold_in(key, 31)
    return second_moment(key, (LAYERS, D, QKV), grad_size(2.0))


def draw_second_out(key, part):
    key = jax.random.fold_in(key, 32)
    return second_moment(key, (LAYERS, D, D), out_size())


def draw_second_gate_up(key, part):
    key = jax.random.fold_in(key, 33)
    return second_moment(key, (LAYERS, D, 2 * FF), grad_size(0.6))


def draw_second_down(key, part):
    key = jax.random.fold_in(key, 34)
    return second_moment(key, (LAYERS, FF, D), grad_size(0.6))


def draw_second_gains(key, part):
    key = jax.random.fold_in(key, 35)
    return second_moment(key, (LAYERS, 2, D), grad_size(1.0))


def levels(rng, shape, shards, least, largest):
    loudness, own = 1.0, jax.random.fold_in(rng, 6)
    for dim, shards_of in shards:
        steps = jnp.exp(jax.random.uniform(jax.random.fold_in(own, dim), (shards_of,), jnp.float32, least / len(shards), largest / len(shards)))
        loudness = loudness * jnp.repeat(steps, shape[dim] // shards_of).reshape([-1 if axis == dim else 1 for axis in range(len(shape))])
    return loudness


def scatter_about(rng, shape, width, reach, cuts=(), kind=jnp.bfloat16):
    level = levels(rng, shape, cuts, -0.22, 0.18) if cuts else 1.0
    values = jax.random.normal(rng, shape, jnp.float32) * width * level
    return jnp.minimum(jnp.maximum(values, -reach), reach).astype(kind)


def setup_inputs(seed: int = 0) -> dict:
    keys = jax.random.split(jax.random.key(seed), 19)
    return {
        "tokens": scatter_about(keys[0], (SEQS, SEQ_LEN, D), 1.0, 6.0, ((0, 8), (1, 4))),
        "cotangent": scatter_about(keys[1], (SEQS, SEQ_LEN, D), 1.0, 6.0, ((0, 8), (1, 4))),
        "positions": draw_positions(jax.random.fold_in(keys[18], 71), 0),
        "w_qkv": scatter_about(keys[3], (LAYERS, D, QKV), D ** -0.5, 0.15625, ((1, 16),), jnp.float32),
        "w_out": scatter_about(keys[4], (LAYERS, D, D), (max(1, 2 * D // SEQ_LEN)) ** -0.5, 2.5, ((1, 16),), jnp.float32),
        "w_gate_up": scatter_about(keys[5], (LAYERS, D, 2 * FF), D ** -0.5, 0.15625, ((1, 16),), jnp.float32),
        "w_down": scatter_about(keys[6], (LAYERS, FF, D), FF ** -0.5, 0.09375, ((1, 16),), jnp.float32),
        "norm_gains": jnp.clip(1.0 + 0.1 * jax.random.normal(keys[7], (LAYERS, 2, D), jnp.float32), 0.5, 1.5),
        "first_qkv": draw_first_qkv(jax.random.fold_in(keys[18], 71), 0),
        "first_out": draw_first_out(jax.random.fold_in(keys[18], 71), 0),
        "first_gate_up": draw_first_gate_up(jax.random.fold_in(keys[18], 71), 0),
        "first_down": draw_first_down(jax.random.fold_in(keys[18], 71), 0),
        "first_gains": draw_first_gains(jax.random.fold_in(keys[18], 71), 0),
        "second_qkv": draw_second_qkv(jax.random.fold_in(keys[18], 71), 0),
        "second_out": draw_second_out(jax.random.fold_in(keys[18], 71), 0),
        "second_gate_up": draw_second_gate_up(jax.random.fold_in(keys[18], 71), 0),
        "second_down": draw_second_down(jax.random.fold_in(keys[18], 71), 0),
        "second_gains": draw_second_gains(jax.random.fold_in(keys[18], 71), 0),
    }


@jax.custom_vjp
def low(v):
    return lax.optimization_barrier(v.astype(jnp.bfloat16)).astype(jnp.float32)

@jax.custom_vjp
def low_back(v):
    return v

def low_keep(v):
    return (low(v), None)

def low_pass(kept, grad):
    return (grad,)

def back_keep(v):
    return (v, None)

def back_low(kept, grad):
    return (low(grad),)
low.defvjp(low_keep, low_pass)
low_back.defvjp(back_keep, back_low)
NORM_EPS = 1e-05
ROPE_BASE = 100000.0
BETA_ONE = 0.9
BETA_TWO = 0.95
ADAM_EPS = 1e-08
DECAY_RATE = 0.1
RATES = (0.05, 1.0, 0.05, 0.03, 0.8)
DECAYS = (DECAY_RATE, DECAY_RATE, DECAY_RATE, DECAY_RATE, 0.0)

def hi_dot(left, right):
    return jnp.dot(left, right, precision=lax.Precision.HIGHEST, preferred_element_type=jnp.float32)

def rope_angles(positions):
    half_dim = HEAD_DIM // 2
    inverse_freq = jnp.exp(-jnp.log(ROPE_BASE) * (2.0 * jnp.arange(half_dim, dtype=jnp.float32) / HEAD_DIM))
    return positions.astype(jnp.float32)[:, None] * inverse_freq[None, :]

def rotate(values, angles):
    half_dim = values.shape[-1] // 2
    cosine = jnp.cos(angles)[:, None, :]
    sine_part = jnp.sin(angles)[:, None, :]
    first_half = values[..., :half_dim]
    second_half = values[..., half_dim:]
    return jnp.concatenate([first_half * cosine - second_half * sine_part, second_half * cosine + first_half * sine_part], axis=-1)

def rms_norm(stream, gain):
    return stream * lax.rsqrt(lax.optimization_barrier(jnp.mean(stream * stream, axis=-1, keepdims=True)) + NORM_EPS) * gain

def attention(query_rot, key_rot, value_rot, allowed):
    length = query_rot.shape[0]
    grouped = jnp.transpose(query_rot.reshape(length, KV_HEADS, HEADS // KV_HEADS, HEAD_DIM), (1, 0, 2, 3))
    keys_t = jnp.transpose(key_rot, (1, 0, 2))
    values_t = jnp.transpose(value_rot, (1, 0, 2))

    def one_head(operands):
        query_head, key_head, value_head = operands
        raw = jnp.einsum('tgd,sd->gts', query_head, key_head, precision=lax.Precision.HIGHEST) * HEAD_DIM ** (-0.5)
        raw = low_back(raw)
        masked = jnp.where(allowed[None], raw, -1000000000.0)
        row_top = lax.optimization_barrier(jnp.max(masked, axis=-1, keepdims=True))
        exp_terms = jnp.exp(masked - row_top)
        attn_probs = low(exp_terms / lax.optimization_barrier(jnp.sum(exp_terms, axis=-1, keepdims=True)))
        return jnp.einsum('gts,sd->tgd', attn_probs, value_head, precision=lax.Precision.HIGHEST)
    attended = lax.map(jax.checkpoint(one_head), (grouped, keys_t, values_t))
    return jnp.transpose(attended, (1, 0, 2, 3)).reshape(length, HEADS * HEAD_DIM)

def layer_forward(stream, angles, allowed, params):
    w_qkv, w_out, w_gate_up, w_down, gains = params
    width_q = HEADS * HEAD_DIM
    width_kv = KV_HEADS * HEAD_DIM
    length = stream.shape[0]
    normed = low(rms_norm(stream, low(gains[0])))
    projected = low_back(hi_dot(normed, low(w_qkv)))
    query_part = projected[:, :width_q].reshape(length, HEADS, HEAD_DIM)
    key_part = projected[:, width_q:width_q + width_kv].reshape(length, KV_HEADS, HEAD_DIM)
    value_part = projected[:, width_q + width_kv:].reshape(length, KV_HEADS, HEAD_DIM)
    attended = attention(low(rotate(query_part, angles)), low(rotate(key_part, angles)), low(value_part), allowed)
    attended = low_back(low(attended))
    middle = stream + low_back(hi_dot(attended, low(w_out)))
    normed_two = low(rms_norm(middle, low(gains[1])))
    gate_up = low_back(hi_dot(normed_two, low(w_gate_up)))
    hidden = low(jax.nn.silu(gate_up[:, :FF]) * gate_up[:, FF:])
    return middle + low_back(hi_dot(hidden, low(w_down)))

def forward(stream, params, positions):
    angles = rope_angles(positions)
    allowed = positions[None, :] <= positions[:, None]
    for layer_index in range(LAYERS):
        stream = layer_forward(stream, angles, allowed, tuple((item[layer_index] for item in params)))
    return stream

def adam_step(weight, moment, square, grad, rate, decay):
    moment = BETA_ONE * moment + (1.0 - BETA_ONE) * grad
    square = BETA_TWO * square + (1.0 - BETA_TWO) * grad * grad
    moment_hat = moment / (1.0 - BETA_ONE ** STEP)
    square_hat = square / (1.0 - BETA_TWO ** STEP)
    weight = weight - rate * (moment_hat / (jnp.sqrt(square_hat) + ADAM_EPS) + decay * weight)
    return (weight, moment, square)

def reference(tokens, cotangent, positions, w_qkv, w_out, w_gate_up, w_down, norm_gains, first_qkv, first_out, first_gate_up, first_down, first_gains, second_qkv, second_out, second_gate_up, second_down, second_gains):
    params = (w_qkv, w_out, w_gate_up, w_down, norm_gains)

    def per_sequence(totals, item):
        sequence, seq_grad, seq_pos = item

        def run(stream, weights):
            return forward(stream, weights, seq_pos)
        result, pull = jax.vjp(run, sequence.astype(jnp.float32), params)
        grad_in, grad_params = pull(seq_grad.astype(jnp.float32))
        totals = jax.tree.map(lambda left, right: left + right, totals, grad_params)
        return (totals, (result.astype(jnp.bfloat16), grad_in))
    zeros = jax.tree.map(jnp.zeros_like, params)
    grads, (outputs, input_grads) = lax.scan(per_sequence, zeros, (tokens, cotangent, positions))
    firsts = (first_qkv, first_out, first_gate_up, first_down, first_gains)
    seconds = (second_qkv, second_out, second_gate_up, second_down, second_gains)
    updated = [adam_step(params[slot], firsts[slot], seconds[slot], grads[slot], RATES[slot], DECAYS[slot]) for slot in range(5)]
    return (outputs, input_grads, updated[0][0], updated[1][0], updated[2][0], updated[3][0], updated[4][0], updated[0][1], updated[1][1], updated[2][1], updated[3][1], updated[4][1], updated[0][2], updated[1][2], updated[2][2], updated[3][2], updated[4][2])
```

```python
import jax
import jax.numpy as jnp
from jax import lax
from jax.sharding import PartitionSpec as P

HEADS = 16
KV_HEADS = 8
HEAD_DIM = 96
FF = 4096
STEP = 10


NORM_EPS = 1e-05
ROPE_BASE = 100000.0
BETA_ONE = 0.9
BETA_TWO = 0.95
ADAM_EPS = 1e-08
DECAY_RATE = 0.1
RATES = (0.05, 1.0, 0.05, 0.03, 0.8)
DECAYS = (DECAY_RATE, DECAY_RATE, DECAY_RATE, DECAY_RATE, 0.0)

BF = jnp.bfloat16
F32 = jnp.float32


def dot(left, right, dims=((1,), (0,))):
    return lax.dot_general(left, right, (dims, ((), ())), preferred_element_type=F32)


def rope_angles(positions):
    half_dim = HEAD_DIM // 2
    inverse_freq = jnp.exp(
        -jnp.log(ROPE_BASE) * (2.0 * jnp.arange(half_dim, dtype=jnp.float32) / HEAD_DIM)
    )
    return positions.astype(jnp.float32)[:, None] * inverse_freq[None, :]


def rotate(values, cosine, sine):
    half_dim = values.shape[-1] // 2
    first_half = values[..., :half_dim]
    second_half = values[..., half_dim:]
    cosine = cosine[:, None, :]
    sine = sine[:, None, :]
    return jnp.concatenate(
        [
            first_half * cosine - second_half * sine,
            second_half * cosine + first_half * sine,
        ],
        axis=-1,
    )


def norm_forward(stream, gain):
    inverse = lax.rsqrt(jnp.mean(stream * stream, axis=-1, keepdims=True) + NORM_EPS)
    return (stream * inverse * gain).astype(BF)


def norm_backward(grad_out, gain, stream):
    inverse = lax.rsqrt(jnp.mean(stream * stream, axis=-1, keepdims=True) + NORM_EPS)
    normal_part = stream * inverse
    scaled = grad_out * gain
    gain_grad = jnp.sum(grad_out * normal_part, axis=0)
    grad_in = inverse * (
        scaled - normal_part * jnp.mean(scaled * normal_part, axis=-1, keepdims=True)
    )
    return (grad_in, gain_grad)


def adam_step(weight, moment, square, grad, rate, decay):
    moment = BETA_ONE * moment + (1.0 - BETA_ONE) * grad
    square = BETA_TWO * square + (1.0 - BETA_TWO) * grad * grad
    moment_hat = moment / (1.0 - BETA_ONE**STEP)
    square_hat = square / (1.0 - BETA_TWO**STEP)
    weight = weight - rate * (moment_hat / (jnp.sqrt(square_hat) + ADAM_EPS) + decay * weight)
    return (weight, moment, square)


def gather_ctx(block):
    return lax.all_gather(block, "ctx", axis=0, tiled=True)


def scatter_ctx(partial):
    return lax.psum_scatter(partial.astype(BF), "ctx", scatter_dimension=0, tiled=True).astype(F32)


def half_rows(shard):
    half = shard.shape[0] // 2
    return lax.dynamic_slice_in_dim(shard, lax.axis_index("dp") * half, half, axis=0)


def gather_columns(shard, pieces):
    ctx = lax.axis_size("ctx")
    mine = half_rows(shard).astype(BF)
    rows = mine.shape[0]
    cut, start = [], 0
    for width in pieces:
        cut.append(mine[:, start : start + width].reshape(rows, ctx, width // ctx))
        start += width
    parts = jnp.transpose(jnp.concatenate(cut, axis=2), (1, 0, 2))
    parts = lax.all_to_all(parts, "ctx", 0, 0, tiled=True)
    whole = lax.all_gather(parts[:, None], ("shard", "dp"), axis=1, tiled=True)
    return whole.reshape(-1, whole.shape[-1])


def gather_rows(shard):
    return lax.all_gather(half_rows(shard).astype(BF), ("shard", "dp"), axis=0, tiled=True)


def scatter_columns(grad, pieces):
    ctx, shards = lax.axis_size("ctx"), lax.axis_size("shard")
    columns = grad.shape[1]
    rows = grad.shape[0] // (ctx * shards * 2)
    parts = grad.astype(BF).reshape(ctx, shards * 2, rows, columns)
    parts = jnp.transpose(parts, (1, 0, 2, 3)).reshape(-1, columns)
    mine = lax.psum_scatter(parts, ("shard", "dp"), scatter_dimension=0, tiled=True)
    mine = mine.reshape(ctx, rows, columns)
    mine = lax.all_to_all(mine, "ctx", 0, 0, tiled=True)
    mine = lax.all_gather(mine, "dp", axis=1, tiled=True)
    out, start = [], 0
    for width in pieces:
        piece = mine[:, :, start : start + width // ctx]
        out.append(jnp.transpose(piece, (1, 0, 2)).reshape(2 * rows, width))
        start += width // ctx
    return jnp.concatenate(out, axis=1).astype(F32)


def scatter_rows(grad):
    mine = lax.psum_scatter(grad.astype(BF), ("shard", "dp"), scatter_dimension=0, tiled=True)
    return lax.all_gather(mine, "dp", axis=0, tiled=True).astype(F32)


def head_scores(query_head, key_head, allowed):
    raw = jnp.einsum(
        "tgd,sd->gts", query_head, key_head, preferred_element_type=jnp.float32
    ) * HEAD_DIM ** (-0.5)
    return jnp.where(allowed[None], raw, -1000000000.0)


def attn_forward(stream, gain, w_qkv, w_out, cosine, sine, allowed):
    normed = gather_ctx(norm_forward(stream, gain))
    rows = normed.shape[0]
    kv_heads = w_qkv.shape[1] // (4 * HEAD_DIM)
    width_q, width_kv = 2 * kv_heads * HEAD_DIM, kv_heads * HEAD_DIM
    projected = dot(normed, w_qkv)
    query = rotate(
        projected[:, :width_q].reshape(rows, 2 * kv_heads, HEAD_DIM), cosine, sine
    ).astype(BF)
    key = rotate(
        projected[:, width_q : width_q + width_kv].reshape(rows, kv_heads, HEAD_DIM), cosine, sine
    ).astype(BF)
    value = projected[:, width_q + width_kv :].astype(BF)
    keys_t = jnp.transpose(key, (1, 0, 2))
    values_t = jnp.transpose(value.reshape(rows, kv_heads, HEAD_DIM), (1, 0, 2))
    query_t = jnp.transpose(query.reshape(rows, kv_heads, 2, HEAD_DIM), (1, 0, 2, 3))

    def head_forward(operands):
        query_head, key_head, value_head = operands
        masked = head_scores(query_head, key_head, allowed)
        row_top = jnp.max(masked, axis=-1, keepdims=True)
        exp_terms = jnp.exp(masked - row_top)
        row_total = jnp.sum(exp_terms, axis=-1, keepdims=True)
        attn_probs = exp_terms / row_total
        mixed_head = jnp.einsum(
            "gts,sd->tgd", attn_probs.astype(BF), value_head, preferred_element_type=F32
        )
        return (mixed_head, row_top, row_total)

    mixed, row_top, row_total = lax.map(head_forward, (query_t, keys_t, values_t))
    attended = jnp.transpose(mixed, (1, 0, 2, 3)).reshape(rows, width_q).astype(BF)
    middle = stream + scatter_ctx(dot(attended, w_out))
    return middle, (normed, query_t, keys_t, values_t, row_top, row_total, attended)


def attn_backward(grad_stream, stream, gain, w_qkv, w_out, cosine, sine, allowed, saved):
    normed, query_t, keys_t, values_t, row_top, row_total, attended = saved
    rows = normed.shape[0]
    kv_heads = w_qkv.shape[1] // (4 * HEAD_DIM)
    width_q, width_kv = 2 * kv_heads * HEAD_DIM, kv_heads * HEAD_DIM
    grad_attn = gather_ctx(grad_stream.astype(BF))
    grad_out_w = dot(attended, grad_attn, ((0,), (0,)))
    grad_mixed = dot(grad_attn, w_out, ((1,), (1,))).astype(BF)
    grad_t = jnp.transpose(grad_mixed.reshape(rows, kv_heads, 2, HEAD_DIM), (1, 0, 2, 3))

    def head_backward(operands):
        query_head, key_head, value_head, grad_head, row_top, row_total = operands
        masked = head_scores(query_head, key_head, allowed)
        attn_probs = jnp.exp(masked - row_top) / row_total
        grad_probs = jnp.einsum(
            "tgd,sd->gts", grad_head, value_head, preferred_element_type=jnp.float32
        )
        inner = jnp.sum(attn_probs * grad_probs, axis=-1, keepdims=True)
        grad_scores = (attn_probs * (grad_probs - inner)).astype(BF)
        grad_query = jnp.einsum(
            "gts,sd->tgd", grad_scores, key_head, preferred_element_type=jnp.float32
        ) * HEAD_DIM ** (-0.5)
        grad_key = jnp.einsum(
            "gts,tgd->sd", grad_scores, query_head, preferred_element_type=jnp.float32
        ) * HEAD_DIM ** (-0.5)
        grad_value = jnp.einsum(
            "gts,tgd->sd", attn_probs.astype(BF), grad_head, preferred_element_type=jnp.float32
        )
        return (grad_query, grad_key, grad_value)

    grad_query, grad_key, grad_value = lax.map(
        head_backward, (query_t, keys_t, values_t, grad_t, row_top, row_total)
    )
    grad_query = jnp.transpose(grad_query, (1, 0, 2, 3)).reshape(rows, 2 * kv_heads, HEAD_DIM)
    grad_projected = jnp.concatenate(
        [
            rotate(grad_query, cosine, -sine).reshape(rows, width_q),
            rotate(jnp.transpose(grad_key, (1, 0, 2)), cosine, -sine).reshape(rows, width_kv),
            jnp.transpose(grad_value, (1, 0, 2)).reshape(rows, width_kv),
        ],
        axis=1,
    ).astype(BF)
    grad_normed = scatter_ctx(dot(grad_projected, w_qkv, ((1,), (1,))))
    grad_wqkv = dot(normed, grad_projected, ((0,), (0,)))
    grad_in, grad_gain = norm_backward(grad_normed, gain, stream)
    return grad_stream + grad_in, grad_wqkv, grad_out_w, grad_gain


def mlp_forward(middle, gain, w_gate_up, w_down):
    normed = gather_ctx(norm_forward(middle, gain))
    gate_up = dot(normed, w_gate_up)
    width = gate_up.shape[1] // 2
    gate, up = gate_up[:, :width], gate_up[:, width:]
    hidden = (jax.nn.silu(gate) * up).astype(BF)
    return middle + scatter_ctx(dot(hidden, w_down)), (normed, gate, up, hidden)


def mlp_backward(grad_stream, middle, gain, w_gate_up, w_down, saved):
    normed, gate, up, hidden = saved
    grad_mlp = gather_ctx(grad_stream.astype(BF))
    grad_hidden = dot(grad_mlp, w_down, ((1,), (1,)))
    sigmoid_gate = jax.nn.sigmoid(gate)
    grad_gate = grad_hidden * up * sigmoid_gate * (1.0 + gate * (1.0 - sigmoid_gate))
    grad_up = grad_hidden * jax.nn.silu(gate)
    grad_gate_up = jnp.concatenate([grad_gate, grad_up], axis=1).astype(BF)
    grad_normed = scatter_ctx(dot(grad_gate_up, w_gate_up, ((1,), (1,))))
    grad_down = dot(hidden, grad_mlp, ((0,), (0,)))
    grad_wgu = dot(normed, grad_gate_up, ((0,), (0,)))
    grad_in, grad_gain = norm_backward(grad_normed, gain, middle)
    return grad_stream + grad_in, grad_wgu, grad_down, grad_gain


def body(
    tokens,
    cotangent,
    positions,
    w_qkv,
    w_out,
    w_gate_up,
    w_down,
    norm_gains,
    first_qkv,
    first_out,
    first_gate_up,
    first_down,
    first_gains,
    second_qkv,
    second_out,
    second_gate_up,
    second_down,
    second_gains,
):
    stream = tokens[0].astype(F32)
    layer_count = w_qkv.shape[0]
    width_q, width_kv = HEADS * HEAD_DIM, KV_HEADS * HEAD_DIM
    qkv_pieces, gate_pieces = (width_q, width_kv, width_kv), (FF, FF)
    seq_pos = gather_ctx(positions[0])
    angles = rope_angles(seq_pos)
    cosine, sine = jnp.cos(angles), jnp.sin(angles)
    allowed = seq_pos[None, :] <= seq_pos[:, None]
    gains = lax.all_gather(norm_gains.astype(BF), ("ctx", "shard"), axis=2, tiled=True).astype(F32)

    weights, saved = [], []
    for layer in range(layer_count):
        wq = gather_columns(w_qkv[layer], qkv_pieces)
        wo = gather_rows(w_out[layer])
        wgu = gather_columns(w_gate_up[layer], gate_pieces)
        wd = gather_rows(w_down[layer])
        weights.append((wq, wo, wgu, wd))
        middle, kept_attn = attn_forward(stream, gains[layer, 0], wq, wo, cosine, sine, allowed)
        after, kept_mlp = mlp_forward(middle, gains[layer, 1], wgu, wd)
        saved.append((stream, middle, kept_attn, kept_mlp))
        stream = after
    output = stream.astype(BF)

    grads = [None] * layer_count
    gain_grads = [None] * layer_count
    grad_stream = cotangent[0].astype(F32)
    for layer in reversed(range(layer_count)):
        wq, wo, wgu, wd = weights[layer]
        before, middle, kept_attn, kept_mlp = saved[layer]
        grad_stream, grad_wgu, grad_wd, grad_g2 = mlp_backward(
            grad_stream, middle, gains[layer, 1], wgu, wd, kept_mlp
        )
        grad_wgu, grad_wd = scatter_columns(grad_wgu, gate_pieces), scatter_rows(grad_wd)
        grad_stream, grad_wq, grad_wo, grad_g1 = attn_backward(
            grad_stream, before, gains[layer, 0], wq, wo, cosine, sine, allowed, kept_attn
        )
        grad_wq, grad_wo = scatter_columns(grad_wq, qkv_pieces), scatter_rows(grad_wo)
        grads[layer] = (grad_wq, grad_wo, grad_wgu, grad_wd)
        gain_grads[layer] = jnp.stack([grad_g1, grad_g2])
    gain_grad = lax.psum(
        lax.psum_scatter(
            jnp.stack(gain_grads), ("ctx", "shard"), scatter_dimension=2, tiled=True
        ),
        "dp",
    )
    grad_list = [jnp.stack([grads[layer][slot] for layer in range(layer_count)]) for slot in range(4)]
    grad_list.append(gain_grad)
    params = (w_qkv, w_out, w_gate_up, w_down, norm_gains)
    firsts = (first_qkv, first_out, first_gate_up, first_down, first_gains)
    seconds = (second_qkv, second_out, second_gate_up, second_down, second_gains)
    updated = [
        adam_step(params[slot], firsts[slot], seconds[slot], grad_list[slot], RATES[slot], DECAYS[slot])
        for slot in range(5)
    ]
    return (
        output[None],
        grad_stream[None],
        *[updated[slot][0] for slot in range(5)],
        *[updated[slot][1] for slot in range(5)],
        *[updated[slot][2] for slot in range(5)],
    )


def solution(mesh):
    rows = P(("dp", "shard"), "ctx", None)
    weight = P(None, ("ctx", "shard"), None)
    gain = P(None, None, ("ctx", "shard"))
    group = (weight, weight, weight, weight, gain)
    return jax.shard_map(
        body,
        mesh=mesh,
        in_specs=(rows, rows, P(("dp", "shard"), "ctx"), *group, *group, *group),
        out_specs=(rows, rows, *group, *group, *group),
        check_vma=False,
    )
```

```python
import functools
import math

import jax
import jax.numpy as jnp
from jax import lax
from jax.experimental import pallas as pl
from jax.experimental.pallas import tpu as pltpu
from jax.sharding import PartitionSpec as P

HEADS = 16
KV_HEADS = 8
HEAD_DIM = 96
FF = 4096
STEP = 10


NORM_EPS = 1e-05
ROPE_BASE = 100000.0
BETA_ONE = 0.9
BETA_TWO = 0.95
ADAM_EPS = 1e-08
DECAY_RATE = 0.1
RATES = (0.05, 1.0, 0.05, 0.03, 0.8)
DECAYS = (DECAY_RATE, DECAY_RATE, DECAY_RATE, DECAY_RATE, 0.0)

BF = jnp.bfloat16
F32 = jnp.float32


def dot(left, right, dims=((1,), (0,))):
    return lax.dot_general(left, right, (dims, ((), ())), preferred_element_type=F32)


def rope_angles(positions):
    half_dim = HEAD_DIM // 2
    inverse_freq = jnp.exp(
        -jnp.log(ROPE_BASE) * (2.0 * jnp.arange(half_dim, dtype=jnp.float32) / HEAD_DIM)
    )
    return positions.astype(jnp.float32)[:, None] * inverse_freq[None, :]


def rotate(values, cosine, sine):
    half_dim = values.shape[-1] // 2
    first_half = values[..., :half_dim]
    second_half = values[..., half_dim:]
    cosine = cosine[:, None, :]
    sine = sine[:, None, :]
    return jnp.concatenate(
        [
            first_half * cosine - second_half * sine,
            second_half * cosine + first_half * sine,
        ],
        axis=-1,
    )


def norm_forward(stream, gain):
    inverse = lax.rsqrt(jnp.mean(stream * stream, axis=-1, keepdims=True) + NORM_EPS)
    return (stream * inverse * gain).astype(BF)


def norm_backward(grad_out, gain, stream):
    inverse = lax.rsqrt(jnp.mean(stream * stream, axis=-1, keepdims=True) + NORM_EPS)
    normal_part = stream * inverse
    scaled = grad_out * gain
    gain_grad = jnp.sum(grad_out * normal_part, axis=0)
    grad_in = inverse * (
        scaled - normal_part * jnp.mean(scaled * normal_part, axis=-1, keepdims=True)
    )
    return (grad_in, gain_grad)


def adam_step(weight, moment, square, grad, rate, decay):
    moment = BETA_ONE * moment + (1.0 - BETA_ONE) * grad
    square = BETA_TWO * square + (1.0 - BETA_TWO) * grad * grad
    moment_hat = moment * (rate / (1.0 - BETA_ONE**STEP))
    square_hat = square * (1.0 / (1.0 - BETA_TWO**STEP))
    weight = weight * (1.0 - rate * decay) - moment_hat / (jnp.sqrt(square_hat) + ADAM_EPS)
    return (weight, moment, square)


MESH = pl.DeviceIdType.MESH
VMEM_LIMIT = 48 * 1024 * 1024


def remote(src, dst, sems, slot, target):
    send, recv = sems
    return pltpu.make_async_remote_copy(
        src_ref=src,
        dst_ref=dst,
        send_sem=send.at[slot],
        recv_sem=recv.at[slot],
        device_id=target,
        device_id_type=MESH,
    )


def greet(targets):
    barrier = pltpu.get_barrier_semaphore()
    for target in targets:
        pl.semaphore_signal(barrier, inc=1, device_id=target, device_id_type=MESH)
    pl.semaphore_wait(barrier, len(targets))


def ctx_peers(ctx):
    me = lax.axis_index("ctx")
    return [{"ctx": lax.rem(me + step, ctx)} for step in range(1, ctx)]


def square():
    me = lax.axis_index("ctx")
    x, y = lax.rem(me, 2), me // 2
    return me, 2 * y + 1 - x, 2 * (1 - y) + x, 3 - me


def gather_kernel(ctx, x_ref, o_ref, send, recv):
    rows = x_ref.shape[0]
    sems = (send, recv)

    def block(owner, part=None):
        if part is None:
            return pl.ds(pl.multiple_of(owner * rows, rows), rows)
        return pl.ds(pl.multiple_of(owner * rows + part * (rows // 2), rows // 2), rows // 2)

    if ctx != 4:
        me = lax.axis_index("ctx")
        peers = ctx_peers(ctx)
        greet(peers)
        copies = [remote(x_ref, o_ref.at[block(me)], sems, i, peer) for i, peer in enumerate(peers)]
        for copy in copies:
            copy.start()
        o_ref[block(me), :] = x_ref[...]
        for copy in copies:
            copy.wait()
        return
    me, xn, yn, _ = square()
    to_x, to_y = {"ctx": xn}, {"ctx": yn}
    greet((to_x, to_y))
    half = rows // 2
    low, high = pl.ds(0, half), pl.ds(half, half)
    first = remote(x_ref.at[low], o_ref.at[block(me, 0)], sems, 0, to_x)
    second = remote(x_ref.at[high], o_ref.at[block(me, 1)], sems, 1, to_y)
    third = remote(x_ref.at[high], o_ref.at[block(me, 1)], sems, 2, to_x)
    fourth = remote(x_ref.at[low], o_ref.at[block(me, 0)], sems, 3, to_y)
    first.start()
    second.start()
    third.start()
    fourth.start()
    o_ref[block(me), :] = x_ref[...]
    first.wait_recv()
    fifth = remote(o_ref.at[block(xn, 0)], o_ref.at[block(xn, 0)], sems, 4, to_y)
    fifth.start()
    second.wait_recv()
    sixth = remote(o_ref.at[block(yn, 1)], o_ref.at[block(yn, 1)], sems, 5, to_x)
    sixth.start()
    first.wait_send()
    second.wait_send()
    third.wait()
    fourth.wait()
    fifth.wait()
    sixth.wait()


def scatter_steps(ctx, p_ref, base_ref, o_ref, relay, mixed, landed, send, recv):
    rows = o_ref.shape[0]
    sems = (send, recv)

    def block(owner, part=None):
        if part is None:
            return pl.ds(pl.multiple_of(owner * rows, rows), rows)
        return pl.ds(pl.multiple_of(owner * rows + part * (rows // 2), rows // 2), rows // 2)

    if ctx != 4:
        me = lax.axis_index("ctx")
        peers = ctx_peers(ctx)
        greet(peers)
        copies = [
            remote(p_ref.at[block(peer["ctx"])], landed.at[i], sems, i, peer)
            for i, peer in enumerate(peers)
        ]
        for copy in copies:
            copy.start()
        yield
        yield
        total = base_ref[...] + p_ref[block(me), :].astype(F32)
        for i, copy in enumerate(copies):
            copy.wait()
            total = total + landed[i].astype(F32)
        o_ref[...] = total.astype(o_ref.dtype)
        return
    me, xn, yn, far = square()
    to_x, to_y = {"ctx": xn}, {"ctx": yn}
    greet((to_x, to_y))
    half = rows // 2
    low, high = pl.ds(0, half), pl.ds(half, half)
    first = remote(p_ref.at[block(far, 0)], relay.at[0], sems, 0, to_x)
    second = remote(p_ref.at[block(far, 1)], relay.at[1], sems, 1, to_y)
    third = remote(p_ref.at[block(xn, 0)], landed.at[0, low], sems, 2, to_x)
    fourth = remote(p_ref.at[block(yn, 1)], landed.at[1, high], sems, 3, to_y)
    first.start()
    second.start()
    third.start()
    fourth.start()
    yield
    first.wait_recv()
    mixed[0] = (relay[0].astype(F32) + p_ref[block(yn, 0), :].astype(F32)).astype(BF)
    fifth = remote(mixed.at[0], landed.at[1, low], sems, 4, to_y)
    fifth.start()
    second.wait_recv()
    mixed[1] = (relay[1].astype(F32) + p_ref[block(xn, 1), :].astype(F32)).astype(BF)
    sixth = remote(mixed.at[1], landed.at[0, high], sems, 5, to_x)
    sixth.start()
    yield
    first.wait_send()
    second.wait_send()
    third.wait()
    fourth.wait()
    fifth.wait()
    sixth.wait()
    o_ref[...] = (
        base_ref[...]
        + p_ref[block(me), :].astype(F32)
        + landed[0].astype(F32)
        + landed[1].astype(F32)
    ).astype(o_ref.dtype)


def scatter_kernel(*args):
    for _ in scatter_steps(*args):
        pass


def scatter_scratch(ctx, rows, columns):
    slots = 2 if ctx == 4 else ctx - 1
    return [
        pltpu.VMEM((2, rows // 2, columns), BF),
        pltpu.VMEM((2, rows // 2, columns), BF),
        pltpu.VMEM((slots, rows, columns), BF),
    ]


def swap_kernel(ctx, x_ref, o_ref, send, recv):
    me = lax.axis_index("ctx")
    peers = ctx_peers(ctx)
    greet(peers)
    copies = [
        remote(x_ref.at[peer["ctx"]], o_ref.at[me], (send, recv), i, peer)
        for i, peer in enumerate(peers)
    ]
    for copy in copies:
        copy.start()
    o_ref[me] = x_ref[me]
    for copy in copies:
        copy.wait()


def share_kernel(ctx, x_ref, y_ref, ox_ref, oy_ref, send, recv):
    me, core = lax.axis_index("ctx"), lax.axis_index("dp")
    peers, other = ctx_peers(ctx), {"dp": 1 - core}
    greet(peers + [other])
    sems = (send, recv)
    across = [
        remote(x_ref.at[peer["ctx"]], ox_ref.at[me, core], sems, i, peer)
        for i, peer in enumerate(peers)
    ]
    inside = [
        remote(x_ref.at[me], ox_ref.at[me, core], sems, ctx, other),
        remote(y_ref, oy_ref.at[core], sems, ctx + 1, other),
    ]
    for copy in across + inside:
        copy.start()
    ox_ref[me, core] = x_ref[me]
    oy_ref[core] = y_ref[...]
    for i, copy in enumerate(across):
        copy.wait_recv()
        source = lax.rem(me + ctx - 1 - i, ctx)
        chunk = ox_ref.at[source, core]
        inside.append(remote(chunk, chunk, sems, ctx + 2 + i, other))
        inside[-1].start()
    for copy in across:
        copy.wait_send()
    for copy in inside:
        copy.wait()


def call(kernel, out_shape, scratch, copies, collective_id, *args):
    return pl.pallas_call(
        kernel,
        out_shape=out_shape,
        in_specs=[pl.BlockSpec(memory_space=pltpu.VMEM)] * len(args),
        out_specs=jax.tree.map(lambda _: pl.BlockSpec(memory_space=pltpu.VMEM), out_shape),
        scratch_shapes=[
            *scratch,
            pltpu.SemaphoreType.DMA((copies,)),
            pltpu.SemaphoreType.DMA((copies,)),
        ],
        compiler_params=pltpu.CompilerParams(
            collective_id=collective_id, has_side_effects=True, vmem_limit_bytes=VMEM_LIMIT
        ),
    )(*args)


def shape_of(shape, dtype=BF):
    return jax.ShapeDtypeStruct(shape, dtype)


def gather_ctx(block):
    ctx = lax.axis_size("ctx")
    rows, columns = block.shape
    return call(
        functools.partial(gather_kernel, ctx), shape_of((ctx * rows, columns)), [], 8, 0, block
    )


def scatter_ctx(partial, base):
    ctx = lax.axis_size("ctx")
    rows, columns = base.shape
    return call(
        functools.partial(scatter_kernel, ctx),
        shape_of((rows, columns), F32),
        scatter_scratch(ctx, rows, columns),
        8,
        1,
        partial.astype(BF),
        base,
    )


def swap_ctx(parts, collective_id):
    ctx = lax.axis_size("ctx")
    return call(
        functools.partial(swap_kernel, ctx), shape_of(parts.shape), [], ctx, collective_id, parts
    )


def share_plane(parts, own, collective_id):
    ctx = lax.axis_size("ctx")
    return call(
        functools.partial(share_kernel, ctx),
        [shape_of((ctx, 2) + parts.shape[1:]), shape_of((2,) + own.shape)],
        [],
        2 * ctx + 1,
        collective_id,
        parts,
        own,
    )


def small_gather_kernel(ctx, shards, x_ref, o_ref, send, recv):
    me, mine = lax.axis_index("ctx"), lax.axis_index("shard")
    along = [{"shard": lax.rem(mine + step, shards)} for step in range(1, shards)]
    across = ctx_peers(ctx)
    greet(along + across)
    o_ref[me, mine] = x_ref[...]
    copies = [
        remote(x_ref, o_ref.at[me, mine], (send, recv), i, target)
        for i, target in enumerate(along)
    ]
    for copy in copies:
        copy.start()
    for copy in copies:
        copy.wait()
    copies = [
        remote(o_ref.at[me], o_ref.at[me], (send, recv), shards + i, target)
        for i, target in enumerate(across)
    ]
    for copy in copies:
        copy.start()
    for copy in copies:
        copy.wait()


def small_reduce_kernel(ctx, shards, x_ref, o_ref, first, column, second, third, send, recv):
    me, mine = lax.axis_index("ctx"), lax.axis_index("shard")
    along = [{"shard": lax.rem(mine + step, shards)} for step in range(1, shards)]
    across = ctx_peers(ctx)
    other = {"dp": 1 - lax.axis_index("dp")}
    greet(along + across + [other])
    sems = (send, recv)
    copies = [
        remote(x_ref.at[target["shard"]], first.at[i], sems, i, target)
        for i, target in enumerate(along)
    ]
    for copy in copies:
        copy.start()
    total = x_ref[mine]
    for i, copy in enumerate(copies):
        copy.wait()
        total = total + first[i]
    column[...] = total
    copies = [
        remote(column.at[target["ctx"]], second.at[i], sems, shards + i, target)
        for i, target in enumerate(across)
    ]
    for copy in copies:
        copy.start()
    total = column[me]
    for i, copy in enumerate(copies):
        copy.wait()
        total = total + second[i]
    third[0] = total
    copy = remote(third.at[0], third.at[1], sems, shards + ctx, other)
    copy.start()
    copy.wait()
    o_ref[...] = third[0] + third[1]


def small_gather(tile):
    ctx, shards = lax.axis_size("ctx"), lax.axis_size("shard")
    return call(
        functools.partial(small_gather_kernel, ctx, shards),
        shape_of((ctx, shards) + tile.shape, F32),
        [],
        ctx + shards + 1,
        6,
        tile,
    )


def small_reduce(tiles):
    shards, ctx = tiles.shape[:2]
    tile = tiles.shape[2:]
    return call(
        functools.partial(small_reduce_kernel, ctx, shards),
        shape_of(tile, F32),
        [
            pltpu.VMEM((shards - 1, ctx) + tile, F32),
            pltpu.VMEM((ctx,) + tile, F32),
            pltpu.VMEM((ctx - 1,) + tile, F32),
            pltpu.VMEM((2,) + tile, F32),
        ],
        ctx + shards + 1,
        7,
        tiles,
    )


def load_mlp(ctx, refs, wgu, wd, sems):
    if len(refs) == 2:
        wide = [pltpu.make_async_copy(refs[0], wgu, sems.at[0])]
        deep = [pltpu.make_async_copy(refs[1], wd, sems.at[1])]
        wide[0].start()
        deep[0].start()
        return wide, deep
    packed_ref = refs[0]
    groups, columns = packed_ref.shape[0], packed_ref.shape[2]
    rows = wgu.shape[0] // (ctx * groups)
    count, width = ctx * rows, wd.shape[1]
    rest = columns - width
    fold = width // rest
    below = packed_ref.shape[1] - count
    part = below // fold
    wide, deep = [], []
    for group in range(groups):
        for member in range(ctx):
            source = packed_ref.at[group, pl.ds(member * rows, rows)]
            target = wgu.at[pl.ds((member * groups + group) * rows, rows)]
            wide.append((source, target))
        start = group * (below + part)
        deep.append(
            (
                packed_ref.at[group, pl.ds(count, below), pl.ds(0, width)],
                wd.at[pl.ds(start, below)],
            )
        )
        for piece in range(fold):
            deep.append(
                (
                    packed_ref.at[group, pl.ds(count + piece * part, part), pl.ds(width, rest)],
                    wd.at[pl.ds(start + below, part), pl.ds(piece * rest, rest)],
                )
            )
    wide = [pltpu.make_async_copy(*pair, sems.at[i]) for i, pair in enumerate(wide)]
    deep = [pltpu.make_async_copy(*pair, sems.at[len(wide) + i]) for i, pair in enumerate(deep)]
    for copy in wide + deep:
        copy.start()
    return wide, deep


def store_gate_grad(ctx, normed_ref, grad_gu, refs):
    width = normed_ref.shape[1] // ctx
    if len(refs) == 2:
        for member in range(ctx):
            part = normed_ref[:, member * width : (member + 1) * width]
            refs[0][member * width : (member + 1) * width, :] = dot(
                part, grad_gu, ((0,), (0,))
            ).astype(BF)
        return
    packed_ref = refs[0]
    groups = packed_ref.shape[0]
    rows = width // groups
    for member in range(ctx):
        part = dot(normed_ref[:, member * width : (member + 1) * width], grad_gu, ((0,), (0,)))
        part = part.astype(BF)
        for group in range(groups):
            packed_ref[group, member * rows : (member + 1) * rows, :] = part[
                group * rows : (group + 1) * rows
            ]


def store_down_grad(ctx, hidden, grad_ref, refs):
    if len(refs) == 2:
        refs[1][...] = dot(hidden[...], grad_ref[...], ((0,), (0,))).astype(BF)
        return
    packed_ref = refs[0]
    groups, columns = packed_ref.shape[0], packed_ref.shape[2]
    width = grad_ref.shape[1]
    count = width // groups
    rest = columns - width
    fold = width // rest
    below = packed_ref.shape[1] - count
    part = below // fold
    rows = below + part
    for group in range(groups):
        block = dot(hidden[:, group * rows : (group + 1) * rows], grad_ref[...], ((0,), (0,)))
        block = block.astype(BF)
        packed_ref[group, count:, :width] = block[:below]
        for piece in range(fold):
            packed_ref[group, count + piece * part : count + (piece + 1) * part, width:] = block[
                below:, piece * rest : (piece + 1) * rest
            ]


def sigmoid(value):
    return 1.0 / (1.0 + jnp.exp(-value))


def mlp_forward_kernel(ctx, count, normed_ref, *refs):
    weights, (part_ref, gu_ref, wgu, wd, sems) = refs[:count], refs[count:]
    wide, deep = load_mlp(ctx, weights, wgu, wd, sems)
    for copy in wide:
        copy.wait()
    gu_ref[...] = dot(normed_ref[...], wgu[...])
    half = gu_ref.shape[1] // 2
    gate, up = gu_ref[:, :half], gu_ref[:, half:]
    hidden = (gate * sigmoid(gate) * up).astype(BF)
    for copy in deep:
        copy.wait()
    part_ref[...] = dot(hidden, wd[...]).astype(BF)


def gate_backward(gate, up, grad_hidden):
    sig = sigmoid(gate)
    silu = gate * sig
    grad_gate = grad_hidden * up * sig * (1.0 + gate * (1.0 - sig))
    return (silu * up).astype(BF), grad_gate.astype(BF), (grad_hidden * silu).astype(BF)


def mlp_backward_kernel(ctx, count, normed_ref, gu_ref, grad_ref, sum_ref, base_ref, *refs):
    weights, outs = refs[:count], refs[count : 2 * count]
    part_ref, sum_out, wgu, wd, dgu, hidden, sems, *sum_scratch = refs[2 * count :]
    wide, deep = load_mlp(ctx, weights, wgu, wd, sems)
    summed = scatter_steps(ctx, sum_ref, base_ref, sum_out, *sum_scratch)
    next(summed)
    for copy in deep:
        copy.wait()
    half = gu_ref.shape[1] // 2
    grad_hidden = dot(grad_ref[...], wd[...], ((1,), (1,)))
    hidden[...], dgu[:, :half], dgu[:, half:] = gate_backward(
        gu_ref[:, :half], gu_ref[:, half:], grad_hidden
    )
    next(summed)
    for copy in wide:
        copy.wait()
    part_ref[...] = dot(dgu[...], wgu[...], ((1,), (1,))).astype(BF)
    store_gate_grad(ctx, normed_ref, dgu[...], outs)
    store_down_grad(ctx, hidden, grad_ref, outs)
    for _ in summed:
        pass


def mlp_last_kernel(ctx, count, normed_ref, grad_ref, *refs):
    weights, outs = refs[:count], refs[count : 2 * count]
    hidden, dgu, wgu, wd, gu, sems = refs[2 * count :]
    wide, deep = load_mlp(ctx, weights, wgu, wd, sems)
    for copy in wide:
        copy.wait()
    gu[...] = dot(normed_ref[...], wgu[...])
    for copy in deep:
        copy.wait()
    half = gu.shape[1] // 2
    grad_hidden = dot(grad_ref[...], wd[...], ((1,), (1,)))
    hidden[...], dgu[:, :half], dgu[:, half:] = gate_backward(
        gu[:, :half], gu[:, half:], grad_hidden
    )
    store_gate_grad(ctx, normed_ref, dgu[...], outs)
    store_down_grad(ctx, hidden, grad_ref, outs)


def mlp_ends_kernel(ctx, count, hidden_ref, dgu_ref, *refs):
    weights, (up_ref, down_ref, wgu, wd, sems) = refs[:count], refs[count:]
    wide, deep = load_mlp(ctx, weights, wgu, wd, sems)
    for copy in wide:
        copy.wait()
    down_ref[...] = dot(dgu_ref[...], wgu[...], ((1,), (1,))).astype(BF)
    for copy in deep:
        copy.wait()
    up_ref[...] = dot(hidden_ref[...], wd[...]).astype(BF)


def local_call(kernel, out_shape, scratch, flops, hbm, *args):
    bytes_moved = sum(a.size * a.dtype.itemsize for a in args)
    bytes_moved += sum(a.size * a.dtype.itemsize for a in out_shape)
    spaces = [pl.ANY if hbm[0] <= i <= hbm[1] else pltpu.VMEM for i in range(len(args))]
    return pl.pallas_call(
        kernel,
        out_shape=out_shape,
        in_specs=[pl.BlockSpec(memory_space=space) for space in spaces],
        out_specs=[pl.BlockSpec(memory_space=pltpu.VMEM) for _ in out_shape],
        scratch_shapes=scratch,
        cost_estimate=pl.CostEstimate(flops=flops, bytes_accessed=bytes_moved, transcendentals=0),
        compiler_params=pltpu.CompilerParams(vmem_limit_bytes=VMEM_LIMIT),
    )(*args)


def mlp_weights(packed, width):
    ctx = lax.axis_size("ctx")
    groups, _, columns = packed.shape
    if columns > width and width // (ctx * groups) % 16 == 0:
        return (packed,)
    return spread(packed, width)


def mlp_scratch(weights, columns, width):
    ctx = lax.axis_size("ctx")
    copies = 2
    if len(weights) == 1:
        copies = weights[0].shape[0] * (ctx + 1 + width // (columns - width))
    return [
        pltpu.VMEM((width, columns), BF),
        pltpu.VMEM((columns // 2, width), BF),
    ], pltpu.SemaphoreType.DMA((copies,))


def mlp_forward_call(normed, weights):
    rows, width = normed.shape
    columns = weights[0].shape[-1]
    scratch, sems = mlp_scratch(weights, columns, width)
    return local_call(
        functools.partial(mlp_forward_kernel, lax.axis_size("ctx"), len(weights)),
        [shape_of((rows, width)), shape_of((rows, columns), F32)],
        [*scratch, sems],
        3 * rows * width * columns,
        (1, len(weights)),
        normed,
        *weights,
    )


def packed_grads(outs):
    return outs[0] if len(outs) == 1 else pack_grads(*outs)


def mlp_backward_call(normed, weights, gate_up, grad_mlp, summed, base):
    ctx = lax.axis_size("ctx")
    rows, width = normed.shape
    own = base.shape[0]
    columns = weights[0].shape[-1]
    scratch, sems = mlp_scratch(weights, columns, width)
    *outs, part, total = pl.pallas_call(
        functools.partial(mlp_backward_kernel, ctx, len(weights)),
        out_shape=[
            *[shape_of(weight.shape) for weight in weights],
            shape_of((rows, width)),
            shape_of((own, width)),
        ],
        in_specs=[pl.BlockSpec(memory_space=pltpu.VMEM)] * 5
        + [pl.BlockSpec(memory_space=pl.ANY)] * len(weights),
        out_specs=[pl.BlockSpec(memory_space=pltpu.VMEM)] * (2 + len(weights)),
        scratch_shapes=[
            *scratch,
            pltpu.VMEM((rows, columns), BF),
            pltpu.VMEM((rows, columns // 2), BF),
            sems,
            *scatter_scratch(ctx, own, width),
            pltpu.SemaphoreType.DMA((8,)),
            pltpu.SemaphoreType.DMA((8,)),
        ],
        compiler_params=pltpu.CompilerParams(
            collective_id=8, has_side_effects=True, vmem_limit_bytes=VMEM_LIMIT
        ),
    )(normed, gate_up, grad_mlp, summed, base, *weights)
    return packed_grads(outs), part, total


def mlp_last_call(normed, weights, grad_mlp):
    rows, width = normed.shape
    columns = weights[0].shape[-1]
    scratch, sems = mlp_scratch(weights, columns, width)
    *outs, hidden, grad_gate_up = local_call(
        functools.partial(mlp_last_kernel, lax.axis_size("ctx"), len(weights)),
        [
            *[shape_of(weight.shape) for weight in weights],
            shape_of((rows, columns // 2)),
            shape_of((rows, columns)),
        ],
        [*scratch, pltpu.VMEM((rows, columns), F32), sems],
        6 * rows * width * columns,
        (2, 1 + len(weights)),
        normed,
        grad_mlp,
        *weights,
    )
    return packed_grads(outs), hidden, grad_gate_up


def mlp_ends_call(hidden, grad_gate_up, weights):
    rows, columns = grad_gate_up.shape
    width = HEADS * HEAD_DIM
    scratch, sems = mlp_scratch(weights, columns, width)
    return local_call(
        functools.partial(mlp_ends_kernel, lax.axis_size("ctx"), len(weights)),
        [shape_of((rows, width)), shape_of((rows, width))],
        [*scratch, sems],
        3 * rows * width * columns,
        (2, 1 + len(weights)),
        hidden,
        grad_gate_up,
        *weights,
    )


def adam_kernel(rate, decay, kept, w_ref, m_ref, v_ref, g_ref, *refs):
    new_w, new_m, new_v = refs[kept:]
    grad = g_ref[...].astype(F32).reshape(w_ref.shape)
    new_w[...], new_m[...], new_v[...] = adam_step(
        w_ref[...], m_ref[...], v_ref[...], grad, rate, decay
    )


def adam_layer(layer, slot, weight, moment, square, grad, done):
    _, rows, columns = weight.shape
    if grad.ndim == 3:
        members, _, both = grad.shape
        grid, width = (2, members), both // 2
        grad_spec = pl.BlockSpec((1, rows, width), lambda i, j: (j, 0, i))
        spec = pl.BlockSpec((1, rows, width), lambda i, j: (layer, 0, i * members + j))
    else:
        grid, width = (1, 3), columns // 3
        grad_spec = pl.BlockSpec((rows, width), lambda i, j: (0, j))
        spec = pl.BlockSpec((1, rows, width), lambda i, j: (layer, 0, j))
    kept = [] if done is None else list(done)
    size = rows * columns
    return pl.pallas_call(
        functools.partial(adam_kernel, RATES[slot], DECAYS[slot], len(kept)),
        grid=grid,
        out_shape=[shape_of(weight.shape, F32)] * 3,
        in_specs=[spec, spec, spec, grad_spec] + [pl.BlockSpec(memory_space=pl.ANY)] * len(kept),
        out_specs=[spec] * 3,
        input_output_aliases={4 + i: i for i in range(len(kept))},
        cost_estimate=pl.CostEstimate(
            flops=20 * size, bytes_accessed=26 * size, transcendentals=size
        ),
        compiler_params=pltpu.CompilerParams(vmem_limit_bytes=VMEM_LIMIT),
    )(weight, moment, square, grad, *kept)


def in_order(first, then):
    return lax.optimization_barrier((first, then))


def half_rows(shard):
    half = shard.shape[0] // 2
    return lax.dynamic_slice_in_dim(shard, lax.axis_index("dp") * half, half, axis=0)


def by_member(shard, pieces):
    ctx, rows = lax.axis_size("ctx"), shard.shape[0]
    cut, start = [], 0
    for width in pieces:
        cut.append(shard[:, start : start + width].reshape(rows, ctx, width // ctx))
        start += width
    return jnp.transpose(jnp.concatenate(cut, axis=2), (1, 0, 2))


def from_members(parts, pieces):
    ctx, rows, _ = parts.shape
    out, start = [], 0
    for width in pieces:
        piece = parts[:, :, start : start + width // ctx]
        out.append(jnp.transpose(piece, (1, 0, 2)).reshape(rows, width))
        start += width // ctx
    return jnp.concatenate(out, axis=1)


def fold(columns, width):
    if width % columns == 0:
        return "even"
    return "bent" if columns > width and width % (columns - width) == 0 else "cut"


def pack(wide, rows_part):
    columns, (m, width) = wide.shape[1], rows_part.shape
    kind = fold(columns, width)
    if kind == "bent":
        rest = columns - width
        whole = m * width // columns
        right = [rows_part[whole:, i * rest : (i + 1) * rest] for i in range(width // rest)]
        below = jnp.concatenate([rows_part[:whole], jnp.concatenate(right, axis=0)], axis=1)
        return jnp.concatenate([wide, below], axis=0)
    unit = math.gcd(columns, width)
    below = jnp.concatenate(jnp.split(rows_part, width // unit, axis=1), axis=0)
    below = jnp.concatenate(jnp.split(below, columns // unit, axis=0), axis=1)
    return jnp.concatenate([wide, below], axis=0)


def unpack(packed, count, width):
    columns = packed.shape[-1]
    wide, below = packed[..., :count, :], packed[..., count:, :]
    kind = fold(columns, width)
    if kind == "bent":
        rest = columns - width
        right = jnp.split(below[..., width:], width // rest, axis=-2)
        return wide, jnp.concatenate(
            [below[..., :width], jnp.concatenate(right, axis=-1)], axis=-2
        )
    unit = math.gcd(columns, width)
    below = jnp.concatenate(jnp.split(below, columns // unit, axis=-1), axis=-2)
    return wide, jnp.concatenate(jnp.split(below, width // unit, axis=-2), axis=-1)


def pack_share(member_parts, rows_part):
    ctx, rows, columns = member_parts.shape
    return pack(member_parts.reshape(ctx * rows, columns), rows_part)


def spread(whole, width):
    ctx = lax.axis_size("ctx")
    groups, _, columns = whole.shape
    rows = width // (ctx * groups)
    wide, rows_whole = unpack(whole, ctx * rows, width)
    wide = jnp.transpose(wide.reshape(groups, ctx, rows, columns), (1, 0, 2, 3))
    return wide.reshape(-1, columns), rows_whole.reshape(-1, width)


def pack_grads(wide, rows_part):
    ctx, shards = lax.axis_size("ctx"), lax.axis_size("shard")
    columns, width = wide.shape[1], rows_part.shape[1]
    groups = shards * 2
    rows = wide.shape[0] // (ctx * groups)
    wide = jnp.transpose(wide.astype(BF).reshape(ctx, groups, rows, columns), (1, 0, 2, 3))
    wide = wide.reshape(groups, ctx * rows, columns)
    return jax.vmap(pack)(wide, rows_part.astype(BF).reshape(groups, -1, width))


def reduce_grads(packed):
    return lax.psum_scatter(
        packed.reshape(-1, packed.shape[-1]), ("shard", "dp"), scatter_dimension=0, tiled=True
    )


def share_grads(mine, width, collective_id):
    ctx, groups = lax.axis_size("ctx"), lax.axis_size("shard") * 2
    columns = mine.shape[1]
    rows = width // (ctx * groups)
    wide, rows_part = unpack(mine, ctx * rows, width)
    wide, rows_part = share_plane(wide.reshape(ctx, rows, columns), rows_part, collective_id)
    return wide.reshape(ctx, 2 * rows, columns), rows_part.reshape(-1, width)


def head_scores(query_head, key_head, allowed):
    raw = jnp.einsum(
        "tgd,sd->gts", query_head, key_head, preferred_element_type=jnp.float32
    ) * HEAD_DIM ** (-0.5)
    return jnp.where(allowed[None], raw, -1000000000.0)


def attn_forward(normed, w_qkv, w_out, cosine, sine, allowed):
    rows = normed.shape[0]
    kv_heads = w_qkv.shape[1] // (4 * HEAD_DIM)
    width_q, width_kv = 2 * kv_heads * HEAD_DIM, kv_heads * HEAD_DIM
    projected = dot(normed, w_qkv)
    query = rotate(
        projected[:, :width_q].reshape(rows, 2 * kv_heads, HEAD_DIM), cosine, sine
    ).astype(BF)
    key = rotate(
        projected[:, width_q : width_q + width_kv].reshape(rows, kv_heads, HEAD_DIM), cosine, sine
    ).astype(BF)
    value = projected[:, width_q + width_kv :].astype(BF)
    keys_t = jnp.transpose(key, (1, 0, 2))
    values_t = jnp.transpose(value.reshape(rows, kv_heads, HEAD_DIM), (1, 0, 2))
    query_t = jnp.transpose(query.reshape(rows, kv_heads, 2, HEAD_DIM), (1, 0, 2, 3))

    def head_forward(operands):
        query_head, key_head, value_head = operands
        masked = head_scores(query_head, key_head, allowed)
        row_top = jnp.max(masked, axis=-1, keepdims=True)
        exp_terms = jnp.exp(masked - row_top)
        row_total = jnp.sum(exp_terms, axis=-1, keepdims=True)
        attn_probs = exp_terms / row_total
        mixed_head = jnp.einsum(
            "gts,sd->tgd", attn_probs.astype(BF), value_head, preferred_element_type=F32
        )
        return (mixed_head, row_top, row_total)

    mixed, row_top, row_total = lax.map(head_forward, (query_t, keys_t, values_t))
    attended = jnp.transpose(mixed, (1, 0, 2, 3)).reshape(rows, width_q).astype(BF)
    return dot(attended, w_out), (normed, query_t, keys_t, values_t, row_top, row_total, attended)


def attn_backward(grad_attn, w_qkv, w_out, cosine, sine, allowed, saved):
    normed, query_t, keys_t, values_t, row_top, row_total, attended = saved
    rows = normed.shape[0]
    kv_heads = w_qkv.shape[1] // (4 * HEAD_DIM)
    width_q, width_kv = 2 * kv_heads * HEAD_DIM, kv_heads * HEAD_DIM
    grad_out_w = dot(attended, grad_attn, ((0,), (0,)))
    grad_mixed = dot(grad_attn, w_out, ((1,), (1,))).astype(BF)
    grad_t = jnp.transpose(grad_mixed.reshape(rows, kv_heads, 2, HEAD_DIM), (1, 0, 2, 3))

    def head_backward(operands):
        query_head, key_head, value_head, grad_head, row_top, row_total = operands
        masked = head_scores(query_head, key_head, allowed)
        attn_probs = jnp.exp(masked - row_top) / row_total
        grad_probs = jnp.einsum(
            "tgd,sd->gts", grad_head, value_head, preferred_element_type=jnp.float32
        )
        inner = jnp.sum(attn_probs * grad_probs, axis=-1, keepdims=True)
        grad_scores = (attn_probs * (grad_probs - inner)).astype(BF)
        grad_query = jnp.einsum(
            "gts,sd->tgd", grad_scores, key_head, preferred_element_type=jnp.float32
        ) * HEAD_DIM ** (-0.5)
        grad_key = jnp.einsum(
            "gts,tgd->sd", grad_scores, query_head, preferred_element_type=jnp.float32
        ) * HEAD_DIM ** (-0.5)
        grad_value = jnp.einsum(
            "gts,tgd->sd", attn_probs.astype(BF), grad_head, preferred_element_type=jnp.float32
        )
        return (grad_query, grad_key, grad_value)

    grad_query, grad_key, grad_value = lax.map(
        head_backward, (query_t, keys_t, values_t, grad_t, row_top, row_total)
    )
    grad_query = jnp.transpose(grad_query, (1, 0, 2, 3)).reshape(rows, 2 * kv_heads, HEAD_DIM)
    grad_projected = jnp.concatenate(
        [
            rotate(grad_query, cosine, -sine).reshape(rows, width_q),
            rotate(jnp.transpose(grad_key, (1, 0, 2)), cosine, -sine).reshape(rows, width_kv),
            jnp.transpose(grad_value, (1, 0, 2)).reshape(rows, width_kv),
        ],
        axis=1,
    ).astype(BF)
    grad_normed = dot(grad_projected, w_qkv, ((1,), (1,)))
    grad_wqkv = dot(normed, grad_projected, ((0,), (0,)))
    return grad_normed, pack_grads(grad_wqkv, grad_out_w)


def body(
    tokens,
    cotangent,
    positions,
    w_qkv,
    w_out,
    w_gate_up,
    w_down,
    norm_gains,
    first_qkv,
    first_out,
    first_gate_up,
    first_down,
    first_gains,
    second_qkv,
    second_out,
    second_gate_up,
    second_down,
    second_gains,
):
    ctx, shards = lax.axis_size("ctx"), lax.axis_size("shard")
    layer_count, own_width, width = w_qkv.shape[0], norm_gains.shape[2], tokens.shape[2]
    width_q, width_kv = HEADS * HEAD_DIM, KV_HEADS * HEAD_DIM
    qkv_pieces, gate_pieces = (width_q, width_kv, width_kv), (FF, FF)
    rows = tokens.shape[1]
    last = layer_count - 1

    def attn_share(layer):
        return by_member(half_rows(w_qkv[layer]).astype(BF), qkv_pieces)

    def mlp_share(layer):
        return by_member(half_rows(w_gate_up[layer]).astype(BF), gate_pieces)

    def gather_whole(packed):
        return lax.all_gather(packed, ("shard", "dp"), axis=0)

    attn_packs, mlp_packs = [], []
    previous = None
    for layer in range(layer_count):
        parts = attn_share(layer)
        if previous is not None:
            previous, parts = in_order(previous, parts)
            mlp_packs.append(gather_whole(previous))
        packed = pack_share(swap_ctx(parts, 2), half_rows(w_out[layer]).astype(BF))
        packed, parts = in_order(packed, mlp_share(layer))
        attn_packs.append(gather_whole(packed))
        previous = pack_share(swap_ctx(parts, 3), half_rows(w_down[layer]).astype(BF))
    mlp_packs.append(gather_whole(previous))
    mlp_sets = [mlp_weights(packed, width) for packed in mlp_packs]

    tile = jnp.pad(
        norm_gains.astype(BF).astype(F32).reshape(2 * layer_count, own_width),
        ((0, 0), (0, rows - own_width)),
    )
    tile = jnp.concatenate([tile, positions.astype(F32)], axis=0)
    tile = jnp.pad(tile, ((0, -tile.shape[0] % 8), (0, 0)))
    tiles = small_gather(tile)
    gains = jnp.transpose(tiles[:, :, : 2 * layer_count, :own_width], (2, 0, 1, 3))
    gains = gains.reshape(layer_count, 2, width)
    seq_pos = lax.dynamic_index_in_dim(
        tiles[:, :, 2 * layer_count], lax.axis_index("shard"), axis=1, keepdims=False
    ).reshape(-1)
    angles = rope_angles(seq_pos)
    cosine, sine = jnp.cos(angles), jnp.sin(angles)
    allowed = seq_pos[None, :] <= seq_pos[:, None]

    stream = tokens[0].astype(F32)
    grad_stream = cotangent[0].astype(F32)
    grad_top = gather_ctx(cotangent[0])
    saved = []
    for layer in range(layer_count):
        normed_one = gather_ctx(norm_forward(stream, gains[layer, 0]))
        weights = spread(attn_packs[layer], width)
        partial, kept = attn_forward(normed_one, *weights, cosine, sine, allowed)
        middle = scatter_ctx(partial, stream)
        normed_two = gather_ctx(norm_forward(middle, gains[layer, 1]))
        saved.append([stream, middle, weights, kept, normed_two])
        if layer < last:
            partial, gate_up = mlp_forward_call(normed_two, mlp_sets[layer])
            saved[-1].append(gate_up)
            stream = scatter_ctx(partial, middle)

    params = (w_qkv, w_out, w_gate_up, w_down)
    firsts = (first_qkv, first_out, first_gate_up, first_down)
    seconds = (second_qkv, second_out, second_gate_up, second_down)
    updated = [None] * 4

    def step(layer, slots, grads):
        for slot, grad in zip(slots, grads):
            updated[slot] = adam_layer(
                layer, slot, params[slot], firsts[slot], seconds[slot], grad, updated[slot]
            )

    def step_mlp(layer, mine):
        step(layer, (2, 3), share_grads(mine, width, 4))

    def step_attn(layer, mine):
        wide, deep = share_grads(mine, width, 5)
        step(layer, (0, 1), (from_members(wide, qkv_pieces), deep))

    attn_mine, mlp_mine = [None] * layer_count, [None] * layer_count
    gain_grads = [None] * layer_count
    for layer in reversed(range(layer_count)):
        before, middle, weights, kept, normed_two = saved[layer][:5]
        if layer < last:
            mlp_mine[layer + 1], grad_stream = in_order(mlp_mine[layer + 1], grad_stream)
        if layer == last:
            packed, hidden, dgu = mlp_last_call(normed_two, mlp_sets[layer], grad_top)
            packed, (hidden, dgu) = in_order(packed, (hidden, dgu))
            up_part, down_part = mlp_ends_call(hidden, dgu, mlp_sets[layer])
        else:
            packed, down_part, total = mlp_backward_call(
                normed_two,
                mlp_sets[layer],
                saved[layer][5],
                gather_ctx(grad_stream.astype(BF)),
                up_part,
                saved[last][1],
            )
            if layer == last - 1:
                output = total
        mlp_mine[layer] = reduce_grads(packed)
        grad_normed = scatter_ctx(down_part, jnp.zeros_like(middle))
        grad_in, grad_g2 = norm_backward(grad_normed, gains[layer, 1], middle)
        grad_stream = grad_stream + grad_in
        if layer < last:
            attn_mine[layer + 1], grad_stream = in_order(attn_mine[layer + 1], grad_stream)
        grad_normed, packed = attn_backward(
            gather_ctx(grad_stream.astype(BF)), *weights, cosine, sine, allowed, kept
        )
        packed, grad_normed = in_order(packed, grad_normed)
        if layer < last:
            packed, mine = in_order(packed, (mlp_mine[layer + 1], attn_mine[layer + 1]))
            step_mlp(layer + 1, mine[0])
            step_attn(layer + 1, mine[1])
            updated, (mlp_mine[layer], packed) = in_order(updated, (mlp_mine[layer], packed))
        attn_mine[layer] = reduce_grads(packed)
        grad_normed = scatter_ctx(grad_normed, jnp.zeros_like(middle))
        grad_in, grad_g1 = norm_backward(grad_normed, gains[layer, 0], before)
        grad_stream = grad_stream + grad_in
        gain_grads[layer] = jnp.stack([grad_g1, grad_g2])
    step_mlp(0, mlp_mine[0])
    updated, mine = in_order(updated, attn_mine[0])
    step_attn(0, mine)

    gain_tiles = jnp.stack(gain_grads).reshape(2 * layer_count, ctx, shards, own_width)
    gain_tiles = jnp.transpose(gain_tiles, (2, 1, 0, 3))
    gain_tiles = jnp.pad(
        gain_tiles, ((0, 0), (0, 0), (0, -2 * layer_count % 8), (0, -own_width % 128))
    )
    gain_grad = small_reduce(gain_tiles)[: 2 * layer_count, :own_width].reshape(norm_gains.shape)

    updated = list(updated)
    updated.append(
        adam_step(norm_gains, first_gains, second_gains, gain_grad, RATES[4], DECAYS[4])
    )
    return (
        output[None],
        grad_stream[None],
        *[updated[slot][0] for slot in range(5)],
        *[updated[slot][1] for slot in range(5)],
        *[updated[slot][2] for slot in range(5)],
    )


def solution(mesh):
    rows = P(("dp", "shard"), "ctx", None)
    weight = P(None, ("ctx", "shard"), None)
    gain = P(None, None, ("ctx", "shard"))
    group = (weight, weight, weight, weight, gain)
    return jax.shard_map(
        body,
        mesh=mesh,
        in_specs=(rows, rows, P(("dp", "shard"), "ctx"), *group, *group, *group),
        out_specs=(rows, rows, *group, *group, *group),
        check_vma=False,
    )
```

```python
import functools
import math

import jax
import jax.numpy as jnp
from jax import lax
from jax.experimental import pallas as pl
from jax.experimental.pallas import tpu as pltpu
from jax.sharding import PartitionSpec as P

HEADS = 16
KV_HEADS = 8
HEAD_DIM = 96
FF = 4096
STEP = 10


NORM_EPS = 1e-05
ROPE_BASE = 100000.0
BETA_ONE = 0.9
BETA_TWO = 0.95
ADAM_EPS = 1e-08
DECAY_RATE = 0.1
RATES = (0.05, 1.0, 0.05, 0.03, 0.8)
DECAYS = (DECAY_RATE, DECAY_RATE, DECAY_RATE, DECAY_RATE, 0.0)

BF = jnp.bfloat16
F32 = jnp.float32


def dot(left, right, dims=((1,), (0,))):
    return lax.dot_general(left, right, (dims, ((), ())), preferred_element_type=F32)


def rope_angles(positions):
    half_dim = HEAD_DIM // 2
    inverse_freq = jnp.exp(
        -jnp.log(ROPE_BASE) * (2.0 * jnp.arange(half_dim, dtype=jnp.float32) / HEAD_DIM)
    )
    return positions.astype(jnp.float32)[:, None] * inverse_freq[None, :]


def norm_forward(stream, gain):
    inverse = lax.rsqrt(jnp.mean(stream * stream, axis=-1, keepdims=True) + NORM_EPS)
    return (stream * inverse * gain).astype(BF)


def norm_backward(grad_out, gain, stream):
    inverse = lax.rsqrt(jnp.mean(stream * stream, axis=-1, keepdims=True) + NORM_EPS)
    normal_part = stream * inverse
    scaled = grad_out * gain
    gain_grad = jnp.sum(grad_out * normal_part, axis=0, keepdims=True)
    grad_in = inverse * (
        scaled - normal_part * jnp.mean(scaled * normal_part, axis=-1, keepdims=True)
    )
    return (grad_in, gain_grad)


def adam_step(weight, moment, square, grad, rate, decay):
    moment = BETA_ONE * moment + (1.0 - BETA_ONE) * grad
    square = BETA_TWO * square + (1.0 - BETA_TWO) * grad * grad
    moment_hat = moment * (rate / (1.0 - BETA_ONE**STEP))
    square_hat = square * (1.0 / (1.0 - BETA_TWO**STEP))
    weight = weight * (1.0 - rate * decay) - moment_hat / (jnp.sqrt(square_hat) + ADAM_EPS)
    return (weight, moment, square)


MESH = pl.DeviceIdType.MESH
VMEM_LIMIT = 48 * 1024 * 1024


def remote(src, dst, sems, slot, target):
    send, recv = sems
    return pltpu.make_async_remote_copy(
        src_ref=src,
        dst_ref=dst,
        send_sem=send.at[slot],
        recv_sem=recv.at[slot],
        device_id=target,
        device_id_type=MESH,
    )


def greet(targets):
    barrier = pltpu.get_barrier_semaphore()
    for target in targets:
        pl.semaphore_signal(barrier, inc=1, device_id=target, device_id_type=MESH)
    pl.semaphore_wait(barrier, len(targets))


def ctx_peers(ctx):
    me = lax.axis_index("ctx")
    return [{"ctx": lax.rem(me + step, ctx)} for step in range(1, ctx)]


def square():
    me = lax.axis_index("ctx")
    x, y = lax.rem(me, 2), me // 2
    return me, 2 * y + 1 - x, 2 * (1 - y) + x, 3 - me


def neighbours(ctx):
    if ctx != 4:
        return ctx_peers(ctx)
    _, xn, yn, _ = square()
    return [{"ctx": xn}, {"ctx": yn}]


def gather_steps(ctx, x_ref, o_ref, send, recv):
    rows = x_ref.shape[0]
    sems = (send, recv)

    def block(owner, part=None):
        if part is None:
            return pl.ds(pl.multiple_of(owner * rows, rows), rows)
        return pl.ds(pl.multiple_of(owner * rows + part * (rows // 2), rows // 2), rows // 2)

    if ctx != 4:
        me = lax.axis_index("ctx")
        copies = [
            remote(x_ref, o_ref.at[block(me)], sems, i, peer)
            for i, peer in enumerate(ctx_peers(ctx))
        ]
        for copy in copies:
            copy.start()
        o_ref[block(me), :] = x_ref[...]
        yield
        yield
        for copy in copies:
            copy.wait()
        return
    me, xn, yn, _ = square()
    to_x, to_y = {"ctx": xn}, {"ctx": yn}
    half = rows // 2
    low, high = pl.ds(0, half), pl.ds(half, half)
    first = remote(x_ref.at[low], o_ref.at[block(me, 0)], sems, 0, to_x)
    second = remote(x_ref.at[high], o_ref.at[block(me, 1)], sems, 1, to_y)
    third = remote(x_ref.at[high], o_ref.at[block(me, 1)], sems, 2, to_x)
    fourth = remote(x_ref.at[low], o_ref.at[block(me, 0)], sems, 3, to_y)
    first.start()
    second.start()
    third.start()
    fourth.start()
    o_ref[block(me), :] = x_ref[...]
    yield
    first.wait_recv()
    fifth = remote(o_ref.at[block(xn, 0)], o_ref.at[block(xn, 0)], sems, 4, to_y)
    fifth.start()
    second.wait_recv()
    sixth = remote(o_ref.at[block(yn, 1)], o_ref.at[block(yn, 1)], sems, 5, to_x)
    sixth.start()
    yield
    first.wait_send()
    second.wait_send()
    third.wait()
    fourth.wait()
    fifth.wait()
    sixth.wait()


def finish(steps):
    for _ in steps:
        pass


def gather_kernel(ctx, *refs):
    greet(neighbours(ctx))
    finish(gather_steps(ctx, *refs))


def scatter_steps(ctx, p_ref, base_ref, o_ref, relay, mixed, landed, send, recv):
    rows = o_ref.shape[0]
    sems = (send, recv)

    def block(owner, part=None):
        if part is None:
            return pl.ds(pl.multiple_of(owner * rows, rows), rows)
        return pl.ds(pl.multiple_of(owner * rows + part * (rows // 2), rows // 2), rows // 2)

    if ctx != 4:
        me = lax.axis_index("ctx")
        peers = ctx_peers(ctx)
        copies = [
            remote(p_ref.at[block(peer["ctx"])], landed.at[i], sems, i, peer)
            for i, peer in enumerate(peers)
        ]
        for copy in copies:
            copy.start()
        yield
        yield
        total = p_ref[block(me), :].astype(F32)
        if base_ref is not None:
            total = total + base_ref[...]
        for i, copy in enumerate(copies):
            copy.wait()
            total = total + landed[i].astype(F32)
        o_ref[...] = total.astype(o_ref.dtype)
        return
    me, xn, yn, far = square()
    to_x, to_y = {"ctx": xn}, {"ctx": yn}
    half = rows // 2
    low, high = pl.ds(0, half), pl.ds(half, half)
    first = remote(p_ref.at[block(far, 0)], relay.at[0], sems, 0, to_x)
    second = remote(p_ref.at[block(far, 1)], relay.at[1], sems, 1, to_y)
    third = remote(p_ref.at[block(xn, 0)], landed.at[0, low], sems, 2, to_x)
    fourth = remote(p_ref.at[block(yn, 1)], landed.at[1, high], sems, 3, to_y)
    first.start()
    second.start()
    third.start()
    fourth.start()
    yield
    first.wait_recv()
    mixed[0] = (relay[0].astype(F32) + p_ref[block(yn, 0), :].astype(F32)).astype(BF)
    fifth = remote(mixed.at[0], landed.at[1, low], sems, 4, to_y)
    fifth.start()
    second.wait_recv()
    mixed[1] = (relay[1].astype(F32) + p_ref[block(xn, 1), :].astype(F32)).astype(BF)
    sixth = remote(mixed.at[1], landed.at[0, high], sems, 5, to_x)
    sixth.start()
    yield
    first.wait_send()
    second.wait_send()
    third.wait()
    fourth.wait()
    fifth.wait()
    sixth.wait()
    total = p_ref[block(me), :].astype(F32)
    if base_ref is not None:
        total = total + base_ref[...]
    total = total + landed[0].astype(F32) + landed[1].astype(F32)
    o_ref[...] = total.astype(o_ref.dtype)


def scatter_scratch(ctx, rows, columns):
    slots = 2 if ctx == 4 else ctx - 1
    return [
        pltpu.VMEM((2, rows // 2, columns), BF),
        pltpu.VMEM((2, rows // 2, columns), BF),
        pltpu.VMEM((slots, rows, columns), BF),
    ]


def swap_kernel(ctx, x_ref, o_ref, send, recv):
    me = lax.axis_index("ctx")
    peers = ctx_peers(ctx)
    greet(peers)
    copies = [
        remote(x_ref.at[peer["ctx"]], o_ref.at[me], (send, recv), i, peer)
        for i, peer in enumerate(peers)
    ]
    for copy in copies:
        copy.start()
    o_ref[me] = x_ref[me]
    for copy in copies:
        copy.wait()


def share_kernel(ctx, x_ref, y_ref, ox_ref, oy_ref, send, recv):
    me, core = lax.axis_index("ctx"), lax.axis_index("dp")
    peers, other = ctx_peers(ctx), {"dp": 1 - core}
    greet(peers + [other])
    sems = (send, recv)
    across = [
        remote(x_ref.at[peer["ctx"]], ox_ref.at[me, core], sems, i, peer)
        for i, peer in enumerate(peers)
    ]
    inside = [
        remote(x_ref.at[me], ox_ref.at[me, core], sems, ctx, other),
        remote(y_ref, oy_ref.at[core], sems, ctx + 1, other),
    ]
    for copy in across + inside:
        copy.start()
    ox_ref[me, core] = x_ref[me]
    oy_ref[core] = y_ref[...]
    for i, copy in enumerate(across):
        copy.wait_recv()
        source = lax.rem(me + ctx - 1 - i, ctx)
        chunk = ox_ref.at[source, core]
        inside.append(remote(chunk, chunk, sems, ctx + 2 + i, other))
        inside[-1].start()
    for copy in across:
        copy.wait_send()
    for copy in inside:
        copy.wait()


def call(kernel, out_shape, scratch, copies, collective_id, *args):
    return pl.pallas_call(
        kernel,
        out_shape=out_shape,
        in_specs=[pl.BlockSpec(memory_space=pltpu.VMEM)] * len(args),
        out_specs=jax.tree.map(lambda _: pl.BlockSpec(memory_space=pltpu.VMEM), out_shape),
        scratch_shapes=[
            *scratch,
            pltpu.SemaphoreType.DMA((copies,)),
            pltpu.SemaphoreType.DMA((copies,)),
        ],
        compiler_params=pltpu.CompilerParams(
            collective_id=collective_id, has_side_effects=True, vmem_limit_bytes=VMEM_LIMIT
        ),
    )(*args)


def shape_of(shape, dtype=BF):
    return jax.ShapeDtypeStruct(shape, dtype)


def gather_ctx(block):
    ctx = lax.axis_size("ctx")
    rows, columns = block.shape
    return call(
        functools.partial(gather_kernel, ctx), shape_of((ctx * rows, columns)), [], 8, 0, block
    )


def swap_ctx(parts, collective_id):
    ctx = lax.axis_size("ctx")
    return call(
        functools.partial(swap_kernel, ctx), shape_of(parts.shape), [], ctx, collective_id, parts
    )


def share_plane(parts, own, collective_id):
    ctx = lax.axis_size("ctx")
    return call(
        functools.partial(share_kernel, ctx),
        [shape_of((ctx, 2) + parts.shape[1:]), shape_of((2,) + own.shape)],
        [],
        2 * ctx + 1,
        collective_id,
        parts,
        own,
    )


def small_gather_kernel(ctx, shards, x_ref, o_ref, send, recv):
    me, mine = lax.axis_index("ctx"), lax.axis_index("shard")
    along = [{"shard": lax.rem(mine + step, shards)} for step in range(1, shards)]
    across = ctx_peers(ctx)
    greet(along + across)
    o_ref[me, mine] = x_ref[...]
    copies = [
        remote(x_ref, o_ref.at[me, mine], (send, recv), i, target)
        for i, target in enumerate(along)
    ]
    for copy in copies:
        copy.start()
    for copy in copies:
        copy.wait()
    copies = [
        remote(o_ref.at[me], o_ref.at[me], (send, recv), shards + i, target)
        for i, target in enumerate(across)
    ]
    for copy in copies:
        copy.start()
    for copy in copies:
        copy.wait()


def small_reduce_kernel(ctx, shards, x_ref, o_ref, first, column, second, third, send, recv):
    me, mine = lax.axis_index("ctx"), lax.axis_index("shard")
    along = [{"shard": lax.rem(mine + step, shards)} for step in range(1, shards)]
    across = ctx_peers(ctx)
    other = {"dp": 1 - lax.axis_index("dp")}
    greet(along + across + [other])
    sems = (send, recv)
    copies = [
        remote(x_ref.at[target["shard"]], first.at[i], sems, i, target)
        for i, target in enumerate(along)
    ]
    for copy in copies:
        copy.start()
    total = x_ref[mine]
    for i, copy in enumerate(copies):
        copy.wait()
        total = total + first[i]
    column[...] = total
    copies = [
        remote(column.at[target["ctx"]], second.at[i], sems, shards + i, target)
        for i, target in enumerate(across)
    ]
    for copy in copies:
        copy.start()
    total = column[me]
    for i, copy in enumerate(copies):
        copy.wait()
        total = total + second[i]
    third[0] = total
    copy = remote(third.at[0], third.at[1], sems, shards + ctx, other)
    copy.start()
    copy.wait()
    o_ref[...] = third[0] + third[1]


def small_gather(tile):
    ctx, shards = lax.axis_size("ctx"), lax.axis_size("shard")
    return call(
        functools.partial(small_gather_kernel, ctx, shards),
        shape_of((ctx, shards) + tile.shape, F32),
        [],
        ctx + shards + 1,
        6,
        tile,
    )


def small_reduce(tiles):
    shards, ctx = tiles.shape[:2]
    tile = tiles.shape[2:]
    return call(
        functools.partial(small_reduce_kernel, ctx, shards),
        shape_of(tile, F32),
        [
            pltpu.VMEM((shards - 1, ctx) + tile, F32),
            pltpu.VMEM((ctx,) + tile, F32),
            pltpu.VMEM((ctx - 1,) + tile, F32),
            pltpu.VMEM((2,) + tile, F32),
        ],
        ctx + shards + 1,
        7,
        tiles,
    )


def below_parts(packed_shape, count, width):
    columns = packed_shape[2]
    below = packed_shape[1] - count
    if fold(columns, width) == "even":
        rows = below * columns // width
        return rows, [
            (count + i * rows, rows, 0, columns, 0, i * columns) for i in range(width // columns)
        ]
    rest = columns - width
    part = below // (width // rest)
    parts = [(count, below, 0, width, 0, 0)]
    for i in range(width // rest):
        parts.append((count + i * part, part, width, rest, below, i * rest))
    return below + part, parts


def load_pair(ctx, refs, wide_ref, deep_ref, sems):
    if len(refs) == 2:
        wide = [pltpu.make_async_copy(refs[0], wide_ref, sems.at[0])]
        deep = [pltpu.make_async_copy(refs[1], deep_ref, sems.at[1])]
        wide[0].start()
        deep[0].start()
        return wide, deep
    packed_ref = refs[0]
    groups = packed_ref.shape[0]
    rows = wide_ref.shape[0] // (ctx * groups)
    own_rows, parts = below_parts(packed_ref.shape, ctx * rows, deep_ref.shape[1])
    wide, deep = [], []
    for group in range(groups):
        for member in range(ctx):
            source = packed_ref.at[group, pl.ds(member * rows, rows)]
            target = wide_ref.at[pl.ds((member * groups + group) * rows, rows)]
            wide.append((source, target))
        for row, count, column, width, own_row, own_column in parts:
            source = packed_ref.at[group, pl.ds(row, count), pl.ds(column, width)]
            target = deep_ref.at[
                pl.ds(group * own_rows + own_row, count), pl.ds(own_column, width)
            ]
            deep.append((source, target))
    wide = [pltpu.make_async_copy(*pair, sems.at[i]) for i, pair in enumerate(wide)]
    deep = [pltpu.make_async_copy(*pair, sems.at[len(wide) + i]) for i, pair in enumerate(deep)]
    for copy in wide + deep:
        copy.start()
    return wide, deep


def wait_all(copies):
    for copy in copies:
        copy.wait()


def store_gate_grad(ctx, normed_ref, grad_gu, refs):
    width = normed_ref.shape[1] // ctx
    for member in range(ctx):
        part = normed_ref[:, member * width : (member + 1) * width]
        part = dot(part, grad_gu[...], ((0,), (0,))).astype(BF)
        if len(refs) == 2:
            refs[0][member * width : (member + 1) * width, :] = part
        else:
            groups = refs[0].shape[0]
            rows = width // groups
            for group in range(groups):
                refs[0][group, member * rows : (member + 1) * rows, :] = part[
                    group * rows : (group + 1) * rows
                ]
        yield


def store_down_grad(ctx, hidden, grad_ref, refs):
    if len(refs) == 2:
        refs[1][...] = dot(hidden[...], grad_ref[...], ((0,), (0,))).astype(BF)
        return
    packed_ref = refs[0]
    groups, width = packed_ref.shape[0], grad_ref.shape[1]
    own_rows, parts = below_parts(packed_ref.shape, width // groups, width)
    step = max(1, 128 // own_rows)
    for start in range(0, groups, step):
        block = hidden[:, start * own_rows : (start + step) * own_rows]
        block = dot(block, grad_ref[...], ((0,), (0,))).astype(BF)
        for group in range(step):
            for row, count, column, size, own_row, own_column in parts:
                own_row += group * own_rows
                packed_ref[start + group, row : row + count, column : column + size] = block[
                    own_row : own_row + count, own_column : own_column + size
                ]


def sigmoid(value):
    return 1.0 / (1.0 + jnp.exp(-value))


def mlp_forward_kernel(ctx, count, stream_ref, gain_ref, *refs):
    weights = refs[:count]
    new_ref, normed_ref, gu_ref, wgu, wd, own, part, sems, *scratch = refs[count:]
    greet(neighbours(ctx))
    own[...] = norm_forward(stream_ref[...], gain_ref[...])
    gathered = gather_steps(ctx, own, normed_ref, *scratch[:2])
    next(gathered)
    wide, deep = load_pair(ctx, weights, wgu, wd, sems)
    finish(gathered)
    wait_all(wide)
    gu_ref[...] = dot(normed_ref[...], wgu[...])
    half = gu_ref.shape[1] // 2
    gate, up = gu_ref[:, :half], gu_ref[:, half:]
    hidden = (gate * sigmoid(gate) * up).astype(BF)
    wait_all(deep)
    part[...] = dot(hidden, wd[...]).astype(BF)
    finish(scatter_steps(ctx, part, stream_ref, new_ref, *scratch[2:]))


def rope(value, tables, back=False):
    cosine, ahead, behind = tables
    width, half_dim = value.shape[1], HEAD_DIM // 2
    turned = pltpu.roll(value, width - half_dim, 1) * ahead[...]
    turned = turned + pltpu.roll(value, half_dim, 1) * behind[...]
    return value * cosine[...] + (-turned if back else turned)


def head_of(ref, index):
    return ref[:, index * HEAD_DIM : (index + 1) * HEAD_DIM]


def attn_forward_kernel(ctx, count, stream_ref, gain_ref, c_ref, a_ref, b_ref, col_ref, row_ref, *refs):
    weights = refs[:count]
    new_ref, normed_ref, qkv_ref, att_ref, lse_ref, wq, wo, bias, own, part, sems, *scratch = refs[
        count:
    ]
    greet(neighbours(ctx))
    own[...] = norm_forward(stream_ref[...], gain_ref[...])
    gathered = gather_steps(ctx, own, normed_ref, *scratch[:2])
    next(gathered)
    wide, deep = load_pair(ctx, weights, wq, wo, sems)
    bias[...] = jnp.where(row_ref[...] <= col_ref[...], 0.0, -1000000000.0)
    finish(gathered)
    wait_all(wide)
    projected = dot(normed_ref[...], wq[...])
    qkv_ref[...] = rope(projected, (c_ref, a_ref, b_ref)).astype(BF)
    kv_heads = qkv_ref.shape[1] // (4 * HEAD_DIM)
    lane = lax.broadcasted_iota(jnp.int32, lse_ref.shape, 1)
    mixed, lse = [], jnp.zeros(lse_ref.shape, F32)
    for head in range(2 * kv_heads):
        query = head_of(qkv_ref, head)
        key = head_of(qkv_ref, 2 * kv_heads + head // 2)
        value = head_of(qkv_ref, 3 * kv_heads + head // 2)
        scores = dot(query, key, ((1,), (1,))) * HEAD_DIM ** (-0.5) + bias[...]
        top = jnp.max(scores, axis=1, keepdims=True)
        terms = jnp.exp(scores - top)
        total = jnp.sum(terms, axis=1, keepdims=True)
        probs = (terms * (1.0 / total)).astype(BF)
        mixed.append(dot(probs, value).astype(BF))
        lse = jnp.where(lane == head, top + jnp.log(total), lse)
    att_ref[...] = jnp.concatenate(mixed, axis=1)
    lse_ref[...] = lse
    wait_all(deep)
    part[...] = dot(att_ref[...], wo[...]).astype(BF)
    finish(scatter_steps(ctx, part, stream_ref, new_ref, *scratch[2:]))


def attn_backward_kernel(
    ctx,
    count,
    dh_ref,
    stream_ref,
    gain_ref,
    normed_ref,
    qkv_ref,
    att_ref,
    lse_ref,
    c_ref,
    a_ref,
    b_ref,
    col_ref,
    row_ref,
    *refs,
):
    weights, outs = refs[:count], refs[count : 2 * count]
    new_dh, gain_grad, wq, wo, bias, own, grads, mixed, dproj, part, dy, sems = refs[
        2 * count : 2 * count + 12
    ]
    scratch = refs[2 * count + 12 :]
    greet(neighbours(ctx))
    own[...] = dh_ref[...].astype(BF)
    gathered = gather_steps(ctx, own, grads, *scratch[:2])
    next(gathered)
    wide, deep = load_pair(ctx, weights, wq, wo, sems)
    bias[...] = jnp.where(row_ref[...] <= col_ref[...], 0.0, -1000000000.0)
    finish(gathered)
    wait_all(deep)
    mixed[...] = dot(grads[...], wo[...], ((1,), (1,))).astype(BF)
    kv_heads = qkv_ref.shape[1] // (4 * HEAD_DIM)
    scale = HEAD_DIM ** (-0.5)
    dq, dk, dv = [], [0.0] * kv_heads, [0.0] * kv_heads
    for head in range(2 * kv_heads):
        group = head // 2
        query, grad = head_of(qkv_ref, head), head_of(mixed, head)
        key = head_of(qkv_ref, 2 * kv_heads + group)
        value = head_of(qkv_ref, 3 * kv_heads + group)
        scores = dot(query, key, ((1,), (1,))) * scale + bias[...]
        probs = jnp.exp(scores - lse_ref[:, head : head + 1])
        dprobs = dot(grad, value, ((1,), (1,)))
        inner = jnp.sum(probs * dprobs, axis=1, keepdims=True)
        dscores = (probs * (dprobs - inner)).astype(BF)
        dq.append(dot(dscores, key) * scale)
        dk[group] = dk[group] + dot(dscores, query, ((0,), (0,))) * scale
        dv[group] = dv[group] + dot(probs.astype(BF), grad, ((0,), (0,)))
    dproj[...] = rope(
        jnp.concatenate(dq + dk + dv, axis=1), (c_ref, a_ref, b_ref), back=True
    ).astype(BF)
    wait_all(wide)
    part[...] = dot(dproj[...], wq[...], ((1,), (1,))).astype(BF)
    scattered = scatter_steps(ctx, part, None, dy, *scratch[2:])
    next(scattered)
    stored = store_gate_grad(ctx, normed_ref, dproj, outs)
    for _ in range(ctx // 2):
        next(stored)
    next(scattered)
    finish(stored)
    store_down_grad(ctx, att_ref, grads, outs)
    finish(scattered)
    dx, gain_grad[...] = norm_backward(dy[...], gain_ref[...], stream_ref[...])
    new_dh[...] = dh_ref[...] + dx


def gate_backward(gate, up, grad_hidden):
    sig = sigmoid(gate)
    silu = gate * sig
    grad_gate = grad_hidden * up * sig * (1.0 + gate * (1.0 - sig))
    return (silu * up).astype(BF), grad_gate.astype(BF), (grad_hidden * silu).astype(BF)


def mlp_backward_kernel(
    ctx,
    count,
    normed_ref,
    gu_ref,
    dh_ref,
    stream_ref,
    gain_ref,
    sum_ref,
    base_ref,
    *refs,
):
    weights, outs = refs[:count], refs[count : 2 * count]
    new_dh, gain_grad, sum_out, wgu, wd, dgu, hidden, own, grads, part, dy, sems = refs[
        2 * count : 2 * count + 12
    ]
    scratch = refs[2 * count + 12 :]
    greet(neighbours(ctx))
    own[...] = dh_ref[...].astype(BF)
    gathered = gather_steps(ctx, own, grads, *scratch[:2])
    summed = scatter_steps(ctx, sum_ref, base_ref, sum_out, *scratch[2:7])
    scattered = scatter_steps(ctx, part, None, dy, *scratch[7:])
    next(gathered)
    wide, deep = load_pair(ctx, weights, wgu, wd, sems)
    next(gathered)
    next(summed)
    finish(gathered)
    for copy in deep:
        copy.wait()
    half = gu_ref.shape[1] // 2
    grad_hidden = dot(grads[...], wd[...], ((1,), (1,)))
    hidden[...], dgu[:, :half], dgu[:, half:] = gate_backward(
        gu_ref[:, :half], gu_ref[:, half:], grad_hidden
    )
    next(summed)
    for copy in wide:
        copy.wait()
    part[...] = dot(dgu[...], wgu[...], ((1,), (1,))).astype(BF)
    next(scattered)
    finish(summed)
    stored = store_gate_grad(ctx, normed_ref, dgu, outs)
    for _ in range(ctx // 2):
        next(stored)
    next(scattered)
    finish(stored)
    store_down_grad(ctx, hidden, grads, outs)
    finish(scattered)
    dx, gain_grad[...] = norm_backward(dy[...], gain_ref[...], stream_ref[...])
    new_dh[...] = dh_ref[...] + dx


def mlp_last_kernel(ctx, count, normed_ref, grad_ref, *refs):
    weights, outs = refs[:count], refs[count : 2 * count]
    hidden, dgu, wgu, wd, gu, sems = refs[2 * count :]
    wide, deep = load_pair(ctx, weights, wgu, wd, sems)
    for copy in wide:
        copy.wait()
    gu[...] = dot(normed_ref[...], wgu[...])
    for copy in deep:
        copy.wait()
    half = gu.shape[1] // 2
    grad_hidden = dot(grad_ref[...], wd[...], ((1,), (1,)))
    hidden[...], dgu[:, :half], dgu[:, half:] = gate_backward(
        gu[:, :half], gu[:, half:], grad_hidden
    )
    finish(store_gate_grad(ctx, normed_ref, dgu, outs))
    store_down_grad(ctx, hidden, grad_ref, outs)


def mlp_ends_kernel(ctx, count, hidden_ref, dgu_ref, dh_ref, stream_ref, gain_ref, *refs):
    weights = refs[:count]
    up_ref, new_dh, gain_grad, wgu, wd, part, dy, sems, *scratch = refs[count:]
    greet(neighbours(ctx))
    wide, deep = load_pair(ctx, weights, wgu, wd, sems)
    for copy in wide:
        copy.wait()
    part[...] = dot(dgu_ref[...], wgu[...], ((1,), (1,))).astype(BF)
    scattered = scatter_steps(ctx, part, None, dy, *scratch)
    next(scattered)
    for copy in deep:
        copy.wait()
    up_ref[...] = dot(hidden_ref[...], wd[...]).astype(BF)
    finish(scattered)
    dx, gain_grad[...] = norm_backward(dy[...], gain_ref[...], stream_ref[...])
    new_dh[...] = dh_ref[...] + dx


def local_call(kernel, out_shape, scratch, flops, hbm, *args):
    bytes_moved = sum(a.size * a.dtype.itemsize for a in args)
    bytes_moved += sum(a.size * a.dtype.itemsize for a in out_shape)
    spaces = [pl.ANY if hbm[0] <= i <= hbm[1] else pltpu.VMEM for i in range(len(args))]
    return pl.pallas_call(
        kernel,
        out_shape=out_shape,
        in_specs=[pl.BlockSpec(memory_space=space) for space in spaces],
        out_specs=[pl.BlockSpec(memory_space=pltpu.VMEM) for _ in out_shape],
        scratch_shapes=scratch,
        cost_estimate=pl.CostEstimate(flops=flops, bytes_accessed=bytes_moved, transcendentals=0),
        compiler_params=pltpu.CompilerParams(vmem_limit_bytes=VMEM_LIMIT),
    )(*args)


def weight_set(packed, width):
    ctx = lax.axis_size("ctx")
    groups, _, columns = packed.shape
    kind, rows = fold(columns, width), width // (ctx * groups)
    if kind != "cut" and rows % 16 == 0:
        return (packed,)
    return spread(packed, width)


def weight_scratch(weights, width):
    ctx = lax.axis_size("ctx")
    columns = weights[0].shape[-1]
    if len(weights) == 2:
        return [pltpu.VMEM(w.shape, BF) for w in weights], pltpu.SemaphoreType.DMA((2,))
    groups, rows, _ = weights[0].shape
    own_rows, parts = below_parts(weights[0].shape, width // groups, width)
    return [
        pltpu.VMEM((width, columns), BF),
        pltpu.VMEM((own_rows * groups, width), BF),
    ], pltpu.SemaphoreType.DMA((groups * (ctx + len(parts)),))


def comm_scratch(ctx, own, width):
    return [
        *pair_of_sems(),
        *scatter_scratch(ctx, own, width),
        *pair_of_sems(),
    ]


def mlp_forward_call(stream, gain, weights):
    ctx = lax.axis_size("ctx")
    own, width = stream.shape
    rows, columns = ctx * own, weights[0].shape[-1]
    scratch, sems = weight_scratch(weights, width)
    return remote_call(
        functools.partial(mlp_forward_kernel, ctx, len(weights)),
        [shape_of((own, width), F32), shape_of((rows, width)), shape_of((rows, columns), F32)],
        [
            *scratch,
            pltpu.VMEM((own, width), BF),
            pltpu.VMEM((rows, width), BF),
            sems,
            *comm_scratch(ctx, own, width),
        ],
        len(weights),
        10,
        stream,
        gain[None],
        *weights,
    )


def attn_forward_call(stream, gain, weights, tables):
    ctx = lax.axis_size("ctx")
    own, width = stream.shape
    rows, columns = ctx * own, weights[0].shape[-1]
    scratch, sems = weight_scratch(weights, width)
    new, *kept = remote_call(
        functools.partial(attn_forward_kernel, ctx, len(weights)),
        [
            shape_of((own, width), F32),
            shape_of((rows, width)),
            shape_of((rows, columns)),
            shape_of((rows, columns // 2)),
            shape_of((rows, 128), F32),
        ],
        [
            *scratch,
            pltpu.VMEM((rows, rows), F32),
            pltpu.VMEM((own, width), BF),
            pltpu.VMEM((rows, width), BF),
            sems,
            *comm_scratch(ctx, own, width),
        ],
        len(weights),
        11,
        stream,
        gain[None],
        *tables,
        *weights,
    )
    return new, kept


def attn_backward_call(grad_stream, stream, gain, kept, weights, tables):
    ctx = lax.axis_size("ctx")
    own, width = stream.shape
    rows, columns = ctx * own, weights[0].shape[-1]
    scratch, sems = weight_scratch(weights, width)
    *outs, new_dh, gain_grad = remote_call(
        functools.partial(attn_backward_kernel, ctx, len(weights)),
        [
            *[shape_of(weight.shape) for weight in weights],
            shape_of((own, width), F32),
            shape_of((1, width), F32),
        ],
        [
            *scratch,
            pltpu.VMEM((rows, rows), F32),
            pltpu.VMEM((own, width), BF),
            pltpu.VMEM((rows, width), BF),
            pltpu.VMEM((rows, columns // 2), BF),
            pltpu.VMEM((rows, columns), BF),
            pltpu.VMEM((rows, width), BF),
            pltpu.VMEM((own, width), F32),
            sems,
            *comm_scratch(ctx, own, width),
        ],
        len(weights),
        12,
        grad_stream,
        stream,
        gain[None],
        *kept,
        *tables,
        *weights,
    )
    return packed_grads(outs), new_dh, gain_grad[0]


def packed_grads(outs):
    return outs[0] if len(outs) == 1 else pack_grads(*outs)


def remote_call(kernel, out_shape, scratch, hbm, collective_id, *args):
    spaces = [pltpu.VMEM] * (len(args) - hbm) + [pl.ANY] * hbm
    return pl.pallas_call(
        kernel,
        out_shape=out_shape,
        in_specs=[pl.BlockSpec(memory_space=space) for space in spaces],
        out_specs=[pl.BlockSpec(memory_space=pltpu.VMEM) for _ in out_shape],
        scratch_shapes=scratch,
        compiler_params=pltpu.CompilerParams(
            collective_id=collective_id, has_side_effects=True, vmem_limit_bytes=VMEM_LIMIT
        ),
    )(*args)


def pair_of_sems():
    return [pltpu.SemaphoreType.DMA((8,)), pltpu.SemaphoreType.DMA((8,))]


def mlp_backward_call(normed, weights, gate_up, grad_stream, stream, gain, summed, base):
    ctx = lax.axis_size("ctx")
    rows, width = normed.shape
    own = base.shape[0]
    columns = weights[0].shape[-1]
    scratch, sems = weight_scratch(weights, width)
    *outs, new_dh, gain_grad, total = remote_call(
        functools.partial(mlp_backward_kernel, ctx, len(weights)),
        [
            *[shape_of(weight.shape) for weight in weights],
            shape_of((own, width), F32),
            shape_of((1, width), F32),
            shape_of((own, width)),
        ],
        [
            *scratch,
            pltpu.VMEM((rows, columns), BF),
            pltpu.VMEM((rows, columns // 2), BF),
            pltpu.VMEM((own, width), BF),
            pltpu.VMEM((rows, width), BF),
            pltpu.VMEM((rows, width), BF),
            pltpu.VMEM((own, width), F32),
            sems,
            *pair_of_sems(),
            *scatter_scratch(ctx, own, width),
            *pair_of_sems(),
            *scatter_scratch(ctx, own, width),
            *pair_of_sems(),
        ],
        len(weights),
        8,
        normed,
        gate_up,
        grad_stream,
        stream,
        gain[None],
        summed,
        base,
        *weights,
    )
    return packed_grads(outs), new_dh, gain_grad[0], total


def mlp_last_call(normed, weights, grad_mlp):
    rows, width = normed.shape
    columns = weights[0].shape[-1]
    scratch, sems = weight_scratch(weights, width)
    *outs, hidden, grad_gate_up = local_call(
        functools.partial(mlp_last_kernel, lax.axis_size("ctx"), len(weights)),
        [
            *[shape_of(weight.shape) for weight in weights],
            shape_of((rows, columns // 2)),
            shape_of((rows, columns)),
        ],
        [*scratch, pltpu.VMEM((rows, columns), F32), sems],
        6 * rows * width * columns,
        (2, 1 + len(weights)),
        normed,
        grad_mlp,
        *weights,
    )
    return packed_grads(outs), hidden, grad_gate_up


def mlp_ends_call(hidden, grad_gate_up, weights, grad_stream, stream, gain):
    ctx = lax.axis_size("ctx")
    rows, columns = grad_gate_up.shape
    own, width = stream.shape
    scratch, sems = weight_scratch(weights, width)
    part, new_dh, gain_grad = remote_call(
        functools.partial(mlp_ends_kernel, ctx, len(weights)),
        [shape_of((rows, width)), shape_of((own, width), F32), shape_of((1, width), F32)],
        [
            *scratch,
            pltpu.VMEM((rows, width), BF),
            pltpu.VMEM((own, width), F32),
            sems,
            *scatter_scratch(ctx, own, width),
            *pair_of_sems(),
        ],
        len(weights),
        9,
        hidden,
        grad_gate_up,
        grad_stream,
        stream,
        gain[None],
        *weights,
    )
    return part, new_dh, gain_grad[0]


def adam_kernel(rate, decay, kept, pieces, w_ref, m_ref, v_ref, g_ref, *refs):
    new_w, new_m, new_v = refs[kept:]
    if w_ref.shape[-1] == g_ref.shape[-1]:
        grad = g_ref[...].astype(F32).reshape(w_ref.shape)
    else:
        grad = from_members(g_ref[...].astype(F32), pieces)[None]
    new_w[...], new_m[...], new_v[...] = adam_step(
        w_ref[...], m_ref[...], v_ref[...], grad, rate, decay
    )


def adam_layer(layer, slot, weight, moment, square, grad, done, pieces):
    _, rows, columns = weight.shape
    if len(pieces) == 3:
        members, _, width = grad.shape
        parts = 2 if rows % 16 == 0 else 1
        grid = (1, parts)
        grad_spec = pl.BlockSpec((members, rows // parts, width), lambda i, j: (0, j, 0))
        spec = pl.BlockSpec((1, rows // parts, columns), lambda i, j: (layer, j, 0))
    elif len(pieces) == 2:
        members, _, both = grad.shape
        grid, width = (2, members), both // 2
        grad_spec = pl.BlockSpec((1, rows, width), lambda i, j: (j, 0, i))
        spec = pl.BlockSpec((1, rows, width), lambda i, j: (layer, 0, i * members + j))
    else:
        grid, width = (1, 3), columns // 3
        grad_spec = pl.BlockSpec((rows, width), lambda i, j: (0, j))
        spec = pl.BlockSpec((1, rows, width), lambda i, j: (layer, 0, j))
    kept = [] if done is None else list(done)
    size = rows * columns
    return pl.pallas_call(
        functools.partial(adam_kernel, RATES[slot], DECAYS[slot], len(kept), pieces),
        grid=grid,
        out_shape=[shape_of(weight.shape, F32)] * 3,
        in_specs=[spec, spec, spec, grad_spec] + [pl.BlockSpec(memory_space=pl.ANY)] * len(kept),
        out_specs=[spec] * 3,
        input_output_aliases={4 + i: i for i in range(len(kept))},
        cost_estimate=pl.CostEstimate(
            flops=20 * size, bytes_accessed=26 * size, transcendentals=size
        ),
        compiler_params=pltpu.CompilerParams(vmem_limit_bytes=VMEM_LIMIT),
    )(weight, moment, square, grad, *kept)


def in_order(first, then):
    return lax.optimization_barrier((first, then))


def half_rows(shard):
    half = shard.shape[0] // 2
    return lax.dynamic_slice_in_dim(shard, lax.axis_index("dp") * half, half, axis=0)


def by_member(shard, pieces):
    ctx, rows = lax.axis_size("ctx"), shard.shape[0]
    cut, start = [], 0
    for width in pieces:
        cut.append(shard[:, start : start + width].reshape(rows, ctx, width // ctx))
        start += width
    return jnp.transpose(jnp.concatenate(cut, axis=2), (1, 0, 2))


def from_members(parts, pieces):
    ctx = parts.shape[0]
    out, start = [], 0
    for width in pieces:
        out += [parts[i, :, start : start + width // ctx] for i in range(ctx)]
        start += width // ctx
    return jnp.concatenate(out, axis=1)


def fold(columns, width):
    if width % columns == 0:
        return "even"
    return "bent" if columns > width and width % (columns - width) == 0 else "cut"


def pack(wide, rows_part):
    columns, (m, width) = wide.shape[1], rows_part.shape
    kind = fold(columns, width)
    if kind == "bent":
        rest = columns - width
        whole = m * width // columns
        right = [rows_part[whole:, i * rest : (i + 1) * rest] for i in range(width // rest)]
        below = jnp.concatenate([rows_part[:whole], jnp.concatenate(right, axis=0)], axis=1)
        return jnp.concatenate([wide, below], axis=0)
    unit = math.gcd(columns, width)
    below = jnp.concatenate(jnp.split(rows_part, width // unit, axis=1), axis=0)
    below = jnp.concatenate(jnp.split(below, columns // unit, axis=0), axis=1)
    return jnp.concatenate([wide, below], axis=0)


def unpack(packed, count, width):
    columns = packed.shape[-1]
    wide, below = packed[..., :count, :], packed[..., count:, :]
    kind = fold(columns, width)
    if kind == "bent":
        rest = columns - width
        right = jnp.split(below[..., width:], width // rest, axis=-2)
        return wide, jnp.concatenate(
            [below[..., :width], jnp.concatenate(right, axis=-1)], axis=-2
        )
    unit = math.gcd(columns, width)
    below = jnp.concatenate(jnp.split(below, columns // unit, axis=-1), axis=-2)
    return wide, jnp.concatenate(jnp.split(below, width // unit, axis=-2), axis=-1)


def pack_share(member_parts, rows_part):
    ctx, rows, columns = member_parts.shape
    return pack(member_parts.reshape(ctx * rows, columns), rows_part)


def spread(whole, width):
    ctx = lax.axis_size("ctx")
    groups, _, columns = whole.shape
    rows = width // (ctx * groups)
    wide, rows_whole = unpack(whole, ctx * rows, width)
    wide = jnp.transpose(wide.reshape(groups, ctx, rows, columns), (1, 0, 2, 3))
    return wide.reshape(-1, columns), rows_whole.reshape(-1, width)


def pack_grads(wide, rows_part):
    ctx, shards = lax.axis_size("ctx"), lax.axis_size("shard")
    columns, width = wide.shape[1], rows_part.shape[1]
    groups = shards * 2
    rows = wide.shape[0] // (ctx * groups)
    wide = jnp.transpose(wide.astype(BF).reshape(ctx, groups, rows, columns), (1, 0, 2, 3))
    wide = wide.reshape(groups, ctx * rows, columns)
    return jax.vmap(pack)(wide, rows_part.astype(BF).reshape(groups, -1, width))


def reduce_grads(packed):
    return lax.psum_scatter(
        packed.reshape(-1, packed.shape[-1]), ("shard", "dp"), scatter_dimension=0, tiled=True
    )


def share_grads(mine, width, collective_id):
    ctx, groups = lax.axis_size("ctx"), lax.axis_size("shard") * 2
    columns = mine.shape[1]
    rows = width // (ctx * groups)
    wide, rows_part = unpack(mine, ctx * rows, width)
    wide, rows_part = share_plane(wide.reshape(ctx, rows, columns), rows_part, collective_id)
    return wide.reshape(ctx, 2 * rows, columns), rows_part.reshape(-1, width)


def body(
    tokens,
    cotangent,
    positions,
    w_qkv,
    w_out,
    w_gate_up,
    w_down,
    norm_gains,
    first_qkv,
    first_out,
    first_gate_up,
    first_down,
    first_gains,
    second_qkv,
    second_out,
    second_gate_up,
    second_down,
    second_gains,
):
    ctx, shards = lax.axis_size("ctx"), lax.axis_size("shard")
    layer_count, own_width, width = w_qkv.shape[0], norm_gains.shape[2], tokens.shape[2]
    width_q, width_kv = HEADS * HEAD_DIM, KV_HEADS * HEAD_DIM
    qkv_pieces, gate_pieces = (width_q, width_kv, width_kv), (FF, FF)
    rows = tokens.shape[1]
    last = layer_count - 1

    def attn_share(layer):
        return by_member(half_rows(w_qkv[layer]).astype(BF), qkv_pieces)

    def mlp_share(layer):
        return by_member(half_rows(w_gate_up[layer]).astype(BF), gate_pieces)

    def gather_whole(packed):
        return lax.all_gather(packed, ("shard", "dp"), axis=0)

    attn_packs, mlp_packs = [], []
    previous = None
    for layer in range(layer_count):
        parts = attn_share(layer)
        if previous is not None:
            previous, parts = in_order(previous, parts)
            mlp_packs.append(gather_whole(previous))
        packed = pack_share(swap_ctx(parts, 2), half_rows(w_out[layer]).astype(BF))
        packed, parts = in_order(packed, mlp_share(layer))
        attn_packs.append(gather_whole(packed))
        previous = pack_share(swap_ctx(parts, 3), half_rows(w_down[layer]).astype(BF))
    mlp_packs.append(gather_whole(previous))
    attn_sets = [weight_set(packed, width) for packed in attn_packs]
    mlp_sets = [weight_set(packed, width) for packed in mlp_packs]

    tile = jnp.pad(
        norm_gains.astype(BF).astype(F32).reshape(2 * layer_count, own_width),
        ((0, 0), (0, rows - own_width)),
    )
    tile = jnp.concatenate([tile, positions.astype(F32)], axis=0)
    tile = jnp.pad(tile, ((0, -tile.shape[0] % 8), (0, 0)))
    tiles = small_gather(tile)
    gains = jnp.transpose(tiles[:, :, : 2 * layer_count, :own_width], (2, 0, 1, 3))
    gains = gains.reshape(layer_count, 2, width)
    seq_pos = lax.dynamic_index_in_dim(
        tiles[:, :, 2 * layer_count], lax.axis_index("shard"), axis=1, keepdims=False
    ).reshape(-1)
    angles = rope_angles(seq_pos)
    cosine, sine = jnp.cos(angles), jnp.sin(angles)
    turned = 3 * KV_HEADS // ctx
    value_part = jnp.zeros((seq_pos.shape[0], KV_HEADS // ctx * HEAD_DIM), F32)
    nothing = jnp.zeros_like(sine)
    tables = (
        jnp.concatenate([cosine, cosine] * turned + [value_part + 1.0], axis=1),
        jnp.concatenate([-sine, nothing] * turned + [value_part], axis=1),
        jnp.concatenate([nothing, sine] * turned + [value_part], axis=1),
        seq_pos[:, None],
        seq_pos[None, :],
    )

    stream = tokens[0].astype(F32)
    grad_stream = cotangent[0].astype(F32)
    grad_top = gather_ctx(cotangent[0])
    saved = []
    for layer in range(layer_count):
        middle, kept = attn_forward_call(stream, gains[layer, 0], attn_sets[layer], tables)
        saved.append([stream, middle, kept])
        if layer < last:
            stream, *gate_kept = mlp_forward_call(middle, gains[layer, 1], mlp_sets[layer])
            saved[-1] += gate_kept
        else:
            saved[-1].append(gather_ctx(norm_forward(middle, gains[layer, 1])))

    params = (w_qkv, w_out, w_gate_up, w_down)
    firsts = (first_qkv, first_out, first_gate_up, first_down)
    seconds = (second_qkv, second_out, second_gate_up, second_down)
    updated = [None] * 4

    def step(layer, slots, grads, pieces):
        for slot, grad, cut in zip(slots, grads, (pieces, ())):
            updated[slot] = adam_layer(
                layer, slot, params[slot], firsts[slot], seconds[slot], grad, updated[slot], cut
            )

    def step_mlp(layer, mine):
        step(layer, (2, 3), share_grads(mine, width, 4), gate_pieces)

    def step_attn(layer, mine):
        step(layer, (0, 1), share_grads(mine, width, 5), qkv_pieces)

    def sum_gains(gain_grads):
        gain_tiles = jnp.stack(gain_grads).reshape(2 * layer_count, ctx, shards, own_width)
        gain_tiles = jnp.transpose(gain_tiles, (2, 1, 0, 3))
        gain_tiles = jnp.pad(
            gain_tiles, ((0, 0), (0, 0), (0, -2 * layer_count % 8), (0, -own_width % 128))
        )
        return small_reduce(gain_tiles)[: 2 * layer_count, :own_width].reshape(norm_gains.shape)

    attn_mine, mlp_mine = [None] * layer_count, [None] * layer_count
    gain_grads = [None] * layer_count
    for layer in reversed(range(layer_count)):
        before, middle, kept, normed_two = saved[layer][:4]
        if layer == last:
            packed, hidden, dgu = mlp_last_call(normed_two, mlp_sets[layer], grad_top)
            packed, (hidden, dgu) = in_order(packed, (hidden, dgu))
            up_part, grad_stream, grad_g2 = mlp_ends_call(
                hidden, dgu, mlp_sets[layer], grad_stream, middle, gains[layer, 1]
            )
        else:
            packed, grad_stream, grad_g2, total = mlp_backward_call(
                normed_two,
                mlp_sets[layer],
                saved[layer][4],
                grad_stream,
                middle,
                gains[layer, 1],
                up_part,
                saved[last][1],
            )
            if layer == last - 1:
                output = total
        mlp_mine[layer] = reduce_grads(packed)
        if layer < last:
            mlp_mine[layer + 1], grad_stream = in_order(mlp_mine[layer + 1], grad_stream)
        packed, grad_stream, grad_g1 = attn_backward_call(
            grad_stream, before, gains[layer, 0], kept, attn_sets[layer], tables
        )
        gain_grads[layer] = jnp.stack([grad_g1, grad_g2])
        if layer == 0:
            gain_grad = sum_gains(gain_grads)
        if layer < last:
            packed, mine = in_order(packed, (mlp_mine[layer + 1], attn_mine[layer + 1]))
            step_mlp(layer + 1, mine[0])
            step_attn(layer + 1, mine[1])
            (updated, gain_grad), (mlp_mine[layer], packed) = in_order(
                (updated, gain_grad), (mlp_mine[layer], packed)
            )
        attn_mine[layer] = reduce_grads(packed)
    step_mlp(0, mlp_mine[0])
    updated, mine = in_order(updated, attn_mine[0])
    step_attn(0, mine)

    updated = list(updated)
    updated.append(
        adam_step(norm_gains, first_gains, second_gains, gain_grad, RATES[4], DECAYS[4])
    )
    return (
        output[None],
        grad_stream[None],
        *[updated[slot][0] for slot in range(5)],
        *[updated[slot][1] for slot in range(5)],
        *[updated[slot][2] for slot in range(5)],
    )


def solution(mesh):
    rows = P(("dp", "shard"), "ctx", None)
    weight = P(None, ("ctx", "shard"), None)
    gain = P(None, None, ("ctx", "shard"))
    group = (weight, weight, weight, weight, gain)
    return jax.shard_map(
        body,
        mesh=mesh,
        in_specs=(rows, rows, P(("dp", "shard"), "ctx"), *group, *group, *group),
        out_specs=(rows, rows, *group, *group, *group),
        check_vma=False,
    )
```

```python
import functools
import math

import jax
import jax.numpy as jnp
import numpy as np
from jax import lax
from jax.experimental import pallas as pl
from jax.experimental.pallas import tpu as pltpu
from jax.sharding import PartitionSpec as P

HEADS = 16
KV_HEADS = 8
HEAD_DIM = 96
FF = 4096
STEP = 10


NORM_EPS = 1e-05
ROPE_BASE = 100000.0
BETA_ONE = 0.9
BETA_TWO = 0.95
ADAM_EPS = 1e-08
DECAY_RATE = 0.1
RATES = (0.05, 1.0, 0.05, 0.03, 0.8)
DECAYS = (DECAY_RATE, DECAY_RATE, DECAY_RATE, DECAY_RATE, 0.0)

BF = jnp.bfloat16
F32 = jnp.float32


def dot(left, right, dims=((1,), (0,))):
    return lax.dot_general(left, right, (dims, ((), ())), preferred_element_type=F32)


def rope_angles(positions):
    powers = 2.0 * np.arange(HEAD_DIM // 2) / HEAD_DIM
    inverse_freq = np.exp(-np.log(ROPE_BASE) * powers).astype(np.float32)
    return positions.astype(F32)[:, None] * inverse_freq[None, :]


def norm_forward(stream, gain):
    inverse = lax.rsqrt(jnp.mean(stream * stream, axis=-1, keepdims=True) + NORM_EPS)
    return (stream * inverse * gain).astype(BF)


def norm_backward(grad_out, gain, stream):
    inverse = lax.rsqrt(jnp.mean(stream * stream, axis=-1, keepdims=True) + NORM_EPS)
    normal_part = stream * inverse
    scaled = grad_out * gain
    gain_grad = jnp.sum(grad_out * normal_part, axis=0, keepdims=True)
    grad_in = inverse * (
        scaled - normal_part * jnp.mean(scaled * normal_part, axis=-1, keepdims=True)
    )
    return (grad_in, gain_grad)


def adam_step(weight, moment, square, grad, rate, decay):
    moment = BETA_ONE * moment + (1.0 - BETA_ONE) * grad
    square = BETA_TWO * square + (1.0 - BETA_TWO) * grad * grad
    moment_hat = moment * (rate / (1.0 - BETA_ONE**STEP))
    square_hat = square * (1.0 / (1.0 - BETA_TWO**STEP))
    weight = weight * (1.0 - rate * decay) - moment_hat / (jnp.sqrt(square_hat) + ADAM_EPS)
    return (weight, moment, square)


MESH = pl.DeviceIdType.MESH
VMEM_LIMIT = 61 * 1024 * 1024
SMALL_LIMIT = 24 * 1024 * 1024


def remote(src, dst, sems, slot, target):
    send, recv = sems
    return pltpu.make_async_remote_copy(
        src_ref=src,
        dst_ref=dst,
        send_sem=send.at[slot],
        recv_sem=recv.at[slot],
        device_id=target,
        device_id_type=MESH,
    )


def greet(targets):
    barrier = pltpu.get_barrier_semaphore()
    for target in targets:
        pl.semaphore_signal(barrier, inc=1, device_id=target, device_id_type=MESH)
    pl.semaphore_wait(barrier, len(targets))


def ctx_peers(ctx):
    me = lax.axis_index("ctx")
    return [{"ctx": lax.rem(me + step, ctx)} for step in range(1, ctx)]


def square():
    me = lax.axis_index("ctx")
    x, y = lax.rem(me, 2), me // 2
    return me, 2 * y + 1 - x, 2 * (1 - y) + x, 3 - me


def neighbours(ctx):
    if ctx != 4:
        return ctx_peers(ctx)
    _, xn, yn, _ = square()
    return [{"ctx": xn}, {"ctx": yn}]


def gather_steps(ctx, x_ref, o_ref, send, recv):
    rows = x_ref.shape[0]
    sems = (send, recv)

    def block(owner, part=None):
        if part is None:
            return pl.ds(pl.multiple_of(owner * rows, rows), rows)
        return pl.ds(pl.multiple_of(owner * rows + part * (rows // 2), rows // 2), rows // 2)

    if ctx != 4:
        me = lax.axis_index("ctx")
        copies = [
            remote(x_ref, o_ref.at[block(me)], sems, i, peer)
            for i, peer in enumerate(ctx_peers(ctx))
        ]
        for copy in copies:
            copy.start()
        o_ref[block(me), :] = x_ref[...]
        yield
        yield
        for copy in copies:
            copy.wait()
        return
    me, xn, yn, _ = square()
    to_x, to_y = {"ctx": xn}, {"ctx": yn}
    half = rows // 2
    low, high = pl.ds(0, half), pl.ds(half, half)
    first = remote(x_ref.at[low], o_ref.at[block(me, 0)], sems, 0, to_x)
    second = remote(x_ref.at[high], o_ref.at[block(me, 1)], sems, 1, to_y)
    third = remote(x_ref.at[high], o_ref.at[block(me, 1)], sems, 2, to_x)
    fourth = remote(x_ref.at[low], o_ref.at[block(me, 0)], sems, 3, to_y)
    first.start()
    second.start()
    third.start()
    fourth.start()
    o_ref[block(me), :] = x_ref[...]
    yield
    first.wait_recv()
    fifth = remote(o_ref.at[block(xn, 0)], o_ref.at[block(xn, 0)], sems, 4, to_y)
    fifth.start()
    second.wait_recv()
    sixth = remote(o_ref.at[block(yn, 1)], o_ref.at[block(yn, 1)], sems, 5, to_x)
    sixth.start()
    yield
    first.wait_send()
    second.wait_send()
    third.wait()
    fourth.wait()
    fifth.wait()
    sixth.wait()


def finish(steps):
    for _ in steps:
        pass


def gather_kernel(ctx, *refs):
    greet(neighbours(ctx))
    finish(gather_steps(ctx, *refs))


def scatter_steps(ctx, p_ref, base_ref, o_ref, relay, mixed, landed, send, recv):
    rows = o_ref.shape[0]
    sems = (send, recv)

    def block(owner, part=None):
        if part is None:
            return pl.ds(pl.multiple_of(owner * rows, rows), rows)
        return pl.ds(pl.multiple_of(owner * rows + part * (rows // 2), rows // 2), rows // 2)

    if ctx != 4:
        me = lax.axis_index("ctx")
        peers = ctx_peers(ctx)
        copies = [
            remote(p_ref.at[block(peer["ctx"])], landed.at[i], sems, i, peer)
            for i, peer in enumerate(peers)
        ]
        for copy in copies:
            copy.start()
        yield
        yield
        total = p_ref[block(me), :].astype(F32)
        if base_ref is not None:
            total = total + base_ref[...].astype(F32)
        for i, copy in enumerate(copies):
            copy.wait()
            total = total + landed[i].astype(F32)
        o_ref[...] = total.astype(o_ref.dtype)
        return
    me, xn, yn, far = square()
    to_x, to_y = {"ctx": xn}, {"ctx": yn}
    half = rows // 2
    low, high = pl.ds(0, half), pl.ds(half, half)
    first = remote(p_ref.at[block(far, 0)], relay.at[0], sems, 0, to_x)
    second = remote(p_ref.at[block(far, 1)], relay.at[1], sems, 1, to_y)
    third = remote(p_ref.at[block(xn, 0)], landed.at[0, low], sems, 2, to_x)
    fourth = remote(p_ref.at[block(yn, 1)], landed.at[1, high], sems, 3, to_y)
    first.start()
    second.start()
    third.start()
    fourth.start()
    yield
    first.wait_recv()
    mixed[0] = (relay[0].astype(F32) + p_ref[block(yn, 0), :].astype(F32)).astype(BF)
    fifth = remote(mixed.at[0], landed.at[1, low], sems, 4, to_y)
    fifth.start()
    second.wait_recv()
    mixed[1] = (relay[1].astype(F32) + p_ref[block(xn, 1), :].astype(F32)).astype(BF)
    sixth = remote(mixed.at[1], landed.at[0, high], sems, 5, to_x)
    sixth.start()
    yield
    first.wait_send()
    second.wait_send()
    third.wait()
    fourth.wait()
    fifth.wait()
    sixth.wait()
    total = p_ref[block(me), :].astype(F32)
    if base_ref is not None:
        total = total + base_ref[...].astype(F32)
    total = total + landed[0].astype(F32) + landed[1].astype(F32)
    o_ref[...] = total.astype(o_ref.dtype)


def scatter_scratch(ctx, rows, columns):
    slots = 2 if ctx == 4 else ctx - 1
    return [
        pltpu.VMEM((2, rows // 2, columns), BF),
        pltpu.VMEM((2, rows // 2, columns), BF),
        pltpu.VMEM((slots, rows, columns), BF),
    ]


def swap_kernel(ctx, x_ref, o_ref, send, recv):
    me = lax.axis_index("ctx")
    peers = ctx_peers(ctx)
    greet(peers)
    copies = [
        remote(x_ref.at[peer["ctx"]], o_ref.at[me], (send, recv), i, peer)
        for i, peer in enumerate(peers)
    ]
    for copy in copies:
        copy.start()
    o_ref[me] = x_ref[me]
    for copy in copies:
        copy.wait()


def share_kernel(ctx, packed, *refs):
    sources, (ox_ref, oy_ref, send, recv) = refs[: 1 if packed else 2], refs[1 if packed else 2 :]
    me, core = lax.axis_index("ctx"), lax.axis_index("dp")
    peers, other = ctx_peers(ctx), {"dp": 1 - core}
    rows, width = ox_ref.shape[2], oy_ref.shape[2]
    greet(peers + [other])
    sems = (send, recv)

    def chunk(member):
        if packed:
            return sources[0].at[pl.ds(pl.multiple_of(member * rows, rows), rows)]
        return sources[0].at[member]

    across = [
        remote(chunk(peer["ctx"]), ox_ref.at[me, core], sems, i, peer)
        for i, peer in enumerate(peers)
    ]
    for copy in across:
        copy.start()
    if packed:
        _, parts = below_parts((1,) + sources[0].shape, ctx * rows, width)
        for row, size, column, part, own_row, own_column in parts:
            oy_ref[core, own_row : own_row + size, own_column : own_column + part] = sources[0][
                row : row + size, column : column + part
            ]
    else:
        oy_ref[core] = sources[1][...]
    ox_ref[me, core] = chunk(me)[...]
    inside = [
        remote(ox_ref.at[me, core], ox_ref.at[me, core], sems, ctx, other),
        remote(oy_ref.at[core], oy_ref.at[core], sems, ctx + 1, other),
    ]
    for copy in inside:
        copy.start()
    for i, copy in enumerate(across):
        copy.wait_recv()
        source = lax.rem(me + ctx - 1 - i, ctx)
        block = ox_ref.at[source, core]
        inside.append(remote(block, block, sems, ctx + 2 + i, other))
        inside[-1].start()
    for copy in across:
        copy.wait_send()
    for copy in inside:
        copy.wait()


def call(kernel, out_shape, scratch, copies, collective_id, *args, limit=VMEM_LIMIT):
    return pl.pallas_call(
        kernel,
        out_shape=out_shape,
        in_specs=[pl.BlockSpec(memory_space=pltpu.VMEM)] * len(args),
        out_specs=jax.tree.map(lambda _: pl.BlockSpec(memory_space=pltpu.VMEM), out_shape),
        scratch_shapes=[
            *scratch,
            pltpu.SemaphoreType.DMA((copies,)),
            pltpu.SemaphoreType.DMA((copies,)),
        ],
        compiler_params=pltpu.CompilerParams(
            collective_id=collective_id, has_side_effects=True, vmem_limit_bytes=limit
        ),
    )(*args)


def shape_of(shape, dtype=BF):
    return jax.ShapeDtypeStruct(shape, dtype)


def gather_ctx(block):
    ctx = lax.axis_size("ctx")
    rows, columns = block.shape
    return call(
        functools.partial(gather_kernel, ctx), shape_of((ctx * rows, columns)), [], 8, 0, block
    )


def swap_ctx(parts, collective_id):
    ctx = lax.axis_size("ctx")
    return call(
        functools.partial(swap_kernel, ctx), shape_of(parts.shape), [], ctx, collective_id, parts
    )


def share_plane(sums, shapes, collective_id):
    ctx = lax.axis_size("ctx")
    return call(
        functools.partial(share_kernel, ctx, len(sums) == 1),
        [shape_of((ctx, 2) + shapes[0]), shape_of((2,) + shapes[1])],
        [],
        2 * ctx + 1,
        collective_id,
        *sums,
        limit=SMALL_LIMIT,
    )


def small_reduce_kernel(ctx, shards, x_ref, o_ref, first, column, second, third, send, recv):
    me, mine = lax.axis_index("ctx"), lax.axis_index("shard")
    along = [{"shard": lax.rem(mine + step, shards)} for step in range(1, shards)]
    across = ctx_peers(ctx)
    other = {"dp": 1 - lax.axis_index("dp")}
    greet(along + across + [other])
    sems = (send, recv)
    copies = [
        remote(x_ref.at[target["shard"]], first.at[i], sems, i, target)
        for i, target in enumerate(along)
    ]
    for copy in copies:
        copy.start()
    total = x_ref[mine]
    for i, copy in enumerate(copies):
        copy.wait()
        total = total + first[i]
    column[...] = total
    copies = [
        remote(column.at[target["ctx"]], second.at[i], sems, shards + i, target)
        for i, target in enumerate(across)
    ]
    for copy in copies:
        copy.start()
    total = column[me]
    for i, copy in enumerate(copies):
        copy.wait()
        total = total + second[i]
    third[0] = total
    copy = remote(third.at[0], third.at[1], sems, shards + ctx, other)
    copy.start()
    copy.wait()
    o_ref[...] = third[0] + third[1]


def small_gather(tile):
    ctx, shards = lax.axis_size("ctx"), lax.axis_size("shard")
    return call(
        functools.partial(small_gather_kernel, ctx, shards),
        shape_of((ctx, shards) + tile.shape, F32),
        [],
        ctx + shards + 1,
        6,
        tile,
    )


def small_reduce(tiles):
    shards, ctx = tiles.shape[:2]
    tile = tiles.shape[2:]
    return call(
        functools.partial(small_reduce_kernel, ctx, shards),
        shape_of(tile, F32),
        [
            pltpu.VMEM((shards - 1, ctx) + tile, F32),
            pltpu.VMEM((ctx,) + tile, F32),
            pltpu.VMEM((ctx - 1,) + tile, F32),
            pltpu.VMEM((2,) + tile, F32),
        ],
        ctx + shards + 1,
        7,
        tiles,
    )


def below_parts(packed_shape, count, width):
    columns = packed_shape[2]
    below = packed_shape[1] - count
    if fold(columns, width) == "even":
        rows = below * columns // width
        return rows, [
            (count + i * rows, rows, 0, columns, 0, i * columns) for i in range(width // columns)
        ]
    rest = columns - width
    part = below // (width // rest)
    parts = [(count, below, 0, width, 0, 0)]
    for i in range(width // rest):
        parts.append((count + i * part, part, width, rest, below, i * rest))
    return below + part, parts


def load_pair(ctx, refs, wide_ref, deep_ref, sems):
    if len(refs) == 2:
        wide = [pltpu.make_async_copy(refs[0], wide_ref, sems.at[0])]
        deep = [pltpu.make_async_copy(refs[1], deep_ref, sems.at[1])]
        wide[0].start()
        deep[0].start()
        return wide, deep
    packed_ref = refs[0]
    groups = packed_ref.shape[0]
    rows = wide_ref.shape[0] // (ctx * groups)
    own_rows, parts = below_parts(packed_ref.shape, ctx * rows, deep_ref.shape[1])
    wide, deep = [], []
    for group in range(groups):
        for member in range(ctx):
            source = packed_ref.at[group, pl.ds(member * rows, rows)]
            target = wide_ref.at[pl.ds((member * groups + group) * rows, rows)]
            wide.append((source, target))
        for row, count, column, width, own_row, own_column in parts:
            source = packed_ref.at[group, pl.ds(row, count), pl.ds(column, width)]
            target = deep_ref.at[
                pl.ds(group * own_rows + own_row, count), pl.ds(own_column, width)
            ]
            deep.append((source, target))
    wide = [pltpu.make_async_copy(*pair, sems.at[i]) for i, pair in enumerate(wide)]
    deep = [pltpu.make_async_copy(*pair, sems.at[len(wide) + i]) for i, pair in enumerate(deep)]
    for copy in wide + deep:
        copy.start()
    return wide, deep


def start_loads(sources, targets, sems):
    copies = [
        pltpu.make_async_copy(source, target, sems.at[i])
        for i, (source, target) in enumerate(zip(sources, targets))
    ]
    for copy in copies:
        copy.start()
    return copies


def wait_all(copies):
    for copy in copies:
        copy.wait()


def z_gather_steps(shards, parts, eager, src, out, local_sems, send, recv):
    mine, core = lax.axis_index("shard"), lax.axis_index("dp")
    other = {"dp": 1 - core}
    sems = (send, recv)
    hops = shards - 1
    inside = 2 * hops * len(parts)

    def source(part):
        return src.at[pl.ds(*parts[part])]

    def place(owner, part):
        return out.at[owner * 2 + core, pl.ds(*parts[part])]

    def number(way, hop, part):
        return (way * hops + hop) * len(parts) + part

    def sent(way, hop, part):
        step = 1 - 2 * way
        owner = mine - step * hop
        block = source(part) if hop == 0 else place(owner, part)
        target = {"shard": mine + step}
        return remote(block, place(owner, part), sems, number(way, hop, part), target)

    def landed(way, hop, part):
        step = 1 - 2 * way
        block = place(mine - step * (hop + 1), part)
        return remote(block, block, sems, number(way, hop, part), {"shard": mine - step})

    def shared(way, hop, part):
        step = 1 - 2 * way
        block = place(mine - step * (hop + 1), part)
        slot = inside + len(parts) + number(way, hop, part)
        return remote(block, block, sems, slot, other)

    def own(part):
        return remote(source(part), place(mine, part), sems, inside + part, other)

    def local(part):
        return pltpu.make_async_copy(source(part), place(mine, part), local_sems.at[part])

    def sends(way, hop):
        if way == 0:
            return jnp.logical_and(mine >= hop, mine < shards - 1)
        return jnp.logical_and(mine < shards - hop, mine > 0)

    def receives(way, hop):
        return mine > hop if way == 0 else mine < shards - 1 - hop

    for part in range(len(parts)):
        for way in range(2):
            pl.when(sends(way, 0))(lambda way=way, part=part: sent(way, 0, part).start())
        if not eager:
            local(part).start()
            own(part).start()
            yield
    if eager:
        for part in range(len(parts)):
            local(part).start()
            own(part).start()
        yield
    for hop in range(hops):
        for part in range(len(parts)):
            for way in range(2):

                def arrived(way=way, hop=hop, part=part):
                    landed(way, hop, part).wait_recv()

                def hand_on(way=way, hop=hop, part=part):
                    sent(way, hop + 1, part).start()

                def share(way=way, hop=hop, part=part):
                    shared(way, hop, part).start()

                pl.when(receives(way, hop))(arrived)
                if hop + 1 < hops:
                    pl.when(sends(way, hop + 1))(hand_on)
                pl.when(receives(way, hop))(share)
            yield
    for part in range(len(parts)):
        local(part).wait()
        own(part).wait()
        for way in range(2):
            for hop in range(hops):
                pl.when(sends(way, hop))(
                    lambda way=way, hop=hop, part=part: sent(way, hop, part).wait_send()
                )
                pl.when(receives(way, hop))(
                    lambda way=way, hop=hop, part=part: shared(way, hop, part).wait()
                )


def halves(rows):
    half = rows // 32 * 16
    return [(0, half), (half, rows - half)]


def greet_line(ctx, shards):
    mine = lax.axis_index("shard")
    barrier = pltpu.get_barrier_semaphore()

    def signal(target):
        pl.semaphore_signal(barrier, inc=1, device_id=target, device_id_type=MESH)

    targets = neighbours(ctx) + [{"dp": 1 - lax.axis_index("dp")}]
    for target in targets:
        signal(target)
    pl.when(mine > 0)(lambda: signal({"shard": mine - 1}))
    pl.when(mine < shards - 1)(lambda: signal({"shard": mine + 1}))
    at_end = jnp.logical_or(mine == 0, mine == shards - 1)
    pl.when(at_end)(lambda: pl.semaphore_wait(barrier, len(targets) + 1))
    pl.when(jnp.logical_not(at_end))(lambda: pl.semaphore_wait(barrier, len(targets) + 2))


def line_sems(shards):
    count = 8 * (shards - 1) + 2
    return [
        pltpu.SemaphoreType.DMA((2,)),
        pltpu.SemaphoreType.DMA((count,)),
        pltpu.SemaphoreType.DMA((count,)),
    ]


def small_gather_steps(ctx, shards, x_ref, o_ref, send, recv):
    me, mine = lax.axis_index("ctx"), lax.axis_index("shard")
    along = [{"shard": lax.rem(mine + step, shards)} for step in range(1, shards)]
    o_ref[me, mine] = x_ref[...]
    copies = [
        remote(x_ref, o_ref.at[me, mine], (send, recv), i, target)
        for i, target in enumerate(along)
    ]
    for copy in copies:
        copy.start()
    yield
    wait_all(copies)
    copies = [
        remote(o_ref.at[me], o_ref.at[me], (send, recv), shards + i, target)
        for i, target in enumerate(ctx_peers(ctx))
    ]
    for copy in copies:
        copy.start()
    yield
    wait_all(copies)


def small_gather_kernel(ctx, shards, *refs):
    mine = lax.axis_index("shard")
    greet([{"shard": lax.rem(mine + step, shards)} for step in range(1, shards)] + ctx_peers(ctx))
    finish(small_gather_steps(ctx, shards, *refs))


def place_deep(block, packed_ref, count):
    columns = packed_ref.shape[1]
    _, parts = below_parts((1,) + packed_ref.shape, count, block.shape[1])
    for row, size, column, width, own_row, own_column in parts:
        packed_ref[row : row + size, column : column + width] = block[
            own_row : own_row + size, own_column : own_column + width
        ]


def gain_rows(tiles_ref, own_width):
    ctx, shards = tiles_ref.shape[:2]
    parts = [tiles_ref[i, j][:, :own_width] for i in range(ctx) for j in range(shards)]
    return jnp.concatenate(parts, axis=1)


def prologue_kernel(ctx, shards, layers, pieces, gains_ref, *refs):
    weights, refs = refs[:4], refs[4:]
    all_gains_ref, whole_ref, *packs = refs[: 2 + 2 * layers]
    stage, refs = refs[2 + 2 * layers : 2 + 6 * layers], refs[2 + 6 * layers :]
    cuts, refs = refs[: 2 * layers], refs[2 * layers :]
    tile_ref, tiles_ref, stage_sems, swap_send, swap_recv, small_send, small_recv, *line = refs
    own_width = gains_ref.shape[2]
    me, mine, core = lax.axis_index("ctx"), lax.axis_index("shard"), lax.axis_index("dp")
    peers = ctx_peers(ctx)
    greet(
        peers
        + [{"shard": lax.rem(mine + step, shards)} for step in range(1, shards)]
        + [{"dp": 1 - core}]
    )
    loads = []
    for layer in range(layers):
        for slot, weight in enumerate(weights):
            target = stage[4 * layer + slot]
            rows = target.shape[0]
            source = weight.at[layer, pl.ds(pl.multiple_of(core * rows, rows), rows)]
            loads.append(pltpu.make_async_copy(source, target, stage_sems.at[len(loads)]))
    loads[1].start()
    for i, load in enumerate(loads):
        if i != 1:
            load.start()
    tile_ref[...] = jnp.zeros_like(tile_ref)
    for layer in range(layers):
        own_gains = gains_ref[layer].astype(BF).astype(F32)
        tile_ref[2 * layer : 2 * layer + 2, :own_width] = own_gains
    small = small_gather_steps(ctx, shards, tile_ref, tiles_ref, small_send, small_recv)
    next(small)
    count = ctx * cuts[0].shape[1]
    first_parts = [(count, packs[0].shape[0] - count), (0, count)]
    line_steps = z_gather_steps(shards, first_parts, False, packs[0], whole_ref, *line)
    swaps = []
    for layer in range(layers):
        for kind in range(2):
            number = 2 * layer + kind
            pack_ref, cut = packs[number], cuts[number]
            wide, deep = 4 * layer + 2 * kind, 4 * layer + 2 * kind + 1
            rows = cut.shape[1]
            loads[deep].wait()
            place_deep(stage[deep][...].astype(BF), pack_ref, ctx * rows)
            if number == 0:
                next(line_steps)
            loads[wide].wait()
            for member, part in enumerate(member_parts(stage[wide][...], pieces[kind], ctx)):
                cut[member] = part.astype(BF)
            here = pl.ds(pl.multiple_of(me * rows, rows), rows)
            first = number * (ctx - 1)
            copies = [
                remote(cut.at[peer["ctx"]], pack_ref.at[here], (swap_send, swap_recv), first + i, peer)
                for i, peer in enumerate(peers)
            ]
            for copy in copies:
                copy.start()
            pack_ref[here, :] = cut[me]
            if number == 0:
                wait_all(copies)
                next(line_steps)
                next(small)
            else:
                swaps += copies
                next(line_steps)
    finish(small)
    all_gains_ref[...] = gain_rows(tiles_ref, own_width)
    finish(line_steps)
    wait_all(swaps)


def store_gate_grad(ctx, normed_ref, grad_gu, refs):
    width = normed_ref.shape[1] // ctx
    for member in range(ctx):
        part = normed_ref[:, member * width : (member + 1) * width]
        part = dot(part, grad_gu[...], ((0,), (0,))).astype(BF)
        if len(refs) == 2:
            refs[0][member * width : (member + 1) * width, :] = part
        else:
            groups = refs[0].shape[0]
            rows = width // groups
            for group in range(groups):
                refs[0][group, member * rows : (member + 1) * rows, :] = part[
                    group * rows : (group + 1) * rows
                ]
        yield


def store_down_grad(ctx, hidden, grad_ref, refs):
    if len(refs) == 2:
        refs[1][...] = dot(hidden[...], grad_ref[...], ((0,), (0,))).astype(BF)
        return
    packed_ref = refs[0]
    groups, width = packed_ref.shape[0], grad_ref.shape[1]
    own_rows, parts = below_parts(packed_ref.shape, width // groups, width)
    step = max(1, 128 // own_rows)
    for start in range(0, groups, step):
        block = hidden[:, start * own_rows : (start + step) * own_rows]
        block = dot(block, grad_ref[...], ((0,), (0,))).astype(BF)
        for group in range(step):
            for row, count, column, size, own_row, own_column in parts:
                own_row += group * own_rows
                packed_ref[start + group, row : row + count, column : column + size] = block[
                    own_row : own_row + count, own_column : own_column + size
                ]


def sigmoid(value):
    return 1.0 / (1.0 + jnp.exp(-value))


def mlp_stage(ctx, serve, load, stream_ref, gain, new_ref, normed_ref, gu_ref, wgu, wd, own, part, comm):
    serve()
    own[...] = norm_forward(stream_ref[...], gain)
    gathered = gather_steps(ctx, own, normed_ref, *comm[:2])
    next(gathered)
    serve()
    wide, deep = load()
    next(gathered)
    serve()
    finish(gathered)
    serve()
    wait_all(wide)
    gu_ref[...] = dot(normed_ref[...], wgu[...])
    serve()
    half = gu_ref.shape[1] // 2
    gate, up = gu_ref[:, :half], gu_ref[:, half:]
    hidden = (gate * sigmoid(gate) * up).astype(BF)
    wait_all(deep)
    part[...] = dot(hidden, wd[...]).astype(BF)
    scattered = scatter_steps(ctx, part, stream_ref, new_ref, *comm[2:])
    next(scattered)
    serve()
    next(scattered)
    serve()
    finish(scattered)
    serve()


def mlp_forward_kernel(ctx, count, row, stream_ref, gains_ref, *refs):
    weights = refs[:count]
    new_ref, normed_ref, gu_ref, wgu, wd, own, part, sems, *comm = refs[count:]
    greet(neighbours(ctx))
    mlp_stage(
        ctx,
        lambda: None,
        lambda: load_pair(ctx, weights, wgu, wd, sems),
        stream_ref,
        gains_ref[row : row + 1],
        new_ref,
        normed_ref,
        gu_ref,
        wgu,
        wd,
        own,
        part,
        comm,
    )


def rope(value, tables, back=False):
    cosine, ahead, behind = tables
    width, half_dim = value.shape[1], HEAD_DIM // 2
    turned = pltpu.roll(value, width - half_dim, 1) * ahead[...]
    turned = turned + pltpu.roll(value, half_dim, 1) * behind[...]
    return value * cosine[...] + (-turned if back else turned)


def head_of(ref, index):
    return ref[:, index * HEAD_DIM : (index + 1) * HEAD_DIM]


def exact_dot(left, right, dims=((1,), (0,))):
    return lax.dot_general(
        left, right, (dims, ((), ())), precision=lax.Precision.HIGHEST, preferred_element_type=F32
    )


def build_tables(angle_ref, select_ref, tables, bias):
    width = tables[0].shape[1]
    for i, table in enumerate(tables):
        table[...] = exact_dot(angle_ref[...], select_ref[:, i * width : (i + 1) * width])
    lanes = lax.broadcasted_iota(jnp.int32, (8, angle_ref.shape[1]), 1)
    pick = jnp.where(lanes == HEAD_DIM, 1.0, 0.0)
    key_pos = exact_dot(pick, angle_ref[...], ((1,), (1,)))[:1]
    query_pos = angle_ref[:, HEAD_DIM : HEAD_DIM + 1]
    bias[...] = jnp.where(key_pos <= query_pos, 0.0, -1000000000.0)


def attn_stage(
    ctx, serve, load, prepare, stream_ref, gain, kept, new_ref, wq, wo, own, part, tables, bias, comm
):
    normed_ref, qkv_ref, att_ref, lse_ref = kept
    own[...] = norm_forward(stream_ref[...].astype(F32), gain)
    gathered = gather_steps(ctx, own, normed_ref, *comm[:2])
    next(gathered)
    wide, deep = load()
    next(gathered)
    prepare()
    finish(gathered)
    serve()
    wait_all(wide)
    qkv_ref[...] = rope(dot(normed_ref[...], wq[...]), tables).astype(BF)
    kv_heads = qkv_ref.shape[1] // (4 * HEAD_DIM)
    lane = lax.broadcasted_iota(jnp.int32, lse_ref.shape, 1)
    mixed, lse = [], jnp.zeros(lse_ref.shape, F32)
    for head in range(2 * kv_heads):
        query = head_of(qkv_ref, head)
        key = head_of(qkv_ref, 2 * kv_heads + head // 2)
        value = head_of(qkv_ref, 3 * kv_heads + head // 2)
        scores = dot(query, key, ((1,), (1,))) * HEAD_DIM ** (-0.5) + bias[...]
        top = jnp.max(scores, axis=1, keepdims=True)
        terms = jnp.exp(scores - top)
        total = jnp.sum(terms, axis=1, keepdims=True)
        probs = (terms * (1.0 / total)).astype(BF)
        mixed.append(dot(probs, value).astype(BF))
        lse = jnp.where(lane == head, top + jnp.log(total), lse)
    att_ref[...] = jnp.concatenate(mixed, axis=1)
    lse_ref[...] = lse
    wait_all(deep)
    part[...] = dot(att_ref[...], wo[...]).astype(BF)
    scattered = scatter_steps(ctx, part, stream_ref, new_ref, *comm[2:])
    next(scattered)
    serve()
    finish(scattered)
    serve()


def attn_forward_kernel(ctx, count, row, is_first, is_last, *refs):
    refs = list(refs)

    def take(on=True):
        return refs.pop(0) if on else None

    stream_ref, gains_ref = take(), take()
    sources = [take() for _ in range(3 if is_first else 2)]
    weights = [take() for _ in range(count)]
    new_ref, *kept = [take() for _ in range(5)]
    angles_out, top_out = take(is_first), take(is_first)
    next_normed = take(is_last)
    wq, wo, bias, own, part, *tables = [take() for _ in range(8)]
    sems = take()
    comm = [take() for _ in range(7)]
    extra = [take() for _ in range(4)]
    loaded = [take() for _ in sources]
    load_sems = take()
    select_ref, angle_ref, *top_ref = loaded
    loads = start_loads(sources, loaded, load_sems)
    greet(neighbours(ctx))

    def prepare():
        wait_all(loads)
        if is_first:
            finish(gather_steps(ctx, angle_ref, angles_out, *extra[:2]))
        build_tables(angles_out if is_first else angle_ref, select_ref, tables, bias)

    attn_stage(
        ctx,
        lambda: None,
        lambda: load_pair(ctx, weights, wq, wo, sems),
        prepare,
        stream_ref,
        gains_ref[row : row + 1],
        kept,
        new_ref,
        wq,
        wo,
        own,
        part,
        tables,
        bias,
        comm,
    )
    if is_first:
        finish(gather_steps(ctx, top_ref[0], top_out, *extra[2:]))
    if is_last:
        own[...] = norm_forward(new_ref[...], gains_ref[row + 1 : row + 2])
        finish(gather_steps(ctx, own, next_normed, *extra[2:]))


def z_stream(hops, gathers, counts):
    next(gathers[0])
    yield 0
    for done, (steps, count) in enumerate(zip(gathers, counts)):
        for turn in range(hops * count):
            next(steps)
            if turn == (hops - 1) * count - 1 and done + 1 < len(gathers):
                next(gathers[done + 1])
            yield done
        finish(steps)
        yield done + 1


def forward_kernel(ctx, shards, layers, *refs):
    refs = list(refs)

    def take(count):
        taken = refs[:count]
        del refs[:count]
        return taken

    last = layers - 1
    stream_ref, gains_ref = take(2)
    sources = take(3)
    (first_whole,) = take(1)
    pack_refs = take(2 * layers - 1)
    kept_out = [take(6) for _ in range(layers)]
    gate_out = [take(2) for _ in range(last)]
    common_out = take(2)
    whole_refs = take(2 * layers - 1)
    kept_refs = [take(6) for _ in range(layers)]
    gate_refs = [take(2) for _ in range(last)]
    angles_ref, tops_ref = common_refs = take(2)
    wq, wo, wgu, wd, bias, own, part = take(7)
    tables = take(3)
    attn_sems, mlp_sems, out_sems = take(3)
    comm, extra, loaded = take(7), take(4), take(3)
    (load_sems,) = take(1)
    lines = [take(3) for _ in pack_refs]
    select_ref, angle_ref, top_ref = loaded
    loads = start_loads(sources, loaded, load_sems)
    greet_line(ctx, shards)
    gathers, counts = [], []
    for pack_ref, whole_ref, line in zip(pack_refs, whole_refs, lines):
        parts = halves(pack_ref.shape[0])
        gathers.append(z_gather_steps(shards, parts, True, pack_ref, whole_ref, *line))
        counts.append(len(parts))
    stream = z_stream(shards - 1, gathers, counts)
    there, stored = [next(stream)], []

    def serve():
        there[0] = next(stream, there[0])

    def wait_for(number):
        while there[0] <= number:
            serve()

    def store(source, target):
        stored.append(pltpu.make_async_copy(source, target, out_sems.at[len(stored)]))
        stored[-1].start()

    def prepare():
        wait_all(loads)
        finish(gather_steps(ctx, angle_ref, angles_ref, *extra[:2]))
        build_tables(angles_ref, select_ref, tables, bias)
        store(angles_ref, common_out[0])

    for layer in range(layers):
        new_ref, *kept, next_normed = kept_refs[layer]

        def load_attn(layer=layer):
            if layer == 0:
                return load_pair(ctx, [first_whole], wq, wo, attn_sems)
            wait_for(2 * layer - 1)
            return load_pair(ctx, [whole_refs[2 * layer - 1]], wq, wo, attn_sems)

        def load_mlp(layer=layer):
            wait_for(2 * layer)
            return load_pair(ctx, [whole_refs[2 * layer]], wgu, wd, mlp_sems)

        attn_stage(
            ctx,
            serve,
            load_attn,
            prepare if layer == 0 else lambda: None,
            stream_ref,
            gains_ref[2 * layer : 2 * layer + 1],
            kept,
            new_ref,
            wq,
            wo,
            own,
            part,
            tables,
            bias,
            comm,
        )
        for source, target in zip(kept_refs[layer][:5], kept_out[layer]):
            store(source, target)
        if layer == 0:
            tops = gather_steps(ctx, top_ref, tops_ref, *extra[2:])
            next(tops)
            next(tops)
            serve()
            finish(tops)
            store(tops_ref, common_out[1])
            serve()
        gain = gains_ref[2 * layer + 1 : 2 * layer + 2]
        if layer < last:
            stream_ref, gu_ref = gate_refs[layer]
            mlp_stage(
                ctx,
                serve,
                load_mlp,
                new_ref,
                gain,
                stream_ref,
                next_normed,
                gu_ref,
                wgu,
                wd,
                own,
                part,
                comm,
            )
            for source, target in zip(gate_refs[layer], gate_out[layer]):
                store(source, target)
        else:
            own[...] = norm_forward(new_ref[...], gain)
            rows = gather_steps(ctx, own, next_normed, *extra[:2])
            next(rows)
            next(rows)
            serve()
            finish(rows)
        store(next_normed, kept_out[layer][5])
    wait_for(len(pack_refs) - 1)
    wait_all(stored)


def attn_backward_kernel(ctx, count, row, dh_ref, gains_ref, *refs):
    sources, refs = refs[:7], refs[7:]
    weights, outs = refs[:count], refs[count : 2 * count]
    new_dh, gain_grad, wq, wo, bias, own, grads, mixed, dproj, part, dy, sems = refs[
        2 * count : 2 * count + 12
    ]
    tables = refs[2 * count + 12 : 2 * count + 15]
    scratch = refs[2 * count + 15 : 2 * count + 22]
    loaded, load_sems = refs[2 * count + 22 : 2 * count + 29], refs[2 * count + 29]
    stream_ref, normed_ref, qkv_ref, att_ref, lse_ref, select_ref, angle_ref = loaded
    loads = start_loads(sources, loaded, load_sems)
    greet(neighbours(ctx))
    own[...] = dh_ref[...].astype(BF)
    gathered = gather_steps(ctx, own, grads, *scratch[:2])
    next(gathered)
    wide, deep = load_pair(ctx, weights, wq, wo, sems)
    next(gathered)
    wait_all(loads)
    build_tables(angle_ref, select_ref, tables, bias)
    finish(gathered)
    wait_all(deep)
    mixed[...] = dot(grads[...], wo[...], ((1,), (1,))).astype(BF)
    kv_heads = qkv_ref.shape[1] // (4 * HEAD_DIM)
    scale = HEAD_DIM ** (-0.5)
    dq, dk, dv = [], [0.0] * kv_heads, [0.0] * kv_heads
    for head in range(2 * kv_heads):
        group = head // 2
        query, grad = head_of(qkv_ref, head), head_of(mixed, head)
        key = head_of(qkv_ref, 2 * kv_heads + group)
        value = head_of(qkv_ref, 3 * kv_heads + group)
        scores = dot(query, key, ((1,), (1,))) * scale + bias[...]
        probs = jnp.exp(scores - lse_ref[:, head : head + 1])
        dprobs = dot(grad, value, ((1,), (1,)))
        inner = jnp.sum(probs * dprobs, axis=1, keepdims=True)
        dscores = (probs * (dprobs - inner)).astype(BF)
        dq.append(dot(dscores, key) * scale)
        dk[group] = dk[group] + dot(dscores, query, ((0,), (0,))) * scale
        dv[group] = dv[group] + dot(probs.astype(BF), grad, ((0,), (0,)))
    dproj[...] = rope(
        jnp.concatenate(dq + dk + dv, axis=1), tables, back=True
    ).astype(BF)
    wait_all(wide)
    part[...] = dot(dproj[...], wq[...], ((1,), (1,))).astype(BF)
    scattered = scatter_steps(ctx, part, None, dy, *scratch[2:])
    next(scattered)
    stored = store_gate_grad(ctx, normed_ref, dproj, outs)
    for _ in range(ctx // 2):
        next(stored)
    next(scattered)
    finish(stored)
    store_down_grad(ctx, att_ref, grads, outs)
    finish(scattered)
    dx, gain_grad[...] = norm_backward(
        dy[...], gains_ref[row : row + 1], stream_ref[...].astype(F32)
    )
    new_dh[...] = dh_ref[...].astype(F32) + dx


def gate_backward(gate, up, grad_hidden):
    sig = sigmoid(gate)
    silu = gate * sig
    grad_gate = grad_hidden * up * sig * (1.0 + gate * (1.0 - sig))
    return (silu * up).astype(BF), grad_gate.astype(BF), (grad_hidden * silu).astype(BF)


def mlp_backward_kernel(ctx, count, row, dh_ref, gains_ref, *refs):
    sources, refs = refs[:5], refs[5:]
    weights, outs = refs[:count], refs[count : 2 * count]
    new_dh, gain_grad, sum_out, wgu, wd, dgu, hidden, own, grads, part, dy, sems = refs[
        2 * count : 2 * count + 12
    ]
    scratch = refs[2 * count + 12 : 2 * count + 24]
    loaded, load_sems = refs[2 * count + 24 : 2 * count + 29], refs[2 * count + 29]
    normed_ref, gu_ref, stream_ref, sum_ref, base_ref = loaded
    loads = start_loads(sources, loaded, load_sems)
    greet(neighbours(ctx))
    own[...] = dh_ref[...].astype(BF)
    gathered = gather_steps(ctx, own, grads, *scratch[:2])
    summed = scatter_steps(ctx, sum_ref, base_ref, sum_out, *scratch[2:7])
    scattered = scatter_steps(ctx, part, None, dy, *scratch[7:])
    next(gathered)
    wide, deep = load_pair(ctx, weights, wgu, wd, sems)
    next(gathered)
    wait_all(loads)
    next(summed)
    finish(gathered)
    for copy in deep:
        copy.wait()
    half = gu_ref.shape[1] // 2
    grad_hidden = dot(grads[...], wd[...], ((1,), (1,)))
    hidden[...], dgu[:, :half], dgu[:, half:] = gate_backward(
        gu_ref[:, :half], gu_ref[:, half:], grad_hidden
    )
    next(summed)
    for copy in wide:
        copy.wait()
    part[...] = dot(dgu[...], wgu[...], ((1,), (1,))).astype(BF)
    next(scattered)
    finish(summed)
    stored = store_gate_grad(ctx, normed_ref, dgu, outs)
    for _ in range(ctx // 2):
        next(stored)
    next(scattered)
    finish(stored)
    store_down_grad(ctx, hidden, grads, outs)
    finish(scattered)
    dx, gain_grad[...] = norm_backward(
        dy[...], gains_ref[row : row + 1], stream_ref[...].astype(F32)
    )
    new_dh[...] = dh_ref[...].astype(F32) + dx


def mlp_last_kernel(ctx, count, *refs):
    sources, refs = refs[:2], refs[2:]
    weights, outs = refs[:count], refs[count : 2 * count]
    hidden, dgu, wgu, wd, gu, sems, normed_ref, grad_ref, load_sems = refs[2 * count :]
    loads = start_loads(sources, (normed_ref, grad_ref), load_sems)
    wide, deep = load_pair(ctx, weights, wgu, wd, sems)
    wait_all(loads)
    for copy in wide:
        copy.wait()
    gu[...] = dot(normed_ref[...], wgu[...])
    for copy in deep:
        copy.wait()
    half = gu.shape[1] // 2
    grad_hidden = dot(grad_ref[...], wd[...], ((1,), (1,)))
    hidden[...], dgu[:, :half], dgu[:, half:] = gate_backward(
        gu[:, :half], gu[:, half:], grad_hidden
    )
    finish(store_gate_grad(ctx, normed_ref, dgu, outs))
    store_down_grad(ctx, hidden, grad_ref, outs)


def mlp_ends_kernel(ctx, count, row, gains_ref, *refs):
    sources, weights, refs = refs[:4], refs[4 : 4 + count], refs[4 + count :]
    up_ref, new_dh, gain_grad, wgu, wd, part, dy, sems, *loaded = refs[:12]
    load_sems, scratch = refs[12], refs[13:]
    loads = start_loads(sources, loaded, load_sems)
    dgu_ref, hidden_ref, dh_ref, stream_ref = loaded
    greet(neighbours(ctx))
    wide, deep = load_pair(ctx, weights, wgu, wd, sems)
    wait_all(loads)
    wait_all(wide)
    part[...] = dot(dgu_ref[...], wgu[...], ((1,), (1,))).astype(BF)
    scattered = scatter_steps(ctx, part, None, dy, *scratch)
    next(scattered)
    for copy in deep:
        copy.wait()
    up_ref[...] = dot(hidden_ref[...], wd[...]).astype(BF)
    finish(scattered)
    dx, gain_grad[...] = norm_backward(
        dy[...], gains_ref[row : row + 1], stream_ref[...].astype(F32)
    )
    new_dh[...] = dh_ref[...].astype(F32) + dx


def local_call(kernel, out_shape, scratch, flops, hbm, *args):
    bytes_moved = sum(a.size * a.dtype.itemsize for a in args)
    bytes_moved += sum(a.size * a.dtype.itemsize for a in out_shape)
    spaces = [pl.ANY if hbm[0] <= i <= hbm[1] else pltpu.VMEM for i in range(len(args))]
    return pl.pallas_call(
        kernel,
        out_shape=out_shape,
        in_specs=[pl.BlockSpec(memory_space=space) for space in spaces],
        out_specs=[pl.BlockSpec(memory_space=pltpu.VMEM) for _ in out_shape],
        scratch_shapes=scratch,
        cost_estimate=pl.CostEstimate(flops=flops, bytes_accessed=bytes_moved, transcendentals=0),
        compiler_params=pltpu.CompilerParams(vmem_limit_bytes=VMEM_LIMIT),
    )(*args)


def weight_set(packed, width):
    ctx = lax.axis_size("ctx")
    groups, _, columns = packed.shape
    kind, rows = fold(columns, width), width // (ctx * groups)
    if kind != "cut" and rows % 16 == 0:
        return (packed,)
    return spread(packed, width)


def weight_scratch(weights, width):
    ctx = lax.axis_size("ctx")
    columns = weights[0].shape[-1]
    if len(weights) == 2:
        return [pltpu.VMEM(w.shape, BF) for w in weights], pltpu.SemaphoreType.DMA((2,))
    groups, rows, _ = weights[0].shape
    own_rows, parts = below_parts(weights[0].shape, width // groups, width)
    return [
        pltpu.VMEM((width, columns), BF),
        pltpu.VMEM((own_rows * groups, width), BF),
    ], pltpu.SemaphoreType.DMA((groups * (ctx + len(parts)),))


def comm_scratch(ctx, own, width):
    return [
        *pair_of_sems(),
        *scatter_scratch(ctx, own, width),
        *pair_of_sems(),
    ]


def kernel_id(kind, layer):
    return 16 + 8 * layer + kind


def mlp_forward_call(layer, stream, gains, weights):
    ctx = lax.axis_size("ctx")
    own, width = stream.shape
    rows, columns = ctx * own, weights[0].shape[-1]
    scratch, sems = weight_scratch(weights, width)
    return remote_call(
        functools.partial(mlp_forward_kernel, ctx, len(weights), 2 * layer + 1),
        [shape_of((own, width), F32), shape_of((rows, width)), shape_of((rows, columns), F32)],
        [
            *scratch,
            pltpu.VMEM((own, width), BF),
            pltpu.VMEM((rows, width), BF),
            sems,
            *comm_scratch(ctx, own, width),
        ],
        len(weights),
        kernel_id(0, layer),
        stream,
        gains,
        *weights,
    )


def attn_forward_call(layer, stream, gains, weights, tables, top, is_last):
    ctx = lax.axis_size("ctx")
    own, width = stream.shape
    rows, columns = ctx * own, weights[0].shape[-1]
    scratch, sems = weight_scratch(weights, width)
    is_first = top is not None
    loaded = [*tables, top] if is_first else list(tables)
    outs = remote_call(
        functools.partial(
            attn_forward_kernel, ctx, len(weights), 2 * layer, is_first, is_last
        ),
        [
            shape_of((own, width), F32),
            shape_of((rows, width)),
            shape_of((rows, columns)),
            shape_of((rows, columns // 2)),
            shape_of((rows, 128), F32),
            *([shape_of((rows, 128), F32), shape_of((rows, width))] if is_first else []),
            *([shape_of((rows, width))] if is_last else []),
        ],
        [
            *scratch,
            pltpu.VMEM((rows, rows), F32),
            pltpu.VMEM((own, width), BF),
            pltpu.VMEM((rows, width), BF),
            *[pltpu.VMEM((rows, columns), F32)] * 3,
            sems,
            *comm_scratch(ctx, own, width),
            *pair_of_sems(),
            *pair_of_sems(),
            *load_scratch(loaded),
        ],
        len(loaded) + len(weights),
        kernel_id(1, layer),
        stream,
        gains,
        *loaded,
        *weights,
    )
    return outs[0], outs[1:5], outs[5:]


def forward_call(stream, gains, tables, top, whole, attn_packs, mlp_packs):
    ctx, shards, layers = lax.axis_size("ctx"), lax.axis_size("shard"), len(mlp_packs)
    own, width = stream.shape
    rows, columns, gate_columns = ctx * own, whole.shape[2], mlp_packs[0].shape[1]
    packs = [mlp_packs[0]]
    for layer in range(1, layers):
        packs += [attn_packs[layer], mlp_packs[layer]]
    attn_scratch, attn_sems = weight_scratch([whole], width)
    mlp_scratch, mlp_sems = weight_scratch(
        [shape_of((2 * shards,) + mlp_packs[0].shape)], width
    )
    kept = [
        shape_of((own, width), F32),
        shape_of((rows, width)),
        shape_of((rows, columns)),
        shape_of((rows, columns // 2)),
        shape_of((rows, 128), F32),
        shape_of((rows, width)),
    ]
    gate_kept = [shape_of((own, width), F32), shape_of((rows, gate_columns), F32)]
    common = [shape_of((rows, 128), F32), shape_of((rows, width))]
    outs = kept * layers + gate_kept * (layers - 1) + common
    wholes = [shape_of((2 * shards,) + pack.shape) for pack in packs]
    loaded = [*tables, top]
    results = remote_call(
        functools.partial(forward_kernel, ctx, shards, layers),
        outs + wholes,
        [
            *[pltpu.VMEM(out.shape, out.dtype) for out in outs],
            *attn_scratch,
            *mlp_scratch,
            pltpu.VMEM((rows, rows), F32),
            pltpu.VMEM((own, width), BF),
            pltpu.VMEM((rows, width), BF),
            *[pltpu.VMEM((rows, columns), F32)] * 3,
            attn_sems,
            mlp_sems,
            pltpu.SemaphoreType.DMA((len(outs),)),
            *comm_scratch(ctx, own, width),
            *pair_of_sems(),
            *pair_of_sems(),
            *load_scratch(loaded),
            *line_sems(shards) * len(packs),
        ],
        len(loaded) + 1 + len(packs),
        kernel_id(5, 0),
        stream,
        gains,
        *loaded,
        whole,
        *packs,
        hbm_out=len(outs) + len(wholes),
    )
    per_layer = [results[6 * layer : 6 * layer + 6] for layer in range(layers)]
    results = results[6 * layers :]
    gates = [results[2 * layer : 2 * layer + 2] for layer in range(layers - 1)]
    return per_layer, gates, results[2 * layers - 2 : 2 * layers], results[2 * layers :]


def attn_backward_call(layer, grad_stream, stream, gains, kept, weights, tables):
    ctx = lax.axis_size("ctx")
    own, width = stream.shape
    rows, columns = ctx * own, weights[0].shape[-1]
    scratch, sems = weight_scratch(weights, width)
    loaded = [stream, *kept, *tables]
    *outs, new_dh, gain_grad = remote_call(
        functools.partial(attn_backward_kernel, ctx, len(weights), 2 * layer),
        [
            *[shape_of(weight.shape) for weight in weights],
            shape_of((own, width), F32),
            shape_of((1, width), F32),
        ],
        [
            *scratch,
            pltpu.VMEM((rows, rows), F32),
            pltpu.VMEM((own, width), BF),
            pltpu.VMEM((rows, width), BF),
            pltpu.VMEM((rows, columns // 2), BF),
            pltpu.VMEM((rows, columns), BF),
            pltpu.VMEM((rows, width), BF),
            pltpu.VMEM((own, width), F32),
            sems,
            *[pltpu.VMEM((rows, columns), F32)] * 3,
            *comm_scratch(ctx, own, width),
            *load_scratch(loaded),
        ],
        len(loaded) + len(weights),
        kernel_id(2, layer),
        grad_stream,
        gains,
        *loaded,
        *weights,
    )
    return packed_grads(outs), new_dh, gain_grad[0]


def packed_grads(outs):
    return outs[0] if len(outs) == 1 else pack_grads(*outs)


def remote_call(kernel, out_shape, scratch, hbm, collective_id, *args, hbm_out=0):
    spaces = [pltpu.VMEM] * (len(args) - hbm) + [pl.ANY] * hbm
    out_spaces = [pltpu.VMEM] * (len(out_shape) - hbm_out) + [pl.ANY] * hbm_out
    return pl.pallas_call(
        kernel,
        out_shape=out_shape,
        in_specs=[pl.BlockSpec(memory_space=space) for space in spaces],
        out_specs=[pl.BlockSpec(memory_space=space) for space in out_spaces],
        scratch_shapes=scratch,
        compiler_params=pltpu.CompilerParams(
            collective_id=collective_id, has_side_effects=True, vmem_limit_bytes=VMEM_LIMIT
        ),
    )(*args)


def prologue_call(gains, weights, pieces):
    ctx, shards = lax.axis_size("ctx"), lax.axis_size("shard")
    layers = weights[0].shape[0]
    tile = (-(-2 * layers // 8) * 8, 128)
    groups = 2 * shards
    stage, cuts, packs = [], [], []
    for _ in range(layers):
        for kind in range(2):
            wide, deep = weights[2 * kind], weights[2 * kind + 1]
            rows, columns = wide.shape[1] // 2, wide.shape[2] // ctx
            below = deep.shape[1] // 2 * deep.shape[2] // columns
            stage += [
                pltpu.VMEM((rows, wide.shape[2]), F32),
                pltpu.VMEM((deep.shape[1] // 2, deep.shape[2]), F32),
            ]
            cuts.append(pltpu.VMEM((ctx, rows, columns), BF))
            packs.append(shape_of((ctx * rows + below, columns)))
    swaps = 2 * layers * (ctx - 1)
    outs = pl.pallas_call(
        functools.partial(prologue_kernel, ctx, shards, layers, pieces),
        out_shape=[
            shape_of((tile[0], ctx * shards * gains.shape[2]), F32),
            shape_of((groups,) + packs[0].shape),
            *packs,
        ],
        in_specs=[pl.BlockSpec(memory_space=pltpu.VMEM)] + [pl.BlockSpec(memory_space=pl.ANY)] * 4,
        out_specs=[
            pl.BlockSpec(memory_space=pltpu.VMEM),
            pl.BlockSpec(memory_space=pl.ANY),
            *[pl.BlockSpec(memory_space=pltpu.VMEM) for _ in packs],
        ],
        scratch_shapes=[
            *stage,
            *cuts,
            pltpu.VMEM(tile, F32),
            pltpu.VMEM((ctx, shards) + tile, F32),
            pltpu.SemaphoreType.DMA((4 * layers,)),
            pltpu.SemaphoreType.DMA((swaps,)),
            pltpu.SemaphoreType.DMA((swaps,)),
            pltpu.SemaphoreType.DMA((ctx + shards + 1,)),
            pltpu.SemaphoreType.DMA((ctx + shards + 1,)),
            *line_sems(shards),
        ],
        compiler_params=pltpu.CompilerParams(
            collective_id=13, has_side_effects=True, vmem_limit_bytes=VMEM_LIMIT
        ),
    )(gains, *weights)
    return outs[0], outs[1], list(outs[2::2]), list(outs[3::2])


def load_scratch(args):
    return [
        *[pltpu.VMEM(arg.shape, arg.dtype) for arg in args],
        pltpu.SemaphoreType.DMA((len(args),)),
    ]


def pair_of_sems():
    return [pltpu.SemaphoreType.DMA((8,)), pltpu.SemaphoreType.DMA((8,))]


def mlp_backward_call(layer, grad_stream, stream, gains, normed, gate_up, weights, summed, base):
    ctx = lax.axis_size("ctx")
    rows, width = normed.shape
    own = base.shape[0]
    columns = weights[0].shape[-1]
    scratch, sems = weight_scratch(weights, width)
    loaded = [normed, gate_up, stream, summed, base]
    *outs, new_dh, gain_grad, total = remote_call(
        functools.partial(mlp_backward_kernel, ctx, len(weights), 2 * layer + 1),
        [
            *[shape_of(weight.shape) for weight in weights],
            shape_of((own, width), F32),
            shape_of((1, width), F32),
            shape_of((own, width)),
        ],
        [
            *scratch,
            pltpu.VMEM((rows, columns), BF),
            pltpu.VMEM((rows, columns // 2), BF),
            pltpu.VMEM((own, width), BF),
            pltpu.VMEM((rows, width), BF),
            pltpu.VMEM((rows, width), BF),
            pltpu.VMEM((own, width), F32),
            sems,
            *pair_of_sems(),
            *scatter_scratch(ctx, own, width),
            *pair_of_sems(),
            *scatter_scratch(ctx, own, width),
            *pair_of_sems(),
            *load_scratch(loaded),
        ],
        len(loaded) + len(weights),
        kernel_id(3, layer),
        grad_stream,
        gains,
        *loaded,
        *weights,
    )
    return packed_grads(outs), new_dh, gain_grad[0], total


def mlp_last_call(normed, weights, grad_mlp):
    rows, width = normed.shape
    columns = weights[0].shape[-1]
    scratch, sems = weight_scratch(weights, width)
    *outs, hidden, grad_gate_up = local_call(
        functools.partial(mlp_last_kernel, lax.axis_size("ctx"), len(weights)),
        [
            *[shape_of(weight.shape) for weight in weights],
            shape_of((rows, columns // 2)),
            shape_of((rows, columns)),
        ],
        [*scratch, pltpu.VMEM((rows, columns), F32), sems, *load_scratch((normed, grad_mlp))],
        6 * rows * width * columns,
        (0, 1 + len(weights)),
        normed,
        grad_mlp,
        *weights,
    )
    return packed_grads(outs), hidden, grad_gate_up


def mlp_ends_call(layer, hidden, grad_gate_up, grad_stream, stream, gains, weights):
    ctx = lax.axis_size("ctx")
    rows, columns = grad_gate_up.shape
    own, width = stream.shape
    scratch, sems = weight_scratch(weights, width)
    loaded = [grad_gate_up, hidden, grad_stream, stream]
    part, new_dh, gain_grad = remote_call(
        functools.partial(mlp_ends_kernel, ctx, len(weights), 2 * layer + 1),
        [shape_of((rows, width)), shape_of((own, width), F32), shape_of((1, width), F32)],
        [
            *scratch,
            pltpu.VMEM((rows, width), BF),
            pltpu.VMEM((own, width), F32),
            sems,
            *load_scratch(loaded),
            *scatter_scratch(ctx, own, width),
            *pair_of_sems(),
        ],
        len(loaded) + len(weights),
        kernel_id(4, layer),
        gains,
        *loaded,
        *weights,
    )
    return part, new_dh, gain_grad[0]


def adam_kernel(rate, decay, kept, pieces, w_ref, m_ref, v_ref, g_ref, *refs):
    new_w, new_m, new_v = refs[kept:]
    if w_ref.shape[-1] == g_ref.shape[-1]:
        grad = g_ref[...].astype(F32).reshape(w_ref.shape)
    else:
        grad = from_members(g_ref[...].astype(F32), pieces)[None]
    new_w[...], new_m[...], new_v[...] = adam_step(
        w_ref[...], m_ref[...], v_ref[...], grad, rate, decay
    )


def adam_layer(layer, slot, weight, moment, square, grad, done, pieces):
    _, rows, columns = weight.shape
    if len(pieces) == 3:
        members, _, width = grad.shape
        parts = 2 if rows % 16 == 0 else 1
        grid = (1, parts)
        grad_spec = pl.BlockSpec((members, rows // parts, width), lambda i, j: (0, j, 0))
        spec = pl.BlockSpec((1, rows // parts, columns), lambda i, j: (layer, j, 0))
    elif len(pieces) == 2:
        members, _, both = grad.shape
        grid, width = (2, members), both // 2
        grad_spec = pl.BlockSpec((1, rows, width), lambda i, j: (j, 0, i))
        spec = pl.BlockSpec((1, rows, width), lambda i, j: (layer, 0, i * members + j))
    else:
        grid, width = (1, 3), columns // 3
        grad_spec = pl.BlockSpec((rows, width), lambda i, j: (0, j))
        spec = pl.BlockSpec((1, rows, width), lambda i, j: (layer, 0, j))
    kept = [] if done is None else list(done)
    size = rows * columns
    return pl.pallas_call(
        functools.partial(adam_kernel, RATES[slot], DECAYS[slot], len(kept), pieces),
        grid=grid,
        out_shape=[shape_of(weight.shape, F32)] * 3,
        in_specs=[spec, spec, spec, grad_spec] + [pl.BlockSpec(memory_space=pl.ANY)] * len(kept),
        out_specs=[spec] * 3,
        input_output_aliases={4 + i: i for i in range(len(kept))},
        cost_estimate=pl.CostEstimate(
            flops=20 * size, bytes_accessed=26 * size, transcendentals=size
        ),
        compiler_params=pltpu.CompilerParams(vmem_limit_bytes=SMALL_LIMIT),
    )(weight, moment, square, grad, *kept)


def in_order(first, then):
    return lax.optimization_barrier((first, then))


def half_rows(shard):
    half = shard.shape[0] // 2
    return lax.dynamic_slice_in_dim(shard, lax.axis_index("dp") * half, half, axis=0)


def member_parts(shard, pieces, ctx):
    parts = []
    for member in range(ctx):
        cut, start = [], 0
        for width in pieces:
            own = width // ctx
            cut.append(shard[:, start + member * own : start + (member + 1) * own])
            start += width
        parts.append(jnp.concatenate(cut, axis=1))
    return parts


def by_member(shard, pieces):
    return jnp.stack(member_parts(shard, pieces, lax.axis_size("ctx")))


def from_members(parts, pieces):
    ctx = parts.shape[0]
    out, start = [], 0
    for width in pieces:
        out += [parts[i, :, start : start + width // ctx] for i in range(ctx)]
        start += width // ctx
    return jnp.concatenate(out, axis=1)


def fold(columns, width):
    if width % columns == 0:
        return "even"
    return "bent" if columns > width and width % (columns - width) == 0 else "cut"


def pack(wide, rows_part):
    columns, (m, width) = wide.shape[1], rows_part.shape
    kind = fold(columns, width)
    if kind == "bent":
        rest = columns - width
        whole = m * width // columns
        right = [rows_part[whole:, i * rest : (i + 1) * rest] for i in range(width // rest)]
        below = jnp.concatenate([rows_part[:whole], jnp.concatenate(right, axis=0)], axis=1)
        return jnp.concatenate([wide, below], axis=0)
    unit = math.gcd(columns, width)
    below = jnp.concatenate(jnp.split(rows_part, width // unit, axis=1), axis=0)
    below = jnp.concatenate(jnp.split(below, columns // unit, axis=0), axis=1)
    return jnp.concatenate([wide, below], axis=0)


def unpack(packed, count, width):
    columns = packed.shape[-1]
    wide, below = packed[..., :count, :], packed[..., count:, :]
    kind = fold(columns, width)
    if kind == "bent":
        rest = columns - width
        right = jnp.split(below[..., width:], width // rest, axis=-2)
        return wide, jnp.concatenate(
            [below[..., :width], jnp.concatenate(right, axis=-1)], axis=-2
        )
    unit = math.gcd(columns, width)
    below = jnp.concatenate(jnp.split(below, columns // unit, axis=-1), axis=-2)
    return wide, jnp.concatenate(jnp.split(below, width // unit, axis=-2), axis=-1)


def pack_share(member_parts, rows_part):
    ctx, rows, columns = member_parts.shape
    return pack(member_parts.reshape(ctx * rows, columns), rows_part)


def spread(whole, width):
    ctx = lax.axis_size("ctx")
    groups, _, columns = whole.shape
    rows = width // (ctx * groups)
    wide, rows_whole = unpack(whole, ctx * rows, width)
    wide = jnp.transpose(wide.reshape(groups, ctx, rows, columns), (1, 0, 2, 3))
    return wide.reshape(-1, columns), rows_whole.reshape(-1, width)


def pack_grads(wide, rows_part):
    ctx, shards = lax.axis_size("ctx"), lax.axis_size("shard")
    columns, width = wide.shape[1], rows_part.shape[1]
    groups = shards * 2
    rows = wide.shape[0] // (ctx * groups)
    wide = jnp.transpose(wide.astype(BF).reshape(ctx, groups, rows, columns), (1, 0, 2, 3))
    wide = wide.reshape(groups, ctx * rows, columns)
    return jax.vmap(pack)(wide, rows_part.astype(BF).reshape(groups, -1, width))


def reduce_grads(packed):
    return lax.psum_scatter(
        packed.reshape(-1, packed.shape[-1]), ("shard", "dp"), scatter_dimension=0, tiled=True
    )


def share_grads(mine, width, collective_id):
    ctx, groups = lax.axis_size("ctx"), lax.axis_size("shard") * 2
    columns = mine.shape[1]
    rows = width // (ctx * groups)
    deep = (mine.shape[0] - ctx * rows) * columns // width
    sums = (mine,)
    if fold(columns, width) == "cut" or rows % 16:
        wide, rows_part = unpack(mine, ctx * rows, width)
        sums = (wide.reshape(ctx, rows, columns), rows_part)
    wide, rows_part = share_plane(sums, ((rows, columns), (deep, width)), collective_id)
    return wide.reshape(ctx, 2 * rows, columns), rows_part.reshape(-1, width)


def rope_select(ctx):
    half_dim = HEAD_DIM // 2
    columns = (HEADS + 2 * KV_HEADS) * HEAD_DIM // ctx
    turned = (HEADS + KV_HEADS) * HEAD_DIM // ctx
    select = np.zeros((3, 128, columns), np.float32)
    for column in range(columns):
        place = column % HEAD_DIM
        if column >= turned:
            select[0, HEAD_DIM + 1, column] = 1.0
        elif place < half_dim:
            select[0, place, column] = 1.0
            select[1, half_dim + place, column] = -1.0
        else:
            select[0, place - half_dim, column] = 1.0
            select[2, place, column] = 1.0
    return np.concatenate(list(select), axis=1)


def body(
    tokens,
    cotangent,
    positions,
    w_qkv,
    w_out,
    w_gate_up,
    w_down,
    norm_gains,
    first_qkv,
    first_out,
    first_gate_up,
    first_down,
    first_gains,
    second_qkv,
    second_out,
    second_gate_up,
    second_down,
    second_gains,
):
    ctx, shards = lax.axis_size("ctx"), lax.axis_size("shard")
    layer_count, own_width, width = w_qkv.shape[0], norm_gains.shape[2], tokens.shape[2]
    width_q, width_kv = HEADS * HEAD_DIM, KV_HEADS * HEAD_DIM
    qkv_pieces, gate_pieces = (width_q, width_kv, width_kv), (FF, FF)
    rows = tokens.shape[1]
    last = layer_count - 1

    lined = shards == 4 and width // (ctx * shards * 2) % 16 == 0
    attn_packs, mlp_packs = [None] * layer_count, [None] * layer_count
    attn_sets, mlp_sets = [None] * layer_count, [None] * layer_count
    if lined:
        gains, whole, attn_packs, mlp_packs = prologue_call(
            norm_gains, (w_qkv, w_out, w_gate_up, w_down), (qkv_pieces, gate_pieces)
        )
        attn_sets[0] = (whole,)
    else:
        tile = norm_gains.astype(BF).astype(F32).reshape(2 * layer_count, own_width)
        tile = jnp.pad(tile, ((0, -2 * layer_count % 8), (0, -own_width % 128)))
        gains = jnp.transpose(small_gather(tile)[..., :own_width], (2, 0, 1, 3))
        gains = gains.reshape(-1, width)
        for layer in range(layer_count):
            parts = by_member(half_rows(w_qkv[layer]).astype(BF), qkv_pieces)
            packed = pack_share(swap_ctx(parts, 2), half_rows(w_out[layer]).astype(BF))
            packed = lax.all_gather(packed, ("shard", "dp"), axis=0)
            attn_sets[layer] = weight_set(packed, width)
            parts = by_member(half_rows(w_gate_up[layer]).astype(BF), gate_pieces)
            packed = pack_share(swap_ctx(parts, 3), half_rows(w_down[layer]).astype(BF))
            packed = lax.all_gather(packed, ("shard", "dp"), axis=0)
            mlp_sets[layer] = weight_set(packed, width)

    angles = rope_angles(positions[0])
    position = positions[0].astype(F32)[:, None]
    angles = jnp.concatenate(
        [jnp.cos(angles), jnp.sin(angles), position, jnp.ones_like(position)], axis=1
    )
    angles = jnp.pad(angles, ((0, 0), (0, 128 - angles.shape[1])))
    select = jnp.asarray(rope_select(ctx))

    stream, grad_stream = tokens[0], cotangent[0]
    saved = []
    if lined:
        per_layer, gates, (angles, grad_top), wholes = forward_call(
            stream, gains, (select, angles), cotangent[0], whole, attn_packs, mlp_packs
        )
        for layer in range(layer_count):
            middle, *kept, normed_two = per_layer[layer]
            saved.append([stream, middle, kept, normed_two])
            mlp_sets[layer] = (wholes[2 * layer],)
            if layer < last:
                stream, gate_up = gates[layer]
                saved[-1].append(gate_up)
                attn_sets[layer + 1] = (wholes[2 * layer + 1],)
    else:
        for layer in range(layer_count):
            middle, kept, more = attn_forward_call(
                layer,
                stream,
                gains,
                attn_sets[layer],
                (select, angles),
                cotangent[0] if layer == 0 else None,
                layer == last,
            )
            saved.append([stream, middle, kept])
            if layer == 0:
                angles, grad_top = more[:2]
            if layer == last:
                saved[-1].append(more[-1])
            else:
                stream, *gate_kept = mlp_forward_call(layer, middle, gains, mlp_sets[layer])
                saved[-1] += gate_kept
    tables = (select, angles)

    params = (w_qkv, w_out, w_gate_up, w_down)
    firsts = (first_qkv, first_out, first_gate_up, first_down)
    seconds = (second_qkv, second_out, second_gate_up, second_down)
    updated = [None] * 4

    def step(layer, slots, grads, pieces):
        for slot, grad, cut in zip(slots, grads, (pieces, ())):
            updated[slot] = adam_layer(
                layer, slot, params[slot], firsts[slot], seconds[slot], grad, updated[slot], cut
            )

    def step_mlp(layer, mine):
        step(layer, (2, 3), share_grads(mine, width, 4), gate_pieces)

    def step_attn(layer, mine):
        step(layer, (0, 1), share_grads(mine, width, 5), qkv_pieces)

    def sum_gains(gain_grads):
        gain_tiles = jnp.stack(gain_grads).reshape(2 * layer_count, ctx, shards, own_width)
        gain_tiles = jnp.transpose(gain_tiles, (2, 1, 0, 3))
        gain_tiles = jnp.pad(
            gain_tiles, ((0, 0), (0, 0), (0, -2 * layer_count % 8), (0, -own_width % 128))
        )
        return small_reduce(gain_tiles)[: 2 * layer_count, :own_width].reshape(norm_gains.shape)

    attn_mine, mlp_mine = [None] * layer_count, [None] * layer_count
    gain_grads = [None] * layer_count
    for layer in reversed(range(layer_count)):
        before, middle, kept, normed_two = saved[layer][:4]
        if layer == last:
            packed, hidden, dgu = mlp_last_call(normed_two, mlp_sets[layer], grad_top)
            packed, (hidden, dgu) = in_order(packed, (hidden, dgu))
            up_part, grad_stream, grad_g2 = mlp_ends_call(
                layer, hidden, dgu, grad_stream, middle, gains, mlp_sets[layer]
            )
        else:
            packed, grad_stream, grad_g2, total = mlp_backward_call(
                layer,
                grad_stream,
                middle,
                gains,
                normed_two,
                saved[layer][4],
                mlp_sets[layer],
                up_part,
                saved[last][1],
            )
            if layer == last - 1:
                output = total
        mlp_mine[layer] = reduce_grads(packed)
        if layer < last:
            mlp_mine[layer + 1], grad_stream = in_order(mlp_mine[layer + 1], grad_stream)
        packed, grad_stream, grad_g1 = attn_backward_call(
            layer, grad_stream, before, gains, kept, attn_sets[layer], tables
        )
        gain_grads[layer] = jnp.stack([grad_g1, grad_g2])
        if layer == 0:
            gain_grad = sum_gains(gain_grads)
        if layer < last:
            packed, mine = in_order(packed, (mlp_mine[layer + 1], attn_mine[layer + 1]))
            step_mlp(layer + 1, mine[0])
            step_attn(layer + 1, mine[1])
            (updated, gain_grad), (mlp_mine[layer], packed) = in_order(
                (updated, gain_grad), (mlp_mine[layer], packed)
            )
        attn_mine[layer] = reduce_grads(packed)
    step_mlp(0, mlp_mine[0])
    updated, mine = in_order(updated, attn_mine[0])
    step_attn(0, mine)

    updated = list(updated)
    updated.append(
        adam_step(norm_gains, first_gains, second_gains, gain_grad, RATES[4], DECAYS[4])
    )
    return (
        output[None],
        grad_stream[None],
        *[updated[slot][0] for slot in range(5)],
        *[updated[slot][1] for slot in range(5)],
        *[updated[slot][2] for slot in range(5)],
    )


def solution(mesh):
    rows = P(("dp", "shard"), "ctx", None)
    weight = P(None, ("ctx", "shard"), None)
    gain = P(None, None, ("ctx", "shard"))
    group = (weight, weight, weight, weight, gain)
    return jax.shard_map(
        body,
        mesh=mesh,
        in_specs=(rows, rows, P(("dp", "shard"), "ctx"), *group, *group, *group),
        out_specs=(rows, rows, *group, *group, *group),
        check_vma=False,
    )
```

```python
import functools
import math

import jax
import jax.numpy as jnp
import numpy as np
from jax import lax
from jax.experimental import pallas as pl
from jax.experimental.pallas import tpu as pltpu
from jax.sharding import PartitionSpec as P

HEADS = 16
KV_HEADS = 8
HEAD_DIM = 96
FF = 4096
STEP = 10


NORM_EPS = 1e-05
ROPE_BASE = 100000.0
BETA_ONE = 0.9
BETA_TWO = 0.95
ADAM_EPS = 1e-08
DECAY_RATE = 0.1
RATES = (0.05, 1.0, 0.05, 0.03, 0.8)
DECAYS = (DECAY_RATE, DECAY_RATE, DECAY_RATE, DECAY_RATE, 0.0)

BF = jnp.bfloat16
F32 = jnp.float32


def dot(left, right, dims=((1,), (0,))):
    return lax.dot_general(left, right, (dims, ((), ())), preferred_element_type=F32)


def rope_angles(positions):
    powers = 2.0 * np.arange(HEAD_DIM // 2) / HEAD_DIM
    inverse_freq = np.exp(-np.log(ROPE_BASE) * powers).astype(np.float32)
    return positions.astype(F32)[:, None] * inverse_freq[None, :]


def norm_forward(stream, gain):
    inverse = lax.rsqrt(jnp.mean(stream * stream, axis=-1, keepdims=True) + NORM_EPS)
    return (stream * inverse * gain).astype(BF)


def norm_backward(grad_out, gain, stream):
    inverse = lax.rsqrt(jnp.mean(stream * stream, axis=-1, keepdims=True) + NORM_EPS)
    normal_part = stream * inverse
    scaled = grad_out * gain
    gain_grad = jnp.sum(grad_out * normal_part, axis=0, keepdims=True)
    grad_in = inverse * (
        scaled - normal_part * jnp.mean(scaled * normal_part, axis=-1, keepdims=True)
    )
    return (grad_in, gain_grad)


def adam_step(weight, moment, square, grad, rate, decay):
    moment = BETA_ONE * moment + (1.0 - BETA_ONE) * grad
    square = BETA_TWO * square + (1.0 - BETA_TWO) * grad * grad
    moment_hat = moment * (rate / (1.0 - BETA_ONE**STEP))
    square_hat = square * (1.0 / (1.0 - BETA_TWO**STEP))
    weight = weight * (1.0 - rate * decay) - moment_hat / (jnp.sqrt(square_hat) + ADAM_EPS)
    return (weight, moment, square)


MESH = pl.DeviceIdType.MESH
VMEM_LIMIT = 61 * 1024 * 1024
SMALL_LIMIT = 24 * 1024 * 1024


def remote(src, dst, sems, slot, target):
    send, recv = sems
    return pltpu.make_async_remote_copy(
        src_ref=src,
        dst_ref=dst,
        send_sem=send.at[slot],
        recv_sem=recv.at[slot],
        device_id=target,
        device_id_type=MESH,
    )


def greet(targets):
    barrier = pltpu.get_barrier_semaphore()
    for target in targets:
        pl.semaphore_signal(barrier, inc=1, device_id=target, device_id_type=MESH)
    pl.semaphore_wait(barrier, len(targets))


def ctx_peers(ctx):
    me = lax.axis_index("ctx")
    return [{"ctx": lax.rem(me + step, ctx)} for step in range(1, ctx)]


def square():
    me = lax.axis_index("ctx")
    x, y = lax.rem(me, 2), me // 2
    return me, 2 * y + 1 - x, 2 * (1 - y) + x, 3 - me


def neighbours(ctx):
    if ctx != 4:
        return ctx_peers(ctx)
    _, xn, yn, _ = square()
    return [{"ctx": xn}, {"ctx": yn}]


def gather_steps(ctx, x_ref, o_ref, send, recv):
    rows = x_ref.shape[0]
    sems = (send, recv)

    def block(owner, part=None):
        if part is None:
            return pl.ds(pl.multiple_of(owner * rows, rows), rows)
        return pl.ds(pl.multiple_of(owner * rows + part * (rows // 2), rows // 2), rows // 2)

    if ctx != 4:
        me = lax.axis_index("ctx")
        copies = [
            remote(x_ref, o_ref.at[block(me)], sems, i, peer)
            for i, peer in enumerate(ctx_peers(ctx))
        ]
        for copy in copies:
            copy.start()
        o_ref[block(me), :] = x_ref[...]
        yield
        yield
        for copy in copies:
            copy.wait()
        return
    me, xn, yn, _ = square()
    to_x, to_y = {"ctx": xn}, {"ctx": yn}
    half = rows // 2
    low, high = pl.ds(0, half), pl.ds(half, half)
    first = remote(x_ref.at[low], o_ref.at[block(me, 0)], sems, 0, to_x)
    second = remote(x_ref.at[high], o_ref.at[block(me, 1)], sems, 1, to_y)
    third = remote(x_ref.at[high], o_ref.at[block(me, 1)], sems, 2, to_x)
    fourth = remote(x_ref.at[low], o_ref.at[block(me, 0)], sems, 3, to_y)
    first.start()
    second.start()
    third.start()
    fourth.start()
    o_ref[block(me), :] = x_ref[...]
    yield
    first.wait_recv()
    fifth = remote(o_ref.at[block(xn, 0)], o_ref.at[block(xn, 0)], sems, 4, to_y)
    fifth.start()
    second.wait_recv()
    sixth = remote(o_ref.at[block(yn, 1)], o_ref.at[block(yn, 1)], sems, 5, to_x)
    sixth.start()
    yield
    first.wait_send()
    second.wait_send()
    third.wait()
    fourth.wait()
    fifth.wait()
    sixth.wait()


def finish(steps):
    for _ in steps:
        pass


def gather_kernel(ctx, *refs):
    greet(neighbours(ctx))
    finish(gather_steps(ctx, *refs))


def scatter_steps(ctx, p_ref, base_ref, o_ref, relay, mixed, landed, send, recv):
    rows = o_ref.shape[0]
    sems = (send, recv)

    def block(owner, part=None):
        if part is None:
            return pl.ds(pl.multiple_of(owner * rows, rows), rows)
        return pl.ds(pl.multiple_of(owner * rows + part * (rows // 2), rows // 2), rows // 2)

    if ctx != 4:
        me = lax.axis_index("ctx")
        peers = ctx_peers(ctx)
        copies = [
            remote(p_ref.at[block(peer["ctx"])], landed.at[i], sems, i, peer)
            for i, peer in enumerate(peers)
        ]
        for copy in copies:
            copy.start()
        yield
        yield
        total = p_ref[block(me), :].astype(F32)
        if base_ref is not None:
            total = total + base_ref[...].astype(F32)
        for i, copy in enumerate(copies):
            copy.wait()
            total = total + landed[i].astype(F32)
        o_ref[...] = total.astype(o_ref.dtype)
        return
    me, xn, yn, far = square()
    to_x, to_y = {"ctx": xn}, {"ctx": yn}
    half = rows // 2
    low, high = pl.ds(0, half), pl.ds(half, half)
    first = remote(p_ref.at[block(far, 0)], relay.at[0], sems, 0, to_x)
    second = remote(p_ref.at[block(far, 1)], relay.at[1], sems, 1, to_y)
    third = remote(p_ref.at[block(xn, 0)], landed.at[0, low], sems, 2, to_x)
    fourth = remote(p_ref.at[block(yn, 1)], landed.at[1, high], sems, 3, to_y)
    first.start()
    second.start()
    third.start()
    fourth.start()
    yield
    first.wait_recv()
    mixed[0] = (relay[0].astype(F32) + p_ref[block(yn, 0), :].astype(F32)).astype(BF)
    fifth = remote(mixed.at[0], landed.at[1, low], sems, 4, to_y)
    fifth.start()
    second.wait_recv()
    mixed[1] = (relay[1].astype(F32) + p_ref[block(xn, 1), :].astype(F32)).astype(BF)
    sixth = remote(mixed.at[1], landed.at[0, high], sems, 5, to_x)
    sixth.start()
    yield
    first.wait_send()
    second.wait_send()
    third.wait()
    fourth.wait()
    fifth.wait()
    sixth.wait()
    total = p_ref[block(me), :].astype(F32)
    if base_ref is not None:
        total = total + base_ref[...].astype(F32)
    total = total + landed[0].astype(F32) + landed[1].astype(F32)
    o_ref[...] = total.astype(o_ref.dtype)


def scatter_scratch(ctx, rows, columns):
    slots = 2 if ctx == 4 else ctx - 1
    return [
        pltpu.VMEM((2, rows // 2, columns), BF),
        pltpu.VMEM((2, rows // 2, columns), BF),
        pltpu.VMEM((slots, rows, columns), BF),
    ]


def swap_kernel(ctx, x_ref, o_ref, send, recv):
    me = lax.axis_index("ctx")
    peers = ctx_peers(ctx)
    greet(peers)
    copies = [
        remote(x_ref.at[peer["ctx"]], o_ref.at[me], (send, recv), i, peer)
        for i, peer in enumerate(peers)
    ]
    for copy in copies:
        copy.start()
    o_ref[me] = x_ref[me]
    for copy in copies:
        copy.wait()


def share_kernel(ctx, packed, *refs):
    sources, (ox_ref, oy_ref, send, recv) = refs[: 1 if packed else 2], refs[1 if packed else 2 :]
    me, core = lax.axis_index("ctx"), lax.axis_index("dp")
    peers, other = ctx_peers(ctx), {"dp": 1 - core}
    rows, width = ox_ref.shape[2], oy_ref.shape[2]
    greet(peers + [other])
    sems = (send, recv)

    def chunk(member):
        if packed:
            return sources[0].at[pl.ds(pl.multiple_of(member * rows, rows), rows)]
        return sources[0].at[member]

    across = [
        remote(chunk(peer["ctx"]), ox_ref.at[me, core], sems, i, peer)
        for i, peer in enumerate(peers)
    ]
    for copy in across:
        copy.start()
    if packed:
        _, parts = below_parts((1,) + sources[0].shape, ctx * rows, width)
        for row, size, column, part, own_row, own_column in parts:
            oy_ref[core, own_row : own_row + size, own_column : own_column + part] = sources[0][
                row : row + size, column : column + part
            ]
    else:
        oy_ref[core] = sources[1][...]
    ox_ref[me, core] = chunk(me)[...]
    inside = [
        remote(ox_ref.at[me, core], ox_ref.at[me, core], sems, ctx, other),
        remote(oy_ref.at[core], oy_ref.at[core], sems, ctx + 1, other),
    ]
    for copy in inside:
        copy.start()
    for i, copy in enumerate(across):
        copy.wait_recv()
        source = lax.rem(me + ctx - 1 - i, ctx)
        block = ox_ref.at[source, core]
        inside.append(remote(block, block, sems, ctx + 2 + i, other))
        inside[-1].start()
    for copy in across:
        copy.wait_send()
    for copy in inside:
        copy.wait()


def call(kernel, out_shape, scratch, copies, collective_id, *args, limit=VMEM_LIMIT):
    return pl.pallas_call(
        kernel,
        out_shape=out_shape,
        in_specs=[pl.BlockSpec(memory_space=pltpu.VMEM)] * len(args),
        out_specs=jax.tree.map(lambda _: pl.BlockSpec(memory_space=pltpu.VMEM), out_shape),
        scratch_shapes=[
            *scratch,
            pltpu.SemaphoreType.DMA((copies,)),
            pltpu.SemaphoreType.DMA((copies,)),
        ],
        compiler_params=pltpu.CompilerParams(
            collective_id=collective_id, has_side_effects=True, vmem_limit_bytes=limit
        ),
    )(*args)


def shape_of(shape, dtype=BF):
    return jax.ShapeDtypeStruct(shape, dtype)


def gather_ctx(block):
    ctx = lax.axis_size("ctx")
    rows, columns = block.shape
    return call(
        functools.partial(gather_kernel, ctx), shape_of((ctx * rows, columns)), [], 8, 0, block
    )


def swap_ctx(parts, collective_id):
    ctx = lax.axis_size("ctx")
    return call(
        functools.partial(swap_kernel, ctx), shape_of(parts.shape), [], ctx, collective_id, parts
    )


def share_plane(sums, shapes, collective_id):
    ctx = lax.axis_size("ctx")
    return call(
        functools.partial(share_kernel, ctx, len(sums) == 1),
        [shape_of((ctx, 2) + shapes[0]), shape_of((2,) + shapes[1])],
        [],
        2 * ctx + 1,
        collective_id,
        *sums,
        limit=SMALL_LIMIT,
    )


def small_reduce_kernel(ctx, shards, x_ref, o_ref, first, column, second, third, send, recv):
    me, mine = lax.axis_index("ctx"), lax.axis_index("shard")
    along = [{"shard": lax.rem(mine + step, shards)} for step in range(1, shards)]
    across = ctx_peers(ctx)
    other = {"dp": 1 - lax.axis_index("dp")}
    greet(along + across + [other])
    sems = (send, recv)
    copies = [
        remote(x_ref.at[target["shard"]], first.at[i], sems, i, target)
        for i, target in enumerate(along)
    ]
    for copy in copies:
        copy.start()
    total = x_ref[mine]
    for i, copy in enumerate(copies):
        copy.wait()
        total = total + first[i]
    column[...] = total
    copies = [
        remote(column.at[target["ctx"]], second.at[i], sems, shards + i, target)
        for i, target in enumerate(across)
    ]
    for copy in copies:
        copy.start()
    total = column[me]
    for i, copy in enumerate(copies):
        copy.wait()
        total = total + second[i]
    third[0] = total
    copy = remote(third.at[0], third.at[1], sems, shards + ctx, other)
    copy.start()
    copy.wait()
    o_ref[...] = third[0] + third[1]


def small_gather(tile):
    ctx, shards = lax.axis_size("ctx"), lax.axis_size("shard")
    return call(
        functools.partial(small_gather_kernel, ctx, shards),
        shape_of((ctx, shards) + tile.shape, F32),
        [],
        ctx + shards + 1,
        6,
        tile,
    )


def small_reduce(tiles):
    shards, ctx = tiles.shape[:2]
    tile = tiles.shape[2:]
    return call(
        functools.partial(small_reduce_kernel, ctx, shards),
        shape_of(tile, F32),
        [
            pltpu.VMEM((shards - 1, ctx) + tile, F32),
            pltpu.VMEM((ctx,) + tile, F32),
            pltpu.VMEM((ctx - 1,) + tile, F32),
            pltpu.VMEM((2,) + tile, F32),
        ],
        ctx + shards + 1,
        7,
        tiles,
    )


def below_parts(packed_shape, count, width):
    columns = packed_shape[2]
    below = packed_shape[1] - count
    if fold(columns, width) == "even":
        rows = below * columns // width
        return rows, [
            (count + i * rows, rows, 0, columns, 0, i * columns) for i in range(width // columns)
        ]
    rest = columns - width
    part = below // (width // rest)
    parts = [(count, below, 0, width, 0, 0)]
    for i in range(width // rest):
        parts.append((count + i * part, part, width, rest, below, i * rest))
    return below + part, parts


def load_pair(ctx, refs, wide_ref, deep_ref, sems):
    if len(refs) == 2:
        wide = [pltpu.make_async_copy(refs[0], wide_ref, sems.at[0])]
        deep = [pltpu.make_async_copy(refs[1], deep_ref, sems.at[1])]
        wide[0].start()
        deep[0].start()
        return wide, deep
    packed_ref = refs[0]
    groups = packed_ref.shape[0]
    rows = wide_ref.shape[0] // (ctx * groups)
    own_rows, parts = below_parts(packed_ref.shape, ctx * rows, deep_ref.shape[1])
    wide, deep = [], []
    for group in range(groups):
        for member in range(ctx):
            source = packed_ref.at[group, pl.ds(member * rows, rows)]
            target = wide_ref.at[pl.ds((member * groups + group) * rows, rows)]
            wide.append((source, target))
        for row, count, column, width, own_row, own_column in parts:
            source = packed_ref.at[group, pl.ds(row, count), pl.ds(column, width)]
            target = deep_ref.at[
                pl.ds(group * own_rows + own_row, count), pl.ds(own_column, width)
            ]
            deep.append((source, target))
    wide = [pltpu.make_async_copy(*pair, sems.at[i]) for i, pair in enumerate(wide)]
    deep = [pltpu.make_async_copy(*pair, sems.at[len(wide) + i]) for i, pair in enumerate(deep)]
    for copy in wide + deep:
        copy.start()
    return wide, deep


def start_loads(sources, targets, sems):
    copies = [
        pltpu.make_async_copy(source, target, sems.at[i])
        for i, (source, target) in enumerate(zip(sources, targets))
    ]
    for copy in copies:
        copy.start()
    return copies


def wait_all(copies):
    for copy in copies:
        copy.wait()


def z_gather_steps(shards, parts, eager, src, out, local_sems, send, recv):
    mine, core = lax.axis_index("shard"), lax.axis_index("dp")
    other = {"dp": 1 - core}
    sems = (send, recv)
    hops = shards - 1
    inside = 2 * hops * len(parts)

    def source(part):
        return src.at[pl.ds(*parts[part])]

    def place(owner, part):
        return out.at[owner * 2 + core, pl.ds(*parts[part])]

    def number(way, hop, part):
        return (way * hops + hop) * len(parts) + part

    def sent(way, hop, part):
        step = 1 - 2 * way
        owner = mine - step * hop
        block = source(part) if hop == 0 else place(owner, part)
        target = {"shard": mine + step}
        return remote(block, place(owner, part), sems, number(way, hop, part), target)

    def landed(way, hop, part):
        step = 1 - 2 * way
        block = place(mine - step * (hop + 1), part)
        return remote(block, block, sems, number(way, hop, part), {"shard": mine - step})

    def shared(way, hop, part):
        step = 1 - 2 * way
        block = place(mine - step * (hop + 1), part)
        slot = inside + len(parts) + number(way, hop, part)
        return remote(block, block, sems, slot, other)

    def own(part):
        return remote(source(part), place(mine, part), sems, inside + part, other)

    def local(part):
        return pltpu.make_async_copy(source(part), place(mine, part), local_sems.at[part])

    def sends(way, hop):
        if way == 0:
            return jnp.logical_and(mine >= hop, mine < shards - 1)
        return jnp.logical_and(mine < shards - hop, mine > 0)

    def receives(way, hop):
        return mine > hop if way == 0 else mine < shards - 1 - hop

    for part in range(len(parts)):
        for way in range(2):
            pl.when(sends(way, 0))(lambda way=way, part=part: sent(way, 0, part).start())
        if not eager:
            local(part).start()
            own(part).start()
            yield
    if eager:
        for part in range(len(parts)):
            local(part).start()
            own(part).start()
        yield
    for hop in range(hops):
        for part in range(len(parts)):
            for way in range(2):

                def arrived(way=way, hop=hop, part=part):
                    landed(way, hop, part).wait_recv()

                def hand_on(way=way, hop=hop, part=part):
                    sent(way, hop + 1, part).start()

                def share(way=way, hop=hop, part=part):
                    shared(way, hop, part).start()

                pl.when(receives(way, hop))(arrived)
                if hop + 1 < hops:
                    pl.when(sends(way, hop + 1))(hand_on)
                pl.when(receives(way, hop))(share)
            yield
    for part in range(len(parts)):
        local(part).wait()
        own(part).wait()
        for way in range(2):
            for hop in range(hops):
                pl.when(sends(way, hop))(
                    lambda way=way, hop=hop, part=part: sent(way, hop, part).wait_send()
                )
                pl.when(receives(way, hop))(
                    lambda way=way, hop=hop, part=part: shared(way, hop, part).wait()
                )


def z_scatter_steps(shards, first, parts, src, out, pair, own, land, load_sems, send, recv):
    mine, core = lax.axis_index("shard"), lax.axis_index("dp")
    other = {"dp": 1 - core}
    sems = (send, recv)
    hops = shards - 1
    rows = pl.ds(first, out.shape[0])
    order = sorted(range(shards), key=lambda owner: min(owner, hops - owner))
    places = (mine, hops - mine)

    def crossed(owner):
        source = src.at[owner * 2 + 1 - core, rows]
        return remote(source, pair.at[owner], sems, owner, other)

    def loaded(owner):
        source = src.at[owner * 2 + core, rows]
        return pltpu.make_async_copy(source, own.at[owner], load_sems.at[owner])

    def slot_of(way, turn, part):
        return shards + (way * hops + turn) * len(parts) + part

    def handed(way, turn, part, block=None):
        target = {"shard": mine + 1 - 2 * way}
        there = land.at[way, turn, pl.ds(*parts[part])]
        number = slot_of(way, turn, part)
        return remote(there if block is None else block, there, sems, number, target)

    def begun(way, turn, part):
        owner = hops - turn if way == 0 else turn
        return handed(way, turn, part, pair.at[owner, pl.ds(*parts[part])])

    for owner in order[:2]:
        crossed(owner).start()
        loaded(owner).start()
    yield
    for owner in order:
        if owner == order[2]:
            yield
        loaded(owner).wait()
        crossed(owner).wait_recv()
        if owner == order[0]:
            for later in order[2:]:
                crossed(later).start()
                loaded(later).start()
        pair[owner] = (own[owner].astype(F32) + pair[owner].astype(F32)).astype(BF)
        for way in range(2):
            if owner == (hops if way == 0 else 0):

                def begin(way=way):
                    for part in range(len(parts)):
                        begun(way, 0, part).start()

                pl.when(places[way] == 0)(begin)
    yield
    for slot in range(1, shards):
        for part in range(len(parts)):
            here = pl.ds(*parts[part])
            for way, place in enumerate(places):
                turn = slot - place

                def go_on(way=way, part=part, slot=slot):
                    begun(way, slot - 1, part).wait_send()
                    begun(way, slot, part).start()

                def hand_on(way=way, turn=turn, part=part, here=here):
                    handed(way, turn, part).wait_recv()
                    block = land.at[way, turn, here]
                    owner = hops - turn if way == 0 else turn
                    added = pair[owner, here].astype(F32)
                    block[...] = (block[...].astype(F32) + added).astype(BF)
                    handed(way, turn, part).start()

                def arrived(way=way, turn=turn, part=part):
                    handed(way, turn, part).wait_recv()

                on_the_way = jnp.logical_and(place > 0, place <= slot)
                if slot < hops:
                    pl.when(place == 0)(go_on)
                    pl.when(on_the_way)(hand_on)
                else:
                    pl.when(on_the_way)(arrived)
            yield
    for owner in range(shards):
        crossed(owner).wait_send()
    for part in range(len(parts)):
        for way, place in enumerate(places):
            pl.when(place == 0)(
                lambda way=way, part=part: begun(way, hops - 1, part).wait_send()
            )
            for turn in range(hops):
                pl.when(jnp.logical_and(place > 0, place + turn < hops))(
                    lambda way=way, part=part, turn=turn: handed(way, turn, part).wait_send()
                )
    out[...] = pair[mine]
    for way, place in enumerate(places):

        def add(way=way, place=place):
            out[...] = (out[...].astype(F32) + land[way, hops - place].astype(F32)).astype(BF)

        pl.when(place > 0)(add)


def scatter_sums(line, shards):
    outs, scratch = [], []
    for grads, _, rows in line:
        block = (rows, grads.shape[2])
        outs.append(shape_of(block))
        count = shards + 4 * (shards - 1)
        scratch += [
            pltpu.VMEM((shards,) + block, BF),
            pltpu.VMEM((shards,) + block, BF),
            pltpu.VMEM((2, shards - 1) + block, BF),
            pltpu.SemaphoreType.DMA((shards,)),
            pltpu.SemaphoreType.DMA((count,)),
            pltpu.SemaphoreType.DMA((count,)),
        ]
    return outs, scratch


def scatter_lines(ctx, shards, firsts, sources, outs, scratch):
    if not firsts:
        greet(neighbours(ctx))
        return []
    greet_line(ctx, shards)
    lines = []
    for i, first in enumerate(firsts):
        parts = halves(outs[i].shape[0])
        lines.append(
            z_scatter_steps(
                shards, first, parts, sources[i], outs[i], *scratch[6 * i : 6 * i + 6]
            )
        )
    return lines


def halves(rows):
    half = rows // 32 * 16
    return [(0, half), (half, rows - half)]


def greet_line(ctx, shards):
    mine = lax.axis_index("shard")
    barrier = pltpu.get_barrier_semaphore()

    def signal(target):
        pl.semaphore_signal(barrier, inc=1, device_id=target, device_id_type=MESH)

    targets = neighbours(ctx) + [{"dp": 1 - lax.axis_index("dp")}]
    for target in targets:
        signal(target)
    pl.when(mine > 0)(lambda: signal({"shard": mine - 1}))
    pl.when(mine < shards - 1)(lambda: signal({"shard": mine + 1}))
    at_end = jnp.logical_or(mine == 0, mine == shards - 1)
    pl.when(at_end)(lambda: pl.semaphore_wait(barrier, len(targets) + 1))
    pl.when(jnp.logical_not(at_end))(lambda: pl.semaphore_wait(barrier, len(targets) + 2))


def line_sems(shards):
    count = 8 * (shards - 1) + 2
    return [
        pltpu.SemaphoreType.DMA((2,)),
        pltpu.SemaphoreType.DMA((count,)),
        pltpu.SemaphoreType.DMA((count,)),
    ]


def small_gather_steps(ctx, shards, x_ref, o_ref, send, recv):
    me, mine = lax.axis_index("ctx"), lax.axis_index("shard")
    along = [{"shard": lax.rem(mine + step, shards)} for step in range(1, shards)]
    o_ref[me, mine] = x_ref[...]
    copies = [
        remote(x_ref, o_ref.at[me, mine], (send, recv), i, target)
        for i, target in enumerate(along)
    ]
    for copy in copies:
        copy.start()
    yield
    wait_all(copies)
    copies = [
        remote(o_ref.at[me], o_ref.at[me], (send, recv), shards + i, target)
        for i, target in enumerate(ctx_peers(ctx))
    ]
    for copy in copies:
        copy.start()
    yield
    wait_all(copies)


def small_gather_kernel(ctx, shards, *refs):
    mine = lax.axis_index("shard")
    greet([{"shard": lax.rem(mine + step, shards)} for step in range(1, shards)] + ctx_peers(ctx))
    finish(small_gather_steps(ctx, shards, *refs))


def place_deep(block, packed_ref, count):
    columns = packed_ref.shape[1]
    _, parts = below_parts((1,) + packed_ref.shape, count, block.shape[1])
    for row, size, column, width, own_row, own_column in parts:
        packed_ref[row : row + size, column : column + width] = block[
            own_row : own_row + size, own_column : own_column + width
        ]


def gain_rows(tiles_ref, own_width):
    ctx, shards = tiles_ref.shape[:2]
    parts = [tiles_ref[i, j][:, :own_width] for i in range(ctx) for j in range(shards)]
    return jnp.concatenate(parts, axis=1)


def prologue_kernel(ctx, shards, layers, pieces, gains_ref, *refs):
    weights, refs = refs[:4], refs[4:]
    all_gains_ref, whole_ref, *packs = refs[: 2 + 2 * layers]
    stage, refs = refs[2 + 2 * layers : 2 + 6 * layers], refs[2 + 6 * layers :]
    cuts, refs = refs[: 2 * layers], refs[2 * layers :]
    tile_ref, tiles_ref, stage_sems, swap_send, swap_recv, small_send, small_recv, *line = refs
    own_width = gains_ref.shape[2]
    me, mine, core = lax.axis_index("ctx"), lax.axis_index("shard"), lax.axis_index("dp")
    peers = ctx_peers(ctx)
    greet(
        peers
        + [{"shard": lax.rem(mine + step, shards)} for step in range(1, shards)]
        + [{"dp": 1 - core}]
    )
    loads = []
    for layer in range(layers):
        for slot, weight in enumerate(weights):
            target = stage[4 * layer + slot]
            rows = target.shape[0]
            source = weight.at[layer, pl.ds(pl.multiple_of(core * rows, rows), rows)]
            loads.append(pltpu.make_async_copy(source, target, stage_sems.at[len(loads)]))
    loads[1].start()
    for i, load in enumerate(loads):
        if i != 1:
            load.start()
    tile_ref[...] = jnp.zeros_like(tile_ref)
    for layer in range(layers):
        own_gains = gains_ref[layer].astype(BF).astype(F32)
        tile_ref[2 * layer : 2 * layer + 2, :own_width] = own_gains
    small = small_gather_steps(ctx, shards, tile_ref, tiles_ref, small_send, small_recv)
    next(small)
    count = ctx * cuts[0].shape[1]
    first_parts = [(count, packs[0].shape[0] - count), (0, count)]
    line_steps = z_gather_steps(shards, first_parts, False, packs[0], whole_ref, *line)
    swaps = []
    for layer in range(layers):
        for kind in range(2):
            number = 2 * layer + kind
            pack_ref, cut = packs[number], cuts[number]
            wide, deep = 4 * layer + 2 * kind, 4 * layer + 2 * kind + 1
            rows = cut.shape[1]
            loads[deep].wait()
            place_deep(stage[deep][...].astype(BF), pack_ref, ctx * rows)
            if number == 0:
                next(line_steps)
            loads[wide].wait()
            for member, part in enumerate(member_parts(stage[wide][...], pieces[kind], ctx)):
                cut[member] = part.astype(BF)
            here = pl.ds(pl.multiple_of(me * rows, rows), rows)
            first = number * (ctx - 1)
            copies = [
                remote(cut.at[peer["ctx"]], pack_ref.at[here], (swap_send, swap_recv), first + i, peer)
                for i, peer in enumerate(peers)
            ]
            for copy in copies:
                copy.start()
            pack_ref[here, :] = cut[me]
            if number == 0:
                wait_all(copies)
                next(line_steps)
                next(small)
            else:
                swaps += copies
                next(line_steps)
    finish(small)
    all_gains_ref[...] = gain_rows(tiles_ref, own_width)
    finish(line_steps)
    wait_all(swaps)


def store_gate_grad(ctx, normed_ref, grad_gu, refs, outs, sems):
    width = normed_ref.shape[1] // ctx
    groups = refs[0].shape[0] if len(refs) == 1 else 1
    rows = width // groups

    def leave(member):
        here = pl.ds(member * rows, rows)
        if len(refs) == 2:
            source, target = refs[0].at[here], outs[0].at[here]
        else:
            source, target = refs[0].at[:, here], outs[0].at[:, here]
        return pltpu.make_async_copy(source, target, sems.at[member])

    def make(member):
        if isinstance(member, int):
            left = normed_ref[:, member * width : (member + 1) * width]
        else:
            left = normed_ref[:, pl.ds(pl.multiple_of(member * width, width), width)]
        part = dot(left, grad_gu[...], ((0,), (0,))).astype(BF)
        for group in range(groups):
            here = pl.ds(member * rows, rows)
            if not isinstance(member, int):
                here = pl.ds(pl.multiple_of(member * rows, rows), rows)
            block = part[group * rows : (group + 1) * rows]
            if len(refs) == 2:
                refs[0][here, :] = block
            else:
                refs[0][group, here, :] = block
        leave(member).start()

    for members in (range(ctx // 2), range(ctx // 2, ctx)):
        if width % 128:
            for member in members:
                make(member)
        else:
            pl.loop(members.start, members.stop)(make)
        yield [leave(member) for member in members]


def store_down_grad(ctx, hidden, grad_ref, refs, outs, sems):
    if len(refs) == 2:
        refs[1][...] = dot(hidden[...], grad_ref[...], ((0,), (0,))).astype(BF)
        copy = pltpu.make_async_copy(refs[1], outs[1], sems.at[ctx])
        copy.start()
        return copy
    packed_ref = refs[0]
    groups, width = packed_ref.shape[0], grad_ref.shape[1]
    count = width // groups
    own_rows, parts = below_parts(packed_ref.shape, count, width)
    together = 128 // math.gcd(128, own_rows)

    @pl.loop(0, groups // together)
    def _(step):
        lanes = together * own_rows
        block = hidden[:, pl.ds(pl.multiple_of(step * lanes, lanes), lanes)]
        block = dot(block, grad_ref[...], ((0,), (0,))).astype(BF)
        for group in range(together):
            for row, size, column, columns, own_row, own_column in parts:
                own_row += group * own_rows
                packed_ref[
                    step * together + group, row : row + size, column : column + columns
                ] = block[own_row : own_row + size, own_column : own_column + columns]

    here = pl.ds(count, packed_ref.shape[1] - count)
    copy = pltpu.make_async_copy(packed_ref.at[:, here], outs[0].at[:, here], sems.at[ctx])
    copy.start()
    return copy


def grad_scratch(weights):
    return [
        *[pltpu.VMEM(weight.shape, BF) for weight in weights],
        pltpu.SemaphoreType.DMA((lax.axis_size("ctx") + 1,)),
    ]


def sigmoid(value):
    return 1.0 / (1.0 + jnp.exp(-value))


def mlp_stage(ctx, serve, load, stream_ref, gain, new_ref, normed_ref, gu_ref, wgu, wd, own, part, comm):
    serve()
    own[...] = norm_forward(stream_ref[...], gain)
    gathered = gather_steps(ctx, own, normed_ref, *comm[:2])
    next(gathered)
    serve()
    wide, deep = load()
    next(gathered)
    serve()
    finish(gathered)
    serve()
    wait_all(wide)
    gu_ref[...] = dot(normed_ref[...], wgu[...])
    serve()
    half = gu_ref.shape[1] // 2
    gate, up = gu_ref[:, :half], gu_ref[:, half:]
    hidden = (gate * sigmoid(gate) * up).astype(BF)
    wait_all(deep)
    part[...] = dot(hidden, wd[...]).astype(BF)
    scattered = scatter_steps(ctx, part, stream_ref, new_ref, *comm[2:])
    next(scattered)
    serve()
    next(scattered)
    serve()
    finish(scattered)
    serve()


def mlp_forward_kernel(ctx, count, row, stream_ref, gains_ref, *refs):
    weights = refs[:count]
    new_ref, normed_ref, gu_ref, wgu, wd, own, part, sems, *comm = refs[count:]
    greet(neighbours(ctx))
    mlp_stage(
        ctx,
        lambda: None,
        lambda: load_pair(ctx, weights, wgu, wd, sems),
        stream_ref,
        gains_ref[row : row + 1],
        new_ref,
        normed_ref,
        gu_ref,
        wgu,
        wd,
        own,
        part,
        comm,
    )


def rope(value, tables, back=False):
    cosine, ahead, behind = tables
    width, half_dim = value.shape[1], HEAD_DIM // 2
    turned = pltpu.roll(value, width - half_dim, 1) * ahead[...]
    turned = turned + pltpu.roll(value, half_dim, 1) * behind[...]
    return value * cosine[...] + (-turned if back else turned)


def head_of(ref, index):
    return ref[:, index * HEAD_DIM : (index + 1) * HEAD_DIM]


def exact_dot(left, right, dims=((1,), (0,))):
    return lax.dot_general(
        left, right, (dims, ((), ())), precision=lax.Precision.HIGHEST, preferred_element_type=F32
    )


def build_tables(angle_ref, select_ref, tables, bias):
    width = tables[0].shape[1]
    for i, table in enumerate(tables):
        table[...] = exact_dot(angle_ref[...], select_ref[:, i * width : (i + 1) * width])
    lanes = lax.broadcasted_iota(jnp.int32, (8, angle_ref.shape[1]), 1)
    pick = jnp.where(lanes == HEAD_DIM, 1.0, 0.0)
    key_pos = exact_dot(pick, angle_ref[...], ((1,), (1,)))[:1]
    query_pos = angle_ref[:, HEAD_DIM : HEAD_DIM + 1]
    bias[...] = jnp.where(key_pos <= query_pos, 0.0, -1000000000.0)


def attn_stage(
    ctx, serve, load, prepare, stream_ref, gain, kept, new_ref, wq, wo, own, part, tables, bias, comm
):
    normed_ref, qkv_ref, att_ref, lse_ref = kept
    own[...] = norm_forward(stream_ref[...].astype(F32), gain)
    gathered = gather_steps(ctx, own, normed_ref, *comm[:2])
    next(gathered)
    wide, deep = load()
    next(gathered)
    prepare()
    finish(gathered)
    serve()
    wait_all(wide)
    qkv_ref[...] = rope(dot(normed_ref[...], wq[...]), tables).astype(BF)
    kv_heads = qkv_ref.shape[1] // (4 * HEAD_DIM)
    lane = lax.broadcasted_iota(jnp.int32, lse_ref.shape, 1)
    mixed, lse = [], jnp.zeros(lse_ref.shape, F32)
    for head in range(2 * kv_heads):
        query = head_of(qkv_ref, head)
        key = head_of(qkv_ref, 2 * kv_heads + head // 2)
        value = head_of(qkv_ref, 3 * kv_heads + head // 2)
        scores = dot(query, key, ((1,), (1,))) * HEAD_DIM ** (-0.5) + bias[...]
        top = jnp.max(scores, axis=1, keepdims=True)
        terms = jnp.exp(scores - top)
        total = jnp.sum(terms, axis=1, keepdims=True)
        probs = (terms * (1.0 / total)).astype(BF)
        mixed.append(dot(probs, value).astype(BF))
        lse = jnp.where(lane == head, top + jnp.log(total), lse)
    att_ref[...] = jnp.concatenate(mixed, axis=1)
    lse_ref[...] = lse
    wait_all(deep)
    part[...] = dot(att_ref[...], wo[...]).astype(BF)
    scattered = scatter_steps(ctx, part, stream_ref, new_ref, *comm[2:])
    next(scattered)
    serve()
    finish(scattered)
    serve()


def attn_forward_kernel(ctx, count, row, is_first, is_last, *refs):
    refs = list(refs)

    def take(on=True):
        return refs.pop(0) if on else None

    stream_ref, gains_ref = take(), take()
    sources = [take() for _ in range(3 if is_first else 2)]
    weights = [take() for _ in range(count)]
    new_ref, *kept = [take() for _ in range(5)]
    angles_out, top_out = take(is_first), take(is_first)
    next_normed = take(is_last)
    wq, wo, bias, own, part, *tables = [take() for _ in range(8)]
    sems = take()
    comm = [take() for _ in range(7)]
    extra = [take() for _ in range(4)]
    loaded = [take() for _ in sources]
    load_sems = take()
    select_ref, angle_ref, *top_ref = loaded
    loads = start_loads(sources, loaded, load_sems)
    greet(neighbours(ctx))

    def prepare():
        wait_all(loads)
        if is_first:
            finish(gather_steps(ctx, angle_ref, angles_out, *extra[:2]))
        build_tables(angles_out if is_first else angle_ref, select_ref, tables, bias)

    attn_stage(
        ctx,
        lambda: None,
        lambda: load_pair(ctx, weights, wq, wo, sems),
        prepare,
        stream_ref,
        gains_ref[row : row + 1],
        kept,
        new_ref,
        wq,
        wo,
        own,
        part,
        tables,
        bias,
        comm,
    )
    if is_first:
        finish(gather_steps(ctx, top_ref[0], top_out, *extra[2:]))
    if is_last:
        own[...] = norm_forward(new_ref[...], gains_ref[row + 1 : row + 2])
        finish(gather_steps(ctx, own, next_normed, *extra[2:]))


def z_stream(hops, gathers, counts):
    next(gathers[0])
    yield 0
    for done, (steps, count) in enumerate(zip(gathers, counts)):
        for turn in range(hops * count):
            next(steps)
            if turn == (hops - 1) * count - 1 and done + 1 < len(gathers):
                next(gathers[done + 1])
            yield done
        finish(steps)
        yield done + 1


def forward_kernel(ctx, shards, layers, *refs):
    refs = list(refs)

    def take(count):
        taken = refs[:count]
        del refs[:count]
        return taken

    last = layers - 1
    stream_ref, gains_ref = take(2)
    sources = take(3)
    (first_whole,) = take(1)
    pack_refs = take(2 * layers - 1)
    kept_out = [take(6) for _ in range(layers)]
    gate_out = [take(2) for _ in range(last)]
    common_out = take(2)
    whole_refs = take(2 * layers - 1)
    kept_refs = [take(6) for _ in range(layers)]
    gate_refs = [take(2) for _ in range(last)]
    angles_ref, tops_ref = common_refs = take(2)
    wq, wo, wgu, wd, bias, own, part = take(7)
    tables = take(3)
    attn_sems, mlp_sems, out_sems = take(3)
    comm, extra, loaded = take(7), take(4), take(3)
    (load_sems,) = take(1)
    lines = [take(3) for _ in pack_refs]
    select_ref, angle_ref, top_ref = loaded
    loads = start_loads(sources, loaded, load_sems)
    greet_line(ctx, shards)
    gathers, counts = [], []
    for pack_ref, whole_ref, line in zip(pack_refs, whole_refs, lines):
        parts = halves(pack_ref.shape[0])
        gathers.append(z_gather_steps(shards, parts, True, pack_ref, whole_ref, *line))
        counts.append(len(parts))
    stream = z_stream(shards - 1, gathers, counts)
    there, stored = [next(stream)], []

    def serve():
        there[0] = next(stream, there[0])

    def wait_for(number):
        while there[0] <= number:
            serve()

    def store(source, target):
        stored.append(pltpu.make_async_copy(source, target, out_sems.at[len(stored)]))
        stored[-1].start()

    def prepare():
        wait_all(loads)
        finish(gather_steps(ctx, angle_ref, angles_ref, *extra[:2]))
        build_tables(angles_ref, select_ref, tables, bias)
        store(angles_ref, common_out[0])

    for layer in range(layers):
        new_ref, *kept, next_normed = kept_refs[layer]

        def load_attn(layer=layer):
            if layer == 0:
                return load_pair(ctx, [first_whole], wq, wo, attn_sems)
            wait_for(2 * layer - 1)
            return load_pair(ctx, [whole_refs[2 * layer - 1]], wq, wo, attn_sems)

        def load_mlp(layer=layer):
            wait_for(2 * layer)
            return load_pair(ctx, [whole_refs[2 * layer]], wgu, wd, mlp_sems)

        attn_stage(
            ctx,
            serve,
            load_attn,
            prepare if layer == 0 else lambda: None,
            stream_ref,
            gains_ref[2 * layer : 2 * layer + 1],
            kept,
            new_ref,
            wq,
            wo,
            own,
            part,
            tables,
            bias,
            comm,
        )
        for source, target in zip(kept_refs[layer][:5], kept_out[layer]):
            store(source, target)
        if layer == 0:
            tops = gather_steps(ctx, top_ref, tops_ref, *extra[2:])
            next(tops)
            next(tops)
            serve()
            finish(tops)
            store(tops_ref, common_out[1])
            serve()
        gain = gains_ref[2 * layer + 1 : 2 * layer + 2]
        if layer < last:
            stream_ref, gu_ref = gate_refs[layer]
            mlp_stage(
                ctx,
                serve,
                load_mlp,
                new_ref,
                gain,
                stream_ref,
                next_normed,
                gu_ref,
                wgu,
                wd,
                own,
                part,
                comm,
            )
            for source, target in zip(gate_refs[layer], gate_out[layer]):
                store(source, target)
        else:
            own[...] = norm_forward(new_ref[...], gain)
            rows = gather_steps(ctx, own, next_normed, *extra[:2])
            next(rows)
            next(rows)
            serve()
            finish(rows)
        store(next_normed, kept_out[layer][5])
    wait_for(len(pack_refs) - 1)
    wait_all(stored)


def attn_backward_kernel(ctx, shards, count, row, ends, firsts, dh_ref, gains_ref, *refs):
    refs = list(refs)

    def take(number):
        taken = refs[:number]
        del refs[:number]
        return taken

    sources = take(10 if ends else 7)
    end_weights = take(ends)
    weights, line_sources = take(count), take(len(firsts))
    new_dh, gain_grad = take(2)
    end_gain_grad, up_ref = take(2) if ends else (None, None)
    line_outs = take(len(firsts))
    outs = take(count)
    made, (made_sems,) = take(count), take(1)
    wq, wo, bias, own, grads, mixed, dproj, part, dy, sems = take(10)
    tables, comm = take(3), take(7)
    loaded, (load_sems,) = take(len(sources)), take(1)
    wgu, wd, end_sems = take(3) if ends else (None, None, None)
    stream_ref, normed_ref, qkv_ref, att_ref, lse_ref, select_ref, angle_ref = loaded[-7:]
    loads = start_loads(sources, loaded, load_sems)
    lines = scatter_lines(ctx, shards, firsts, line_sources, line_outs, refs)

    def serve():
        for line in lines:
            next(line, None)

    serve()
    if ends:
        end_wide, end_deep = load_pair(ctx, end_weights, wgu, wd, end_sems)
    wide, deep = load_pair(ctx, weights, wq, wo, sems)
    serve()
    grad_stream = dh_ref[...].astype(F32)
    if ends:
        dgu, hidden, end_stream = loaded[:3]
        wait_all(loads[:3])
        wait_all(end_wide)
        part[...] = dot(dgu[...], wgu[...], ((1,), (1,))).astype(BF)
        scattered = scatter_steps(ctx, part, None, dy, *comm[2:])
        next(scattered)
        serve()
        wait_all(end_deep)
        up_ref[...] = dot(hidden[...], wd[...]).astype(BF)
        wait_all(loads[3:])
        build_tables(angle_ref, select_ref, tables, bias)
        next(scattered)
        serve()
        finish(scattered)
        dx, end_gain_grad[...] = norm_backward(
            dy[...], gains_ref[row + 1 : row + 2], end_stream[...].astype(F32)
        )
        new_dh[...] = grad_stream + dx
    else:
        new_dh[...] = grad_stream
    own[...] = new_dh[...].astype(BF)
    gathered = gather_steps(ctx, own, grads, *comm[:2])
    next(gathered)
    next(gathered)
    serve()
    if not ends:
        wait_all(loads)
        build_tables(angle_ref, select_ref, tables, bias)
    finish(gathered)
    serve()
    wait_all(deep)
    mixed[...] = dot(grads[...], wo[...], ((1,), (1,))).astype(BF)
    kv_heads = qkv_ref.shape[1] // (4 * HEAD_DIM)
    scale = HEAD_DIM ** (-0.5)
    dq, dk, dv = [], [0.0] * kv_heads, [0.0] * kv_heads
    for head in range(2 * kv_heads):
        group = head // 2
        query, grad = head_of(qkv_ref, head), head_of(mixed, head)
        key = head_of(qkv_ref, 2 * kv_heads + group)
        value = head_of(qkv_ref, 3 * kv_heads + group)
        scores = dot(query, key, ((1,), (1,))) * scale + bias[...]
        probs = jnp.exp(scores - lse_ref[:, head : head + 1])
        dprobs = dot(grad, value, ((1,), (1,)))
        inner = jnp.sum(probs * dprobs, axis=1, keepdims=True)
        dscores = (probs * (dprobs - inner)).astype(BF)
        dq.append(dot(dscores, key) * scale)
        dk[group] = dk[group] + dot(dscores, query, ((0,), (0,))) * scale
        dv[group] = dv[group] + dot(probs.astype(BF), grad, ((0,), (0,)))
    serve()
    dproj[...] = rope(jnp.concatenate(dq + dk + dv, axis=1), tables, back=True).astype(BF)
    wait_all(wide)
    part[...] = dot(dproj[...], wq[...], ((1,), (1,))).astype(BF)
    scattered = scatter_steps(ctx, part, None, dy, *comm[2:])
    next(scattered)
    stored = store_gate_grad(ctx, normed_ref, dproj, made, outs, made_sems)
    copies = next(stored)
    next(scattered)
    copies += next(stored)
    copies.append(store_down_grad(ctx, att_ref, grads, made, outs, made_sems))
    serve()
    finish(scattered)
    dx, gain_grad[...] = norm_backward(
        dy[...], gains_ref[row : row + 1], stream_ref[...].astype(F32)
    )
    new_dh[...] = new_dh[...] + dx
    wait_all(copies)
    for line in lines:
        finish(line)


def gate_backward(gate, up, grad_hidden):
    sig = sigmoid(gate)
    silu = gate * sig
    grad_gate = grad_hidden * up * sig * (1.0 + gate * (1.0 - sig))
    return (silu * up).astype(BF), grad_gate.astype(BF), (grad_hidden * silu).astype(BF)


def mlp_backward_kernel(ctx, shards, count, row, firsts, dh_ref, gains_ref, *refs):
    refs = list(refs)

    def take(number):
        taken = refs[:number]
        del refs[:number]
        return taken

    sources, weights, line_sources = take(5), take(count), take(len(firsts))
    new_dh, gain_grad, sum_out = take(3)
    line_outs = take(len(firsts))
    outs = take(count)
    made, (made_sems,) = take(count), take(1)
    wgu, wd, dgu, hidden, own, grads, part, dy, sems = take(9)
    scratch = take(12)
    loaded, (load_sems,) = take(5), take(1)
    normed_ref, gu_ref, stream_ref, sum_ref, base_ref = loaded
    loads = start_loads(sources, loaded, load_sems)
    lines = scatter_lines(ctx, shards, firsts, line_sources, line_outs, refs)

    def serve():
        for line in lines:
            next(line, None)

    own[...] = dh_ref[...].astype(BF)
    gathered = gather_steps(ctx, own, grads, *scratch[:2])
    summed = scatter_steps(ctx, sum_ref, base_ref, sum_out, *scratch[2:7])
    scattered = scatter_steps(ctx, part, None, dy, *scratch[7:])
    next(gathered)
    serve()
    wide, deep = load_pair(ctx, weights, wgu, wd, sems)
    next(gathered)
    serve()
    wait_all(loads)
    next(summed)
    serve()
    finish(gathered)
    serve()
    wait_all(deep)
    half = gu_ref.shape[1] // 2
    grad_hidden = dot(grads[...], wd[...], ((1,), (1,)))
    hidden[...], dgu[:, :half], dgu[:, half:] = gate_backward(
        gu_ref[:, :half], gu_ref[:, half:], grad_hidden
    )
    next(summed)
    serve()
    wait_all(wide)
    part[...] = dot(dgu[...], wgu[...], ((1,), (1,))).astype(BF)
    next(scattered)
    serve()
    finish(summed)
    stored = store_gate_grad(ctx, normed_ref, dgu, made, outs, made_sems)
    copies = next(stored)
    next(scattered)
    serve()
    copies += next(stored)
    copies.append(store_down_grad(ctx, hidden, grads, made, outs, made_sems))
    serve()
    finish(scattered)
    dx, gain_grad[...] = norm_backward(
        dy[...], gains_ref[row : row + 1], stream_ref[...].astype(F32)
    )
    new_dh[...] = dh_ref[...].astype(F32) + dx
    wait_all(copies)
    for line in lines:
        finish(line)


def mlp_last_kernel(ctx, count, *refs):
    sources, refs = refs[:2], refs[2:]
    weights, outs = refs[:count], refs[count : 2 * count]
    hidden_out, dgu_out, *refs = refs[2 * count :]
    made, (made_sems, hidden, dgu, wgu, wd, sems, *loaded) = refs[:count], refs[count:]
    *loaded, load_sems = loaded
    normed_ref, grad_ref = loaded
    loads = start_loads(sources, loaded, load_sems)
    wide, deep = load_pair(ctx, weights, wgu, wd, sems)
    wait_all(loads + wide + deep)
    half = dgu.shape[1] // 2
    tile = half // 2

    @pl.loop(0, half // tile)
    def _(step):
        start = pl.multiple_of(step * tile, tile)
        one, two = pl.ds(start, tile), pl.ds(pl.multiple_of(half + start, tile), tile)
        gate = dot(normed_ref[...], wgu[:, one])
        up = dot(normed_ref[...], wgu[:, two])
        grad_hidden = dot(grad_ref[...], wd[one, :], ((1,), (1,)))
        hidden[:, one], dgu[:, one], dgu[:, two] = gate_backward(gate, up, grad_hidden)

    copies = start_loads((hidden, dgu), (hidden_out, dgu_out), load_sems)
    for left in store_gate_grad(ctx, normed_ref, dgu, made, outs, made_sems):
        copies += left
    copies.append(store_down_grad(ctx, hidden, grad_ref, made, outs, made_sems))
    wait_all(copies)


def local_call(kernel, out_shape, scratch, flops, hbm, *args):
    bytes_moved = sum(a.size * a.dtype.itemsize for a in args)
    bytes_moved += sum(a.size * a.dtype.itemsize for a in out_shape)
    spaces = [pl.ANY if hbm[0] <= i <= hbm[1] else pltpu.VMEM for i in range(len(args))]
    return pl.pallas_call(
        kernel,
        out_shape=out_shape,
        in_specs=[pl.BlockSpec(memory_space=space) for space in spaces],
        out_specs=[pl.BlockSpec(memory_space=pl.ANY) for _ in out_shape],
        scratch_shapes=scratch,
        cost_estimate=pl.CostEstimate(flops=flops, bytes_accessed=bytes_moved, transcendentals=0),
        compiler_params=pltpu.CompilerParams(vmem_limit_bytes=VMEM_LIMIT),
    )(*args)


def weight_set(packed, width):
    ctx = lax.axis_size("ctx")
    groups, _, columns = packed.shape
    kind, rows = fold(columns, width), width // (ctx * groups)
    if kind != "cut" and rows % 16 == 0:
        return (packed,)
    return spread(packed, width)


def weight_scratch(weights, width):
    ctx = lax.axis_size("ctx")
    columns = weights[0].shape[-1]
    if len(weights) == 2:
        return [pltpu.VMEM(w.shape, BF) for w in weights], pltpu.SemaphoreType.DMA((2,))
    groups, rows, _ = weights[0].shape
    own_rows, parts = below_parts(weights[0].shape, width // groups, width)
    return [
        pltpu.VMEM((width, columns), BF),
        pltpu.VMEM((own_rows * groups, width), BF),
    ], pltpu.SemaphoreType.DMA((groups * (ctx + len(parts)),))


def comm_scratch(ctx, own, width):
    return [
        *pair_of_sems(),
        *scatter_scratch(ctx, own, width),
        *pair_of_sems(),
    ]


def kernel_id(kind, layer):
    return 16 + 8 * layer + kind


def mlp_forward_call(layer, stream, gains, weights):
    ctx = lax.axis_size("ctx")
    own, width = stream.shape
    rows, columns = ctx * own, weights[0].shape[-1]
    scratch, sems = weight_scratch(weights, width)
    return remote_call(
        functools.partial(mlp_forward_kernel, ctx, len(weights), 2 * layer + 1),
        [shape_of((own, width), F32), shape_of((rows, width)), shape_of((rows, columns), F32)],
        [
            *scratch,
            pltpu.VMEM((own, width), BF),
            pltpu.VMEM((rows, width), BF),
            sems,
            *comm_scratch(ctx, own, width),
        ],
        len(weights),
        kernel_id(0, layer),
        stream,
        gains,
        *weights,
    )


def attn_forward_call(layer, stream, gains, weights, tables, top, is_last):
    ctx = lax.axis_size("ctx")
    own, width = stream.shape
    rows, columns = ctx * own, weights[0].shape[-1]
    scratch, sems = weight_scratch(weights, width)
    is_first = top is not None
    loaded = [*tables, top] if is_first else list(tables)
    outs = remote_call(
        functools.partial(
            attn_forward_kernel, ctx, len(weights), 2 * layer, is_first, is_last
        ),
        [
            shape_of((own, width), F32),
            shape_of((rows, width)),
            shape_of((rows, columns)),
            shape_of((rows, columns // 2)),
            shape_of((rows, 128), F32),
            *([shape_of((rows, 128), F32), shape_of((rows, width))] if is_first else []),
            *([shape_of((rows, width))] if is_last else []),
        ],
        [
            *scratch,
            pltpu.VMEM((rows, rows), F32),
            pltpu.VMEM((own, width), BF),
            pltpu.VMEM((rows, width), BF),
            *[pltpu.VMEM((rows, columns), F32)] * 3,
            sems,
            *comm_scratch(ctx, own, width),
            *pair_of_sems(),
            *pair_of_sems(),
            *load_scratch(loaded),
        ],
        len(loaded) + len(weights),
        kernel_id(1, layer),
        stream,
        gains,
        *loaded,
        *weights,
    )
    return outs[0], outs[1:5], outs[5:]


def forward_call(stream, gains, tables, top, whole, attn_packs, mlp_packs):
    ctx, shards, layers = lax.axis_size("ctx"), lax.axis_size("shard"), len(mlp_packs)
    own, width = stream.shape
    rows, columns, gate_columns = ctx * own, whole.shape[2], mlp_packs[0].shape[1]
    packs = [mlp_packs[0]]
    for layer in range(1, layers):
        packs += [attn_packs[layer], mlp_packs[layer]]
    attn_scratch, attn_sems = weight_scratch([whole], width)
    mlp_scratch, mlp_sems = weight_scratch(
        [shape_of((2 * shards,) + mlp_packs[0].shape)], width
    )
    kept = [
        shape_of((own, width), F32),
        shape_of((rows, width)),
        shape_of((rows, columns)),
        shape_of((rows, columns // 2)),
        shape_of((rows, 128), F32),
        shape_of((rows, width)),
    ]
    gate_kept = [shape_of((own, width), F32), shape_of((rows, gate_columns), F32)]
    common = [shape_of((rows, 128), F32), shape_of((rows, width))]
    outs = kept * layers + gate_kept * (layers - 1) + common
    wholes = [shape_of((2 * shards,) + pack.shape) for pack in packs]
    loaded = [*tables, top]
    results = remote_call(
        functools.partial(forward_kernel, ctx, shards, layers),
        outs + wholes,
        [
            *[pltpu.VMEM(out.shape, out.dtype) for out in outs],
            *attn_scratch,
            *mlp_scratch,
            pltpu.VMEM((rows, rows), F32),
            pltpu.VMEM((own, width), BF),
            pltpu.VMEM((rows, width), BF),
            *[pltpu.VMEM((rows, columns), F32)] * 3,
            attn_sems,
            mlp_sems,
            pltpu.SemaphoreType.DMA((len(outs),)),
            *comm_scratch(ctx, own, width),
            *pair_of_sems(),
            *pair_of_sems(),
            *load_scratch(loaded),
            *line_sems(shards) * len(packs),
        ],
        len(loaded) + 1 + len(packs),
        kernel_id(5, 0),
        stream,
        gains,
        *loaded,
        whole,
        *packs,
        hbm_out=len(outs) + len(wholes),
    )
    per_layer = [results[6 * layer : 6 * layer + 6] for layer in range(layers)]
    results = results[6 * layers :]
    gates = [results[2 * layer : 2 * layer + 2] for layer in range(layers - 1)]
    return per_layer, gates, results[2 * layers - 2 : 2 * layers], results[2 * layers :]


def attn_backward_call(
    layer, grad_stream, stream, gains, kept, weights, tables, ends, end_weights, line
):
    ctx, shards = lax.axis_size("ctx"), lax.axis_size("shard")
    own, width = stream.shape
    rows, columns = ctx * own, weights[0].shape[-1]
    scratch, sems = weight_scratch(weights, width)
    line_outs, line_scratch = scatter_sums(line, shards)
    loaded = [*ends, stream, *kept, *tables]
    end_scratch = []
    if ends:
        end_scratch, end_sems = weight_scratch(end_weights, width)
        end_scratch.append(end_sems)
    firsts = [first for _, first, _ in line]
    results = remote_call(
        functools.partial(
            attn_backward_kernel,
            ctx,
            shards,
            len(weights),
            2 * layer,
            len(end_weights),
            firsts,
        ),
        [
            shape_of((own, width), F32),
            shape_of((1, width), F32),
            *([shape_of((1, width), F32), shape_of((rows, width))] if ends else []),
            *line_outs,
            *[shape_of(weight.shape) for weight in weights],
        ],
        [
            *grad_scratch(weights),
            *scratch,
            pltpu.VMEM((rows, rows), F32),
            pltpu.VMEM((own, width), BF),
            pltpu.VMEM((rows, width), BF),
            pltpu.VMEM((rows, columns // 2), BF),
            pltpu.VMEM((rows, columns), BF),
            pltpu.VMEM((rows, width), BF),
            pltpu.VMEM((own, width), F32),
            sems,
            *[pltpu.VMEM((rows, columns), F32)] * 3,
            *comm_scratch(ctx, own, width),
            *load_scratch(loaded),
            *end_scratch,
            *line_scratch,
        ],
        len(loaded) + len(end_weights) + len(weights) + len(line),
        kernel_id(2, layer),
        grad_stream,
        gains,
        *loaded,
        *end_weights,
        *weights,
        *[grads for grads, _, _ in line],
        hbm_out=len(weights),
    )
    results, outs = results[: -len(weights)], results[-len(weights) :]
    new_dh, gain_grad, *more = results
    if ends:
        return packed_grads(outs), new_dh, gain_grad[0], (more[0][0], more[1]), more[2:]
    return packed_grads(outs), new_dh, gain_grad[0], (), more


def packed_grads(outs):
    return outs[0] if len(outs) == 1 else pack_grads(*outs)


def remote_call(kernel, out_shape, scratch, hbm, collective_id, *args, hbm_out=0):
    spaces = [pltpu.VMEM] * (len(args) - hbm) + [pl.ANY] * hbm
    out_spaces = [pltpu.VMEM] * (len(out_shape) - hbm_out) + [pl.ANY] * hbm_out
    return pl.pallas_call(
        kernel,
        out_shape=out_shape,
        in_specs=[pl.BlockSpec(memory_space=space) for space in spaces],
        out_specs=[pl.BlockSpec(memory_space=space) for space in out_spaces],
        scratch_shapes=scratch,
        compiler_params=pltpu.CompilerParams(
            collective_id=collective_id, has_side_effects=True, vmem_limit_bytes=VMEM_LIMIT
        ),
    )(*args)


def prologue_call(gains, weights, pieces):
    ctx, shards = lax.axis_size("ctx"), lax.axis_size("shard")
    layers = weights[0].shape[0]
    tile = (-(-2 * layers // 8) * 8, 128)
    groups = 2 * shards
    stage, cuts, packs = [], [], []
    for _ in range(layers):
        for kind in range(2):
            wide, deep = weights[2 * kind], weights[2 * kind + 1]
            rows, columns = wide.shape[1] // 2, wide.shape[2] // ctx
            below = deep.shape[1] // 2 * deep.shape[2] // columns
            stage += [
                pltpu.VMEM((rows, wide.shape[2]), F32),
                pltpu.VMEM((deep.shape[1] // 2, deep.shape[2]), F32),
            ]
            cuts.append(pltpu.VMEM((ctx, rows, columns), BF))
            packs.append(shape_of((ctx * rows + below, columns)))
    swaps = 2 * layers * (ctx - 1)
    outs = pl.pallas_call(
        functools.partial(prologue_kernel, ctx, shards, layers, pieces),
        out_shape=[
            shape_of((tile[0], ctx * shards * gains.shape[2]), F32),
            shape_of((groups,) + packs[0].shape),
            *packs,
        ],
        in_specs=[pl.BlockSpec(memory_space=pltpu.VMEM)] + [pl.BlockSpec(memory_space=pl.ANY)] * 4,
        out_specs=[
            pl.BlockSpec(memory_space=pltpu.VMEM),
            pl.BlockSpec(memory_space=pl.ANY),
            *[pl.BlockSpec(memory_space=pltpu.VMEM) for _ in packs],
        ],
        scratch_shapes=[
            *stage,
            *cuts,
            pltpu.VMEM(tile, F32),
            pltpu.VMEM((ctx, shards) + tile, F32),
            pltpu.SemaphoreType.DMA((4 * layers,)),
            pltpu.SemaphoreType.DMA((swaps,)),
            pltpu.SemaphoreType.DMA((swaps,)),
            pltpu.SemaphoreType.DMA((ctx + shards + 1,)),
            pltpu.SemaphoreType.DMA((ctx + shards + 1,)),
            *line_sems(shards),
        ],
        compiler_params=pltpu.CompilerParams(
            collective_id=13, has_side_effects=True, vmem_limit_bytes=VMEM_LIMIT
        ),
    )(gains, *weights)
    return outs[0], outs[1], list(outs[2::2]), list(outs[3::2])


def load_scratch(args):
    return [
        *[pltpu.VMEM(arg.shape, arg.dtype) for arg in args],
        pltpu.SemaphoreType.DMA((len(args),)),
    ]


def pair_of_sems():
    return [pltpu.SemaphoreType.DMA((8,)), pltpu.SemaphoreType.DMA((8,))]


def mlp_backward_call(
    layer, grad_stream, stream, gains, normed, gate_up, weights, summed, base, line
):
    ctx = lax.axis_size("ctx")
    rows, width = normed.shape
    own = base.shape[0]
    columns = weights[0].shape[-1]
    scratch, sems = weight_scratch(weights, width)
    shards = lax.axis_size("shard")
    line_outs, line_scratch = scatter_sums(line, shards)
    firsts = [first for _, first, _ in line]
    loaded = [normed, gate_up, stream, summed, base]
    results = remote_call(
        functools.partial(
            mlp_backward_kernel, ctx, shards, len(weights), 2 * layer + 1, firsts
        ),
        [
            shape_of((own, width), F32),
            shape_of((1, width), F32),
            shape_of((own, width)),
            *line_outs,
            *[shape_of(weight.shape) for weight in weights],
        ],
        [
            *grad_scratch(weights),
            *scratch,
            pltpu.VMEM((rows, columns), BF),
            pltpu.VMEM((rows, columns // 2), BF),
            pltpu.VMEM((own, width), BF),
            pltpu.VMEM((rows, width), BF),
            pltpu.VMEM((rows, width), BF),
            pltpu.VMEM((own, width), F32),
            sems,
            *pair_of_sems(),
            *scatter_scratch(ctx, own, width),
            *pair_of_sems(),
            *scatter_scratch(ctx, own, width),
            *pair_of_sems(),
            *load_scratch(loaded),
            *line_scratch,
        ],
        len(loaded) + len(weights) + len(line),
        kernel_id(3, layer),
        grad_stream,
        gains,
        *loaded,
        *weights,
        *[grads for grads, _, _ in line],
        hbm_out=len(weights),
    )
    (new_dh, gain_grad, total, *sums), outs = results[: -len(weights)], results[-len(weights) :]
    return packed_grads(outs), new_dh, gain_grad[0], total, sums


def mlp_last_call(normed, weights, grad_mlp):
    rows, width = normed.shape
    columns = weights[0].shape[-1]
    scratch, sems = weight_scratch(weights, width)
    *outs, hidden, grad_gate_up = local_call(
        functools.partial(mlp_last_kernel, lax.axis_size("ctx"), len(weights)),
        [
            *[shape_of(weight.shape) for weight in weights],
            shape_of((rows, columns // 2)),
            shape_of((rows, columns)),
        ],
        [
            *grad_scratch(weights),
            pltpu.VMEM((rows, columns // 2), BF),
            pltpu.VMEM((rows, columns), BF),
            *scratch,
            sems,
            *load_scratch((normed, grad_mlp)),
        ],
        6 * rows * width * columns,
        (0, 1 + len(weights)),
        normed,
        grad_mlp,
        *weights,
    )
    return packed_grads(outs), hidden, grad_gate_up


def adam_kernel(rate, decay, kept, pieces, w_ref, m_ref, v_ref, g_ref, *refs):
    new_w, new_m, new_v = refs[kept:]
    if w_ref.shape[-1] == g_ref.shape[-1]:
        grad = g_ref[...].astype(F32).reshape(w_ref.shape)
    else:
        grad = from_members(g_ref[...].astype(F32), pieces)[None]
    new_w[...], new_m[...], new_v[...] = adam_step(
        w_ref[...], m_ref[...], v_ref[...], grad, rate, decay
    )


def adam_layer(layer, slot, weight, moment, square, grad, done, pieces):
    _, rows, columns = weight.shape
    if len(pieces) == 3:
        members, _, width = grad.shape
        parts = 2 if rows % 16 == 0 else 1
        grid = (1, parts)
        grad_spec = pl.BlockSpec((members, rows // parts, width), lambda i, j: (0, j, 0))
        spec = pl.BlockSpec((1, rows // parts, columns), lambda i, j: (layer, j, 0))
    elif len(pieces) == 2:
        members, _, both = grad.shape
        grid, width = (2, members), both // 2
        grad_spec = pl.BlockSpec((1, rows, width), lambda i, j: (j, 0, i))
        spec = pl.BlockSpec((1, rows, width), lambda i, j: (layer, 0, i * members + j))
    else:
        grid, width = (1, 3), columns // 3
        grad_spec = pl.BlockSpec((rows, width), lambda i, j: (0, j))
        spec = pl.BlockSpec((1, rows, width), lambda i, j: (layer, 0, j))
    kept = [] if done is None else list(done)
    size = rows * columns
    return pl.pallas_call(
        functools.partial(adam_kernel, RATES[slot], DECAYS[slot], len(kept), pieces),
        grid=grid,
        out_shape=[shape_of(weight.shape, F32)] * 3,
        in_specs=[spec, spec, spec, grad_spec] + [pl.BlockSpec(memory_space=pl.ANY)] * len(kept),
        out_specs=[spec] * 3,
        input_output_aliases={4 + i: i for i in range(len(kept))},
        cost_estimate=pl.CostEstimate(
            flops=20 * size, bytes_accessed=26 * size, transcendentals=size
        ),
        compiler_params=pltpu.CompilerParams(vmem_limit_bytes=SMALL_LIMIT),
    )(weight, moment, square, grad, *kept)


def in_order(first, then):
    return lax.optimization_barrier((first, then))


def half_rows(shard):
    half = shard.shape[0] // 2
    return lax.dynamic_slice_in_dim(shard, lax.axis_index("dp") * half, half, axis=0)


def member_parts(shard, pieces, ctx):
    parts = []
    for member in range(ctx):
        cut, start = [], 0
        for width in pieces:
            own = width // ctx
            cut.append(shard[:, start + member * own : start + (member + 1) * own])
            start += width
        parts.append(jnp.concatenate(cut, axis=1))
    return parts


def by_member(shard, pieces):
    return jnp.stack(member_parts(shard, pieces, lax.axis_size("ctx")))


def from_members(parts, pieces):
    ctx = parts.shape[0]
    out, start = [], 0
    for width in pieces:
        out += [parts[i, :, start : start + width // ctx] for i in range(ctx)]
        start += width // ctx
    return jnp.concatenate(out, axis=1)


def fold(columns, width):
    if width % columns == 0:
        return "even"
    return "bent" if columns > width and width % (columns - width) == 0 else "cut"


def pack(wide, rows_part):
    columns, (m, width) = wide.shape[1], rows_part.shape
    kind = fold(columns, width)
    if kind == "bent":
        rest = columns - width
        whole = m * width // columns
        right = [rows_part[whole:, i * rest : (i + 1) * rest] for i in range(width // rest)]
        below = jnp.concatenate([rows_part[:whole], jnp.concatenate(right, axis=0)], axis=1)
        return jnp.concatenate([wide, below], axis=0)
    unit = math.gcd(columns, width)
    below = jnp.concatenate(jnp.split(rows_part, width // unit, axis=1), axis=0)
    below = jnp.concatenate(jnp.split(below, columns // unit, axis=0), axis=1)
    return jnp.concatenate([wide, below], axis=0)


def unpack(packed, count, width):
    columns = packed.shape[-1]
    wide, below = packed[..., :count, :], packed[..., count:, :]
    kind = fold(columns, width)
    if kind == "bent":
        rest = columns - width
        right = jnp.split(below[..., width:], width // rest, axis=-2)
        return wide, jnp.concatenate(
            [below[..., :width], jnp.concatenate(right, axis=-1)], axis=-2
        )
    unit = math.gcd(columns, width)
    below = jnp.concatenate(jnp.split(below, columns // unit, axis=-1), axis=-2)
    return wide, jnp.concatenate(jnp.split(below, width // unit, axis=-2), axis=-1)


def pack_share(member_parts, rows_part):
    ctx, rows, columns = member_parts.shape
    return pack(member_parts.reshape(ctx * rows, columns), rows_part)


def spread(whole, width):
    ctx = lax.axis_size("ctx")
    groups, _, columns = whole.shape
    rows = width // (ctx * groups)
    wide, rows_whole = unpack(whole, ctx * rows, width)
    wide = jnp.transpose(wide.reshape(groups, ctx, rows, columns), (1, 0, 2, 3))
    return wide.reshape(-1, columns), rows_whole.reshape(-1, width)


def pack_grads(wide, rows_part):
    ctx, shards = lax.axis_size("ctx"), lax.axis_size("shard")
    columns, width = wide.shape[1], rows_part.shape[1]
    groups = shards * 2
    rows = wide.shape[0] // (ctx * groups)
    wide = jnp.transpose(wide.astype(BF).reshape(ctx, groups, rows, columns), (1, 0, 2, 3))
    wide = wide.reshape(groups, ctx * rows, columns)
    return jax.vmap(pack)(wide, rows_part.astype(BF).reshape(groups, -1, width))


def reduce_grads(packed):
    return lax.psum_scatter(
        packed.reshape(-1, packed.shape[-1]), ("shard", "dp"), scatter_dimension=0, tiled=True
    )


def share_grads(mine, width, collective_id):
    ctx, groups = lax.axis_size("ctx"), lax.axis_size("shard") * 2
    columns = mine.shape[1]
    rows = width // (ctx * groups)
    deep = (mine.shape[0] - ctx * rows) * columns // width
    sums = (mine,)
    if fold(columns, width) == "cut" or rows % 16:
        wide, rows_part = unpack(mine, ctx * rows, width)
        sums = (wide.reshape(ctx, rows, columns), rows_part)
    wide, rows_part = share_plane(sums, ((rows, columns), (deep, width)), collective_id)
    return wide.reshape(ctx, 2 * rows, columns), rows_part.reshape(-1, width)


def rope_select(ctx):
    half_dim = HEAD_DIM // 2
    columns = (HEADS + 2 * KV_HEADS) * HEAD_DIM // ctx
    turned = (HEADS + KV_HEADS) * HEAD_DIM // ctx
    select = np.zeros((3, 128, columns), np.float32)
    for column in range(columns):
        place = column % HEAD_DIM
        if column >= turned:
            select[0, HEAD_DIM + 1, column] = 1.0
        elif place < half_dim:
            select[0, place, column] = 1.0
            select[1, half_dim + place, column] = -1.0
        else:
            select[0, place - half_dim, column] = 1.0
            select[2, place, column] = 1.0
    return np.concatenate(list(select), axis=1)


def body(
    tokens,
    cotangent,
    positions,
    w_qkv,
    w_out,
    w_gate_up,
    w_down,
    norm_gains,
    first_qkv,
    first_out,
    first_gate_up,
    first_down,
    first_gains,
    second_qkv,
    second_out,
    second_gate_up,
    second_down,
    second_gains,
):
    ctx, shards = lax.axis_size("ctx"), lax.axis_size("shard")
    layer_count, own_width, width = w_qkv.shape[0], norm_gains.shape[2], tokens.shape[2]
    width_q, width_kv = HEADS * HEAD_DIM, KV_HEADS * HEAD_DIM
    qkv_pieces, gate_pieces = (width_q, width_kv, width_kv), (FF, FF)
    rows = tokens.shape[1]
    last = layer_count - 1

    lined = shards == 4 and width // (ctx * shards * 2) % 16 == 0
    attn_packs, mlp_packs = [None] * layer_count, [None] * layer_count
    attn_sets, mlp_sets = [None] * layer_count, [None] * layer_count
    if lined:
        gains, whole, attn_packs, mlp_packs = prologue_call(
            norm_gains, (w_qkv, w_out, w_gate_up, w_down), (qkv_pieces, gate_pieces)
        )
        attn_sets[0] = (whole,)
    else:
        tile = norm_gains.astype(BF).astype(F32).reshape(2 * layer_count, own_width)
        tile = jnp.pad(tile, ((0, -2 * layer_count % 8), (0, -own_width % 128)))
        gains = jnp.transpose(small_gather(tile)[..., :own_width], (2, 0, 1, 3))
        gains = gains.reshape(-1, width)
        for layer in range(layer_count):
            parts = by_member(half_rows(w_qkv[layer]).astype(BF), qkv_pieces)
            packed = pack_share(swap_ctx(parts, 2), half_rows(w_out[layer]).astype(BF))
            packed = lax.all_gather(packed, ("shard", "dp"), axis=0)
            attn_sets[layer] = weight_set(packed, width)
            parts = by_member(half_rows(w_gate_up[layer]).astype(BF), gate_pieces)
            packed = pack_share(swap_ctx(parts, 3), half_rows(w_down[layer]).astype(BF))
            packed = lax.all_gather(packed, ("shard", "dp"), axis=0)
            mlp_sets[layer] = weight_set(packed, width)

    angles = rope_angles(positions[0])
    position = positions[0].astype(F32)[:, None]
    angles = jnp.concatenate(
        [jnp.cos(angles), jnp.sin(angles), position, jnp.ones_like(position)], axis=1
    )
    angles = jnp.pad(angles, ((0, 0), (0, 128 - angles.shape[1])))
    select = jnp.asarray(rope_select(ctx))

    stream, grad_stream = tokens[0], cotangent[0]
    saved = []
    if lined:
        per_layer, gates, (angles, grad_top), wholes = forward_call(
            stream, gains, (select, angles), cotangent[0], whole, attn_packs, mlp_packs
        )
        for layer in range(layer_count):
            middle, *kept, normed_two = per_layer[layer]
            saved.append([stream, middle, kept, normed_two])
            mlp_sets[layer] = (wholes[2 * layer],)
            if layer < last:
                stream, gate_up = gates[layer]
                saved[-1].append(gate_up)
                attn_sets[layer + 1] = (wholes[2 * layer + 1],)
    else:
        for layer in range(layer_count):
            middle, kept, more = attn_forward_call(
                layer,
                stream,
                gains,
                attn_sets[layer],
                (select, angles),
                cotangent[0] if layer == 0 else None,
                layer == last,
            )
            saved.append([stream, middle, kept])
            if layer == 0:
                angles, grad_top = more[:2]
            if layer == last:
                saved[-1].append(more[-1])
            else:
                stream, *gate_kept = mlp_forward_call(layer, middle, gains, mlp_sets[layer])
                saved[-1] += gate_kept
    tables = (select, angles)

    params = (w_qkv, w_out, w_gate_up, w_down)
    firsts = (first_qkv, first_out, first_gate_up, first_down)
    seconds = (second_qkv, second_out, second_gate_up, second_down)
    updated = [None] * 4

    def step(layer, slots, grads, pieces):
        for slot, grad, cut in zip(slots, grads, (pieces, ())):
            updated[slot] = adam_layer(
                layer, slot, params[slot], firsts[slot], seconds[slot], grad, updated[slot], cut
            )

    def step_mlp(layer, mine):
        step(layer, (2, 3), share_grads(mine, width, 4), gate_pieces)

    def step_attn(layer, mine):
        step(layer, (0, 1), share_grads(mine, width, 5), qkv_pieces)

    def sum_gains(gain_grads):
        gain_tiles = jnp.stack(gain_grads).reshape(2 * layer_count, ctx, shards, own_width)
        gain_tiles = jnp.transpose(gain_tiles, (2, 1, 0, 3))
        gain_tiles = jnp.pad(
            gain_tiles, ((0, 0), (0, 0), (0, -2 * layer_count % 8), (0, -own_width % 128))
        )
        return small_reduce(gain_tiles)[: 2 * layer_count, :own_width].reshape(norm_gains.shape)

    attn_mine, mlp_mine = [None] * layer_count, [None] * layer_count
    gain_grads = [None] * layer_count
    for layer in reversed(range(layer_count)):
        before, middle, kept, normed_two = saved[layer][:4]
        ends = []
        if layer == last:
            packed, hidden, grad_gate_up = mlp_last_call(normed_two, mlp_sets[layer], grad_top)
            ends = [grad_gate_up, hidden, middle]
        else:
            line = []
            if lined:
                line = [
                    (mlp_mine[layer + 1], cut, mlp_mine[layer + 1].shape[1] - cut),
                    (attn_mine[layer + 1], 0, attn_mine[layer + 1].shape[1]),
                ]
            packed, grad_stream, grad_g2, total, sums = mlp_backward_call(
                layer,
                grad_stream,
                middle,
                gains,
                normed_two,
                saved[layer][4],
                mlp_sets[layer],
                up_part,
                saved[last][1],
                line,
            )
            if lined:
                mlp_mine[layer + 1] = jnp.concatenate([head_sums[0], sums[0]], axis=0)
                attn_mine[layer + 1] = sums[1]
            if layer == last - 1:
                output = total
        line = []
        if lined and layer > 0:
            mlp_mine[layer] = packed
            cut = packed.shape[1] * 8 // 9 // 16 * 16
            line = [(packed, 0, cut)]
        else:
            mlp_mine[layer] = reduce_grads(packed)
        if layer < last and not lined:
            mlp_mine[layer + 1], grad_stream = in_order(mlp_mine[layer + 1], grad_stream)
        packed, grad_stream, grad_g1, more, head_sums = attn_backward_call(
            layer,
            grad_stream,
            before,
            gains,
            kept,
            attn_sets[layer],
            tables,
            ends,
            mlp_sets[layer] if ends else (),
            line,
        )
        if ends:
            grad_g2, up_part = more
        gain_grads[layer] = jnp.stack([grad_g1, grad_g2])
        if layer == 0:
            gain_grad = sum_gains(gain_grads)
        if layer < last:
            packed, mine = in_order(packed, (mlp_mine[layer + 1], attn_mine[layer + 1]))
            step_mlp(layer + 1, mine[0])
            step_attn(layer + 1, mine[1])
            (updated, gain_grad), (mlp_mine[layer], packed) = in_order(
                (updated, gain_grad), (mlp_mine[layer], packed)
            )
        attn_mine[layer] = packed if lined and layer > 0 else reduce_grads(packed)
    step_mlp(0, mlp_mine[0])
    updated, mine = in_order(updated, attn_mine[0])
    step_attn(0, mine)

    updated = list(updated)
    updated.append(
        adam_step(norm_gains, first_gains, second_gains, gain_grad, RATES[4], DECAYS[4])
    )
    return (
        output[None],
        grad_stream[None],
        *[updated[slot][0] for slot in range(5)],
        *[updated[slot][1] for slot in range(5)],
        *[updated[slot][2] for slot in range(5)],
    )


def solution(mesh):
    rows = P(("dp", "shard"), "ctx", None)
    weight = P(None, ("ctx", "shard"), None)
    gain = P(None, None, ("ctx", "shard"))
    group = (weight, weight, weight, weight, gain)
    return jax.shard_map(
        body,
        mesh=mesh,
        in_specs=(rows, rows, P(("dp", "shard"), "ctx"), *group, *group, *group),
        out_specs=(rows, rows, *group, *group, *group),
        check_vma=False,
    )
```

```python
import functools
import math

import jax
import jax.numpy as jnp
import numpy as np
from jax import lax
from jax.experimental import pallas as pl
from jax.experimental.pallas import tpu as pltpu
from jax.sharding import PartitionSpec as P

HEADS = 16
KV_HEADS = 8
HEAD_DIM = 96
FF = 4096
STEP = 10


NORM_EPS = 1e-05
ROPE_BASE = 100000.0
BETA_ONE = 0.9
BETA_TWO = 0.95
ADAM_EPS = 1e-08
DECAY_RATE = 0.1
RATES = (0.05, 1.0, 0.05, 0.03, 0.8)
DECAYS = (DECAY_RATE, DECAY_RATE, DECAY_RATE, DECAY_RATE, 0.0)

BF = jnp.bfloat16
F32 = jnp.float32


def dot(left, right, dims=((1,), (0,))):
    return lax.dot_general(left, right, (dims, ((), ())), preferred_element_type=F32)


def rope_angles(positions):
    powers = 2.0 * np.arange(HEAD_DIM // 2) / HEAD_DIM
    inverse_freq = np.exp(-np.log(ROPE_BASE) * powers).astype(np.float32)
    return positions.astype(F32)[:, None] * inverse_freq[None, :]


def norm_forward(stream, gain):
    inverse = lax.rsqrt(jnp.mean(stream * stream, axis=-1, keepdims=True) + NORM_EPS)
    return (stream * inverse * gain).astype(BF)


def norm_backward(grad_out, gain, stream):
    inverse = lax.rsqrt(jnp.mean(stream * stream, axis=-1, keepdims=True) + NORM_EPS)
    normal_part = stream * inverse
    scaled = grad_out * gain
    gain_grad = jnp.sum(grad_out * normal_part, axis=0, keepdims=True)
    grad_in = inverse * (
        scaled - normal_part * jnp.mean(scaled * normal_part, axis=-1, keepdims=True)
    )
    return (grad_in, gain_grad)


def adam_step(weight, moment, square, grad, rate, decay):
    moment = BETA_ONE * moment + (1.0 - BETA_ONE) * grad
    square = BETA_TWO * square + (1.0 - BETA_TWO) * grad * grad
    moment_hat = moment * (rate / (1.0 - BETA_ONE**STEP))
    square_hat = square * (1.0 / (1.0 - BETA_TWO**STEP))
    weight = weight * (1.0 - rate * decay) - moment_hat / (jnp.sqrt(square_hat) + ADAM_EPS)
    return (weight, moment, square)


MESH = pl.DeviceIdType.MESH
VMEM_LIMIT = 61 * 1024 * 1024
SMALL_LIMIT = 24 * 1024 * 1024


def remote(src, dst, sems, slot, target):
    send, recv = sems
    return pltpu.make_async_remote_copy(
        src_ref=src,
        dst_ref=dst,
        send_sem=send.at[slot],
        recv_sem=recv.at[slot],
        device_id=target,
        device_id_type=MESH,
    )


def greet(targets):
    barrier = pltpu.get_barrier_semaphore()
    for target in targets:
        pl.semaphore_signal(barrier, inc=1, device_id=target, device_id_type=MESH)
    pl.semaphore_wait(barrier, len(targets))


def ctx_peers(ctx):
    me = lax.axis_index("ctx")
    return [{"ctx": lax.rem(me + step, ctx)} for step in range(1, ctx)]


def square():
    me = lax.axis_index("ctx")
    x, y = lax.rem(me, 2), me // 2
    return me, 2 * y + 1 - x, 2 * (1 - y) + x, 3 - me


def neighbours(ctx):
    if ctx != 4:
        return ctx_peers(ctx)
    _, xn, yn, _ = square()
    return [{"ctx": xn}, {"ctx": yn}]


def gather_steps(ctx, x_ref, o_ref, send, recv):
    rows = x_ref.shape[0]
    sems = (send, recv)

    def block(owner, part=None):
        if part is None:
            return pl.ds(pl.multiple_of(owner * rows, rows), rows)
        return pl.ds(pl.multiple_of(owner * rows + part * (rows // 2), rows // 2), rows // 2)

    if ctx != 4:
        me = lax.axis_index("ctx")
        copies = [
            remote(x_ref, o_ref.at[block(me)], sems, i, peer)
            for i, peer in enumerate(ctx_peers(ctx))
        ]
        for copy in copies:
            copy.start()
        o_ref[block(me), :] = x_ref[...]
        yield
        yield
        for copy in copies:
            copy.wait()
        return
    me, xn, yn, _ = square()
    to_x, to_y = {"ctx": xn}, {"ctx": yn}
    half = rows // 2
    low, high = pl.ds(0, half), pl.ds(half, half)
    first = remote(x_ref.at[low], o_ref.at[block(me, 0)], sems, 0, to_x)
    second = remote(x_ref.at[high], o_ref.at[block(me, 1)], sems, 1, to_y)
    third = remote(x_ref.at[high], o_ref.at[block(me, 1)], sems, 2, to_x)
    fourth = remote(x_ref.at[low], o_ref.at[block(me, 0)], sems, 3, to_y)
    first.start()
    second.start()
    third.start()
    fourth.start()
    o_ref[block(me), :] = x_ref[...]
    yield
    first.wait_recv()
    fifth = remote(o_ref.at[block(xn, 0)], o_ref.at[block(xn, 0)], sems, 4, to_y)
    fifth.start()
    second.wait_recv()
    sixth = remote(o_ref.at[block(yn, 1)], o_ref.at[block(yn, 1)], sems, 5, to_x)
    sixth.start()
    yield
    first.wait_send()
    second.wait_send()
    third.wait()
    fourth.wait()
    fifth.wait()
    sixth.wait()


def finish(steps):
    for _ in steps:
        pass


def gather_kernel(ctx, *refs):
    greet(neighbours(ctx))
    finish(gather_steps(ctx, *refs))


def scatter_steps(ctx, p_ref, base_ref, o_ref, relay, mixed, landed, send, recv):
    rows = o_ref.shape[0]
    sems = (send, recv)

    def block(owner, part=None):
        if part is None:
            return pl.ds(pl.multiple_of(owner * rows, rows), rows)
        return pl.ds(pl.multiple_of(owner * rows + part * (rows // 2), rows // 2), rows // 2)

    if ctx != 4:
        me = lax.axis_index("ctx")
        peers = ctx_peers(ctx)
        copies = [
            remote(p_ref.at[block(peer["ctx"])], landed.at[i], sems, i, peer)
            for i, peer in enumerate(peers)
        ]
        for copy in copies:
            copy.start()
        yield
        yield
        total = p_ref[block(me), :].astype(F32)
        if base_ref is not None:
            total = total + base_ref[...].astype(F32)
        for i, copy in enumerate(copies):
            copy.wait()
            total = total + landed[i].astype(F32)
        o_ref[...] = total.astype(o_ref.dtype)
        return
    me, xn, yn, far = square()
    to_x, to_y = {"ctx": xn}, {"ctx": yn}
    half = rows // 2
    low, high = pl.ds(0, half), pl.ds(half, half)
    first = remote(p_ref.at[block(far, 0)], relay.at[0], sems, 0, to_x)
    second = remote(p_ref.at[block(far, 1)], relay.at[1], sems, 1, to_y)
    third = remote(p_ref.at[block(xn, 0)], landed.at[0, low], sems, 2, to_x)
    fourth = remote(p_ref.at[block(yn, 1)], landed.at[1, high], sems, 3, to_y)
    first.start()
    second.start()
    third.start()
    fourth.start()
    yield
    first.wait_recv()
    mixed[0] = (relay[0].astype(F32) + p_ref[block(yn, 0), :].astype(F32)).astype(BF)
    fifth = remote(mixed.at[0], landed.at[1, low], sems, 4, to_y)
    fifth.start()
    second.wait_recv()
    mixed[1] = (relay[1].astype(F32) + p_ref[block(xn, 1), :].astype(F32)).astype(BF)
    sixth = remote(mixed.at[1], landed.at[0, high], sems, 5, to_x)
    sixth.start()
    yield
    first.wait_send()
    second.wait_send()
    third.wait()
    fourth.wait()
    fifth.wait()
    sixth.wait()
    total = p_ref[block(me), :].astype(F32)
    if base_ref is not None:
        total = total + base_ref[...].astype(F32)
    total = total + landed[0].astype(F32) + landed[1].astype(F32)
    o_ref[...] = total.astype(o_ref.dtype)


def scatter_scratch(ctx, rows, columns):
    slots = 2 if ctx == 4 else ctx - 1
    return [
        pltpu.VMEM((2, rows // 2, columns), BF),
        pltpu.VMEM((2, rows // 2, columns), BF),
        pltpu.VMEM((slots, rows, columns), BF),
    ]


def swap_kernel(ctx, x_ref, o_ref, send, recv):
    me = lax.axis_index("ctx")
    peers = ctx_peers(ctx)
    greet(peers)
    copies = [
        remote(x_ref.at[peer["ctx"]], o_ref.at[me], (send, recv), i, peer)
        for i, peer in enumerate(peers)
    ]
    for copy in copies:
        copy.start()
    o_ref[me] = x_ref[me]
    for copy in copies:
        copy.wait()


def share_kernel(ctx, packed, *refs):
    sources, (ox_ref, oy_ref, send, recv) = refs[: 1 if packed else 2], refs[1 if packed else 2 :]
    me, core = lax.axis_index("ctx"), lax.axis_index("dp")
    peers, other = ctx_peers(ctx), {"dp": 1 - core}
    rows, width = ox_ref.shape[2], oy_ref.shape[2]
    greet(peers + [other])
    sems = (send, recv)

    def chunk(member):
        if packed:
            return sources[0].at[pl.ds(pl.multiple_of(member * rows, rows), rows)]
        return sources[0].at[member]

    across = [
        remote(chunk(peer["ctx"]), ox_ref.at[me, core], sems, i, peer)
        for i, peer in enumerate(peers)
    ]
    for copy in across:
        copy.start()
    if packed:
        _, parts = below_parts((1,) + sources[0].shape, ctx * rows, width)
        for row, size, column, part, own_row, own_column in parts:
            oy_ref[core, own_row : own_row + size, own_column : own_column + part] = sources[0][
                row : row + size, column : column + part
            ]
    else:
        oy_ref[core] = sources[1][...]
    ox_ref[me, core] = chunk(me)[...]
    inside = [
        remote(ox_ref.at[me, core], ox_ref.at[me, core], sems, ctx, other),
        remote(oy_ref.at[core], oy_ref.at[core], sems, ctx + 1, other),
    ]
    for copy in inside:
        copy.start()
    for i, copy in enumerate(across):
        copy.wait_recv()
        source = lax.rem(me + ctx - 1 - i, ctx)
        block = ox_ref.at[source, core]
        inside.append(remote(block, block, sems, ctx + 2 + i, other))
        inside[-1].start()
    for copy in across:
        copy.wait_send()
    for copy in inside:
        copy.wait()


def call(kernel, out_shape, scratch, copies, collective_id, *args, limit=VMEM_LIMIT):
    return pl.pallas_call(
        kernel,
        out_shape=out_shape,
        in_specs=[pl.BlockSpec(memory_space=pltpu.VMEM)] * len(args),
        out_specs=jax.tree.map(lambda _: pl.BlockSpec(memory_space=pltpu.VMEM), out_shape),
        scratch_shapes=[
            *scratch,
            pltpu.SemaphoreType.DMA((copies,)),
            pltpu.SemaphoreType.DMA((copies,)),
        ],
        compiler_params=pltpu.CompilerParams(
            collective_id=collective_id, has_side_effects=True, vmem_limit_bytes=limit
        ),
    )(*args)


def shape_of(shape, dtype=BF):
    return jax.ShapeDtypeStruct(shape, dtype)


def gather_ctx(block):
    ctx = lax.axis_size("ctx")
    rows, columns = block.shape
    return call(
        functools.partial(gather_kernel, ctx), shape_of((ctx * rows, columns)), [], 8, 0, block
    )


def swap_ctx(parts, collective_id):
    ctx = lax.axis_size("ctx")
    return call(
        functools.partial(swap_kernel, ctx), shape_of(parts.shape), [], ctx, collective_id, parts
    )


def share_plane(sums, shapes, collective_id):
    ctx = lax.axis_size("ctx")
    return call(
        functools.partial(share_kernel, ctx, len(sums) == 1),
        [shape_of((ctx, 2) + shapes[0]), shape_of((2,) + shapes[1])],
        [],
        2 * ctx + 1,
        collective_id,
        *sums,
        limit=SMALL_LIMIT,
    )


def small_reduce_kernel(ctx, shards, x_ref, o_ref, first, column, second, third, send, recv):
    me, mine = lax.axis_index("ctx"), lax.axis_index("shard")
    along = [{"shard": lax.rem(mine + step, shards)} for step in range(1, shards)]
    across = ctx_peers(ctx)
    other = {"dp": 1 - lax.axis_index("dp")}
    greet(along + across + [other])
    sems = (send, recv)
    copies = [
        remote(x_ref.at[target["shard"]], first.at[i], sems, i, target)
        for i, target in enumerate(along)
    ]
    for copy in copies:
        copy.start()
    total = x_ref[mine]
    for i, copy in enumerate(copies):
        copy.wait()
        total = total + first[i]
    column[...] = total
    copies = [
        remote(column.at[target["ctx"]], second.at[i], sems, shards + i, target)
        for i, target in enumerate(across)
    ]
    for copy in copies:
        copy.start()
    total = column[me]
    for i, copy in enumerate(copies):
        copy.wait()
        total = total + second[i]
    third[0] = total
    copy = remote(third.at[0], third.at[1], sems, shards + ctx, other)
    copy.start()
    copy.wait()
    o_ref[...] = third[0] + third[1]


def small_gather(tile):
    ctx, shards = lax.axis_size("ctx"), lax.axis_size("shard")
    return call(
        functools.partial(small_gather_kernel, ctx, shards),
        shape_of((ctx, shards) + tile.shape, F32),
        [],
        ctx + shards + 1,
        6,
        tile,
    )


def small_reduce(tiles):
    shards, ctx = tiles.shape[:2]
    tile = tiles.shape[2:]
    return call(
        functools.partial(small_reduce_kernel, ctx, shards),
        shape_of(tile, F32),
        [
            pltpu.VMEM((shards - 1, ctx) + tile, F32),
            pltpu.VMEM((ctx,) + tile, F32),
            pltpu.VMEM((ctx - 1,) + tile, F32),
            pltpu.VMEM((2,) + tile, F32),
        ],
        ctx + shards + 1,
        7,
        tiles,
    )


def below_parts(packed_shape, count, width):
    columns = packed_shape[2]
    below = packed_shape[1] - count
    if fold(columns, width) == "even":
        rows = below * columns // width
        return rows, [
            (count + i * rows, rows, 0, columns, 0, i * columns) for i in range(width // columns)
        ]
    rest = columns - width
    part = below // (width // rest)
    parts = [(count, below, 0, width, 0, 0)]
    for i in range(width // rest):
        parts.append((count + i * part, part, width, rest, below, i * rest))
    return below + part, parts


def load_pair(ctx, refs, wide_ref, deep_ref, sems):
    if len(refs) == 2:
        wide = [pltpu.make_async_copy(refs[0], wide_ref, sems.at[0])]
        deep = [pltpu.make_async_copy(refs[1], deep_ref, sems.at[1])]
        wide[0].start()
        deep[0].start()
        return wide, deep
    packed_ref = refs[0]
    groups = packed_ref.shape[0]
    rows = wide_ref.shape[0] // (ctx * groups)
    own_rows, parts = below_parts(packed_ref.shape, ctx * rows, deep_ref.shape[1])
    wide, deep = [], []
    for group in range(groups):
        for member in range(ctx):
            source = packed_ref.at[group, pl.ds(member * rows, rows)]
            target = wide_ref.at[pl.ds((member * groups + group) * rows, rows)]
            wide.append((source, target))
        for row, count, column, width, own_row, own_column in parts:
            source = packed_ref.at[group, pl.ds(row, count), pl.ds(column, width)]
            target = deep_ref.at[
                pl.ds(group * own_rows + own_row, count), pl.ds(own_column, width)
            ]
            deep.append((source, target))
    wide = [pltpu.make_async_copy(*pair, sems.at[i]) for i, pair in enumerate(wide)]
    deep = [pltpu.make_async_copy(*pair, sems.at[len(wide) + i]) for i, pair in enumerate(deep)]
    for copy in wide + deep:
        copy.start()
    return wide, deep


def start_loads(sources, targets, sems):
    copies = [
        pltpu.make_async_copy(source, target, sems.at[i])
        for i, (source, target) in enumerate(zip(sources, targets))
    ]
    for copy in copies:
        copy.start()
    return copies


def wait_all(copies):
    for copy in copies:
        copy.wait()


def z_gather_steps(shards, parts, eager, src, out, local_sems, send, recv):
    mine, core = lax.axis_index("shard"), lax.axis_index("dp")
    other = {"dp": 1 - core}
    sems = (send, recv)
    hops = shards - 1
    inside = 2 * hops * len(parts)

    def source(part):
        return src.at[pl.ds(*parts[part])]

    def place(owner, part):
        return out.at[owner * 2 + core, pl.ds(*parts[part])]

    def number(way, hop, part):
        return (way * hops + hop) * len(parts) + part

    def sent(way, hop, part):
        step = 1 - 2 * way
        owner = mine - step * hop
        block = source(part) if hop == 0 else place(owner, part)
        target = {"shard": mine + step}
        return remote(block, place(owner, part), sems, number(way, hop, part), target)

    def landed(way, hop, part):
        step = 1 - 2 * way
        block = place(mine - step * (hop + 1), part)
        return remote(block, block, sems, number(way, hop, part), {"shard": mine - step})

    def shared(way, hop, part):
        step = 1 - 2 * way
        block = place(mine - step * (hop + 1), part)
        slot = inside + len(parts) + number(way, hop, part)
        return remote(block, block, sems, slot, other)

    def own(part):
        return remote(source(part), place(mine, part), sems, inside + part, other)

    def local(part):
        return pltpu.make_async_copy(source(part), place(mine, part), local_sems.at[part])

    def sends(way, hop):
        if way == 0:
            return jnp.logical_and(mine >= hop, mine < shards - 1)
        return jnp.logical_and(mine < shards - hop, mine > 0)

    def receives(way, hop):
        return mine > hop if way == 0 else mine < shards - 1 - hop

    for part in range(len(parts)):
        for way in range(2):
            pl.when(sends(way, 0))(lambda way=way, part=part: sent(way, 0, part).start())
        if not eager:
            local(part).start()
            own(part).start()
            yield
    if eager:
        for part in range(len(parts)):
            local(part).start()
            own(part).start()
        yield
    for hop in range(hops):
        for part in range(len(parts)):
            for way in range(2):

                def arrived(way=way, hop=hop, part=part):
                    landed(way, hop, part).wait_recv()

                def hand_on(way=way, hop=hop, part=part):
                    sent(way, hop + 1, part).start()

                def share(way=way, hop=hop, part=part):
                    shared(way, hop, part).start()

                pl.when(receives(way, hop))(arrived)
                if hop + 1 < hops:
                    pl.when(sends(way, hop + 1))(hand_on)
                pl.when(receives(way, hop))(share)
            yield
    for part in range(len(parts)):
        local(part).wait()
        own(part).wait()
        for way in range(2):
            for hop in range(hops):
                pl.when(sends(way, hop))(
                    lambda way=way, hop=hop, part=part: sent(way, hop, part).wait_send()
                )
                pl.when(receives(way, hop))(
                    lambda way=way, hop=hop, part=part: shared(way, hop, part).wait()
                )


def z_scatter_steps(shards, first, parts, src, out, pair, own, land, load_sems, send, recv):
    mine, core = lax.axis_index("shard"), lax.axis_index("dp")
    other = {"dp": 1 - core}
    sems = (send, recv)
    hops = shards - 1
    rows = pl.ds(first, out.shape[0])
    order = sorted(range(shards), key=lambda owner: min(owner, hops - owner))
    places = (mine, hops - mine)

    def crossed(owner):
        source = src.at[owner * 2 + 1 - core, rows]
        return remote(source, pair.at[owner], sems, owner, other)

    def loaded(owner):
        source = src.at[owner * 2 + core, rows]
        return pltpu.make_async_copy(source, own.at[owner], load_sems.at[owner])

    def slot_of(way, turn, part):
        return shards + (way * hops + turn) * len(parts) + part

    def handed(way, turn, part, block=None):
        target = {"shard": mine + 1 - 2 * way}
        there = land.at[way, turn, pl.ds(*parts[part])]
        number = slot_of(way, turn, part)
        return remote(there if block is None else block, there, sems, number, target)

    def begun(way, turn, part):
        owner = hops - turn if way == 0 else turn
        return handed(way, turn, part, pair.at[owner, pl.ds(*parts[part])])

    for owner in order[:2]:
        crossed(owner).start()
        loaded(owner).start()
    yield
    for owner in order:
        if owner == order[2]:
            yield
        loaded(owner).wait()
        crossed(owner).wait_recv()
        if owner == order[0]:
            for later in order[2:]:
                crossed(later).start()
                loaded(later).start()
        pair[owner] = (own[owner].astype(F32) + pair[owner].astype(F32)).astype(BF)
        for way in range(2):
            if owner == (hops if way == 0 else 0):

                def begin(way=way):
                    for part in range(len(parts)):
                        begun(way, 0, part).start()

                pl.when(places[way] == 0)(begin)
    yield
    for slot in range(1, shards):
        for part in range(len(parts)):
            here = pl.ds(*parts[part])
            for way, place in enumerate(places):
                turn = slot - place

                def go_on(way=way, part=part, slot=slot):
                    begun(way, slot - 1, part).wait_send()
                    begun(way, slot, part).start()

                def hand_on(way=way, turn=turn, part=part, here=here):
                    handed(way, turn, part).wait_recv()
                    block = land.at[way, turn, here]
                    owner = hops - turn if way == 0 else turn
                    added = pair[owner, here].astype(F32)
                    block[...] = (block[...].astype(F32) + added).astype(BF)
                    handed(way, turn, part).start()

                def arrived(way=way, turn=turn, part=part):
                    handed(way, turn, part).wait_recv()

                on_the_way = jnp.logical_and(place > 0, place <= slot)
                if slot < hops:
                    pl.when(place == 0)(go_on)
                    pl.when(on_the_way)(hand_on)
                else:
                    pl.when(on_the_way)(arrived)
            yield
    for owner in range(shards):
        crossed(owner).wait_send()
    for part in range(len(parts)):
        for way, place in enumerate(places):
            pl.when(place == 0)(
                lambda way=way, part=part: begun(way, hops - 1, part).wait_send()
            )
            for turn in range(hops):
                pl.when(jnp.logical_and(place > 0, place + turn < hops))(
                    lambda way=way, part=part, turn=turn: handed(way, turn, part).wait_send()
                )
    out[...] = pair[mine]
    for way, place in enumerate(places):

        def add(way=way, place=place):
            out[...] = (out[...].astype(F32) + land[way, hops - place].astype(F32)).astype(BF)

        pl.when(place > 0)(add)


def scatter_sums(line, shards):
    outs, scratch = [], []
    for grads, _, rows in line:
        block = (rows, grads.shape[2])
        outs.append(shape_of(block))
        count = shards + 4 * (shards - 1)
        scratch += [
            pltpu.VMEM((shards,) + block, BF),
            pltpu.VMEM((shards,) + block, BF),
            pltpu.VMEM((2, shards - 1) + block, BF),
            pltpu.SemaphoreType.DMA((shards,)),
            pltpu.SemaphoreType.DMA((count,)),
            pltpu.SemaphoreType.DMA((count,)),
        ]
    return outs, scratch


def scatter_lines(ctx, shards, firsts, sources, outs, scratch):
    if not firsts:
        greet(neighbours(ctx))
        return []
    greet_line(ctx, shards)
    lines = []
    for i, first in enumerate(firsts):
        parts = halves(outs[i].shape[0])
        lines.append(
            z_scatter_steps(
                shards, first, parts, sources[i], outs[i], *scratch[6 * i : 6 * i + 6]
            )
        )
    return lines


def halves(rows):
    half = rows // 32 * 16
    return [(0, half), (half, rows - half)]


def greet_line(ctx, shards):
    mine = lax.axis_index("shard")
    barrier = pltpu.get_barrier_semaphore()

    def signal(target):
        pl.semaphore_signal(barrier, inc=1, device_id=target, device_id_type=MESH)

    targets = neighbours(ctx) + [{"dp": 1 - lax.axis_index("dp")}]
    for target in targets:
        signal(target)
    pl.when(mine > 0)(lambda: signal({"shard": mine - 1}))
    pl.when(mine < shards - 1)(lambda: signal({"shard": mine + 1}))
    at_end = jnp.logical_or(mine == 0, mine == shards - 1)
    pl.when(at_end)(lambda: pl.semaphore_wait(barrier, len(targets) + 1))
    pl.when(jnp.logical_not(at_end))(lambda: pl.semaphore_wait(barrier, len(targets) + 2))


def line_sems(shards):
    count = 8 * (shards - 1) + 2
    return [
        pltpu.SemaphoreType.DMA((2,)),
        pltpu.SemaphoreType.DMA((count,)),
        pltpu.SemaphoreType.DMA((count,)),
    ]


def small_gather_steps(ctx, shards, x_ref, o_ref, send, recv):
    me, mine = lax.axis_index("ctx"), lax.axis_index("shard")
    along = [{"shard": lax.rem(mine + step, shards)} for step in range(1, shards)]
    o_ref[me, mine] = x_ref[...]
    copies = [
        remote(x_ref, o_ref.at[me, mine], (send, recv), i, target)
        for i, target in enumerate(along)
    ]
    for copy in copies:
        copy.start()
    yield
    wait_all(copies)
    copies = [
        remote(o_ref.at[me], o_ref.at[me], (send, recv), shards + i, target)
        for i, target in enumerate(ctx_peers(ctx))
    ]
    for copy in copies:
        copy.start()
    yield
    wait_all(copies)


def small_gather_kernel(ctx, shards, *refs):
    mine = lax.axis_index("shard")
    greet([{"shard": lax.rem(mine + step, shards)} for step in range(1, shards)] + ctx_peers(ctx))
    finish(small_gather_steps(ctx, shards, *refs))


def place_deep(block, packed_ref, count):
    columns = packed_ref.shape[1]
    _, parts = below_parts((1,) + packed_ref.shape, count, block.shape[1])
    for row, size, column, width, own_row, own_column in parts:
        packed_ref[row : row + size, column : column + width] = block[
            own_row : own_row + size, own_column : own_column + width
        ]


def gain_rows(tiles_ref, own_width):
    ctx, shards = tiles_ref.shape[:2]
    parts = [tiles_ref[i, j][:, :own_width] for i in range(ctx) for j in range(shards)]
    return jnp.concatenate(parts, axis=1)


def begin_packs(ctx, numbers, pieces, loads, stage, cuts, packs, swap_sems, begin, serve):
    me = lax.axis_index("ctx")
    peers = ctx_peers(ctx)
    swaps = []
    for number in numbers:
        pack_ref, cut = packs[number], cuts[number]
        wide, deep = 2 * number, 2 * number + 1
        rows = cut.shape[1]
        loads[deep].wait()
        place_deep(stage[deep][...].astype(BF), pack_ref, ctx * rows)
        if number == 0:
            begin()
        loads[wide].wait()
        for member, part in enumerate(member_parts(stage[wide][...], pieces[number % 2], ctx)):
            cut[member] = part.astype(BF)
        here = pl.ds(pl.multiple_of(me * rows, rows), rows)
        first = number * (ctx - 1)
        copies = [
            remote(cut.at[peer["ctx"]], pack_ref.at[here], swap_sems, first + i, peer)
            for i, peer in enumerate(peers)
        ]
        for copy in copies:
            copy.start()
        pack_ref[here, :] = cut[me]
        if number == 0:
            wait_all(copies)
            begin()
        else:
            swaps += copies
            if number == 1:
                serve()
    return swaps


def store_gate_grad(ctx, normed_ref, grad_gu, refs, outs, sems):
    width = normed_ref.shape[1] // ctx
    groups = refs[0].shape[0] if len(refs) == 1 else 1
    rows = width // groups

    def leave(member):
        here = pl.ds(member * rows, rows)
        if len(refs) == 2:
            source, target = refs[0].at[here], outs[0].at[here]
        else:
            source, target = refs[0].at[:, here], outs[0].at[:, here]
        return pltpu.make_async_copy(source, target, sems.at[member])

    def make(member):
        if isinstance(member, int):
            left = normed_ref[:, member * width : (member + 1) * width]
        else:
            left = normed_ref[:, pl.ds(pl.multiple_of(member * width, width), width)]
        part = dot(left, grad_gu[...], ((0,), (0,))).astype(BF)
        for group in range(groups):
            here = pl.ds(member * rows, rows)
            if not isinstance(member, int):
                here = pl.ds(pl.multiple_of(member * rows, rows), rows)
            block = part[group * rows : (group + 1) * rows]
            if len(refs) == 2:
                refs[0][here, :] = block
            else:
                refs[0][group, here, :] = block
        leave(member).start()

    for members in (range(ctx // 2), range(ctx // 2, ctx)):
        if width % 128:
            for member in members:
                make(member)
        else:
            pl.loop(members.start, members.stop)(make)
        yield [leave(member) for member in members]


def store_down_grad(ctx, hidden, grad_ref, refs, outs, sems):
    if len(refs) == 2:
        refs[1][...] = dot(hidden[...], grad_ref[...], ((0,), (0,))).astype(BF)
        copy = pltpu.make_async_copy(refs[1], outs[1], sems.at[ctx])
        copy.start()
        return copy
    packed_ref = refs[0]
    groups, width = packed_ref.shape[0], grad_ref.shape[1]
    count = width // groups
    own_rows, parts = below_parts(packed_ref.shape, count, width)
    together = 128 // math.gcd(128, own_rows)

    @pl.loop(0, groups // together)
    def _(step):
        lanes = together * own_rows
        block = hidden[:, pl.ds(pl.multiple_of(step * lanes, lanes), lanes)]
        block = dot(block, grad_ref[...], ((0,), (0,))).astype(BF)
        for group in range(together):
            for row, size, column, columns, own_row, own_column in parts:
                own_row += group * own_rows
                packed_ref[
                    step * together + group, row : row + size, column : column + columns
                ] = block[own_row : own_row + size, own_column : own_column + columns]

    here = pl.ds(count, packed_ref.shape[1] - count)
    copy = pltpu.make_async_copy(packed_ref.at[:, here], outs[0].at[:, here], sems.at[ctx])
    copy.start()
    return copy


def grad_scratch(weights):
    return [
        *[pltpu.VMEM(weight.shape, BF) for weight in weights],
        pltpu.SemaphoreType.DMA((lax.axis_size("ctx") + 1,)),
    ]


def sigmoid(value):
    return 1.0 / (1.0 + jnp.exp(-value))


def mlp_stage(ctx, serve, load, stream_ref, gain, new_ref, normed_ref, gu_ref, wgu, wd, own, part, comm):
    serve()
    own[...] = norm_forward(stream_ref[...], gain)
    gathered = gather_steps(ctx, own, normed_ref, *comm[:2])
    next(gathered)
    serve()
    wide, deep = load()
    next(gathered)
    serve()
    finish(gathered)
    serve()
    wait_all(wide)
    gu_ref[...] = dot(normed_ref[...], wgu[...])
    serve()
    half = gu_ref.shape[1] // 2
    gate, up = gu_ref[:, :half], gu_ref[:, half:]
    hidden = (gate * sigmoid(gate) * up).astype(BF)
    wait_all(deep)
    part[...] = dot(hidden, wd[...]).astype(BF)
    scattered = scatter_steps(ctx, part, stream_ref, new_ref, *comm[2:])
    next(scattered)
    serve()
    next(scattered)
    serve()
    finish(scattered)
    serve()


def mlp_forward_kernel(ctx, count, row, stream_ref, gains_ref, *refs):
    weights = refs[:count]
    new_ref, normed_ref, gu_ref, wgu, wd, own, part, sems, *comm = refs[count:]
    greet(neighbours(ctx))
    mlp_stage(
        ctx,
        lambda: None,
        lambda: load_pair(ctx, weights, wgu, wd, sems),
        stream_ref,
        gains_ref[row : row + 1],
        new_ref,
        normed_ref,
        gu_ref,
        wgu,
        wd,
        own,
        part,
        comm,
    )


def rope(value, tables, back=False):
    cosine, ahead, behind = tables
    width, half_dim = value.shape[1], HEAD_DIM // 2
    turned = pltpu.roll(value, width - half_dim, 1) * ahead[...]
    turned = turned + pltpu.roll(value, half_dim, 1) * behind[...]
    return value * cosine[...] + (-turned if back else turned)


def head_of(ref, index):
    return ref[:, index * HEAD_DIM : (index + 1) * HEAD_DIM]


def exact_dot(left, right, dims=((1,), (0,))):
    return lax.dot_general(
        left, right, (dims, ((), ())), precision=lax.Precision.HIGHEST, preferred_element_type=F32
    )


def build_tables(angle_ref, select_ref, tables, bias):
    width = tables[0].shape[1]
    for i, table in enumerate(tables):
        table[...] = exact_dot(angle_ref[...], select_ref[:, i * width : (i + 1) * width])
    lanes = lax.broadcasted_iota(jnp.int32, (8, angle_ref.shape[1]), 1)
    pick = jnp.where(lanes == HEAD_DIM, 1.0, 0.0)
    key_pos = exact_dot(pick, angle_ref[...], ((1,), (1,)))[:1]
    query_pos = angle_ref[:, HEAD_DIM : HEAD_DIM + 1]
    bias[...] = jnp.where(key_pos <= query_pos, 0.0, -1000000000.0)


def attn_stage(
    ctx, serve, load, prepare, stream_ref, gain, kept, new_ref, wq, wo, own, part, tables, bias, comm
):
    normed_ref, qkv_ref, att_ref, lse_ref = kept
    own[...] = norm_forward(stream_ref[...].astype(F32), gain)
    gathered = gather_steps(ctx, own, normed_ref, *comm[:2])
    next(gathered)
    wide, deep = load()
    next(gathered)
    prepare()
    finish(gathered)
    serve()
    wait_all(wide)
    qkv_ref[...] = rope(dot(normed_ref[...], wq[...]), tables).astype(BF)
    kv_heads = qkv_ref.shape[1] // (4 * HEAD_DIM)
    lane = lax.broadcasted_iota(jnp.int32, lse_ref.shape, 1)
    mixed, lse = [], jnp.zeros(lse_ref.shape, F32)
    for head in range(2 * kv_heads):
        query = head_of(qkv_ref, head)
        key = head_of(qkv_ref, 2 * kv_heads + head // 2)
        value = head_of(qkv_ref, 3 * kv_heads + head // 2)
        scores = dot(query, key, ((1,), (1,))) * HEAD_DIM ** (-0.5) + bias[...]
        top = jnp.max(scores, axis=1, keepdims=True)
        terms = jnp.exp(scores - top)
        total = jnp.sum(terms, axis=1, keepdims=True)
        probs = (terms * (1.0 / total)).astype(BF)
        mixed.append(dot(probs, value).astype(BF))
        lse = jnp.where(lane == head, top + jnp.log(total), lse)
    att_ref[...] = jnp.concatenate(mixed, axis=1)
    lse_ref[...] = lse
    wait_all(deep)
    part[...] = dot(att_ref[...], wo[...]).astype(BF)
    scattered = scatter_steps(ctx, part, stream_ref, new_ref, *comm[2:])
    next(scattered)
    serve()
    finish(scattered)
    serve()


def attn_forward_kernel(ctx, count, row, is_first, is_last, *refs):
    refs = list(refs)

    def take(on=True):
        return refs.pop(0) if on else None

    stream_ref, gains_ref = take(), take()
    sources = [take() for _ in range(3 if is_first else 2)]
    weights = [take() for _ in range(count)]
    new_ref, *kept = [take() for _ in range(5)]
    angles_out, top_out = take(is_first), take(is_first)
    next_normed = take(is_last)
    wq, wo, bias, own, part, *tables = [take() for _ in range(8)]
    sems = take()
    comm = [take() for _ in range(7)]
    extra = [take() for _ in range(4)]
    loaded = [take() for _ in sources]
    load_sems = take()
    select_ref, angle_ref, *top_ref = loaded
    loads = start_loads(sources, loaded, load_sems)
    greet(neighbours(ctx))

    def prepare():
        wait_all(loads)
        if is_first:
            finish(gather_steps(ctx, angle_ref, angles_out, *extra[:2]))
        build_tables(angles_out if is_first else angle_ref, select_ref, tables, bias)

    attn_stage(
        ctx,
        lambda: None,
        lambda: load_pair(ctx, weights, wq, wo, sems),
        prepare,
        stream_ref,
        gains_ref[row : row + 1],
        kept,
        new_ref,
        wq,
        wo,
        own,
        part,
        tables,
        bias,
        comm,
    )
    if is_first:
        finish(gather_steps(ctx, top_ref[0], top_out, *extra[2:]))
    if is_last:
        own[...] = norm_forward(new_ref[...], gains_ref[row + 1 : row + 2])
        finish(gather_steps(ctx, own, next_normed, *extra[2:]))


def z_stream(hops, gathers, counts):
    for done, (steps, count) in enumerate(zip(gathers, counts)):
        for turn in range(hops * count):
            next(steps)
            if turn == (hops - 1) * count - 1 and done + 1 < len(gathers):
                next(gathers[done + 1])
            yield done
        finish(steps)
        yield done + 1


def forward_kernel(ctx, shards, layers, pieces, *refs):
    refs = list(refs)

    def take(count):
        taken = refs[:count]
        del refs[:count]
        return taken

    last = layers - 1
    stream_ref, own_gains_ref = take(2)
    sources = take(3)
    weights = take(4)
    kept_out = [take(6) for _ in range(layers)]
    gate_out = [take(2) for _ in range(last)]
    common_out = take(3)
    whole_refs = take(2 * layers)
    kept_refs = [take(6) for _ in range(layers)]
    gate_refs = [take(2) for _ in range(last)]
    angles_ref, tops_ref, gains_ref = take(3)
    wq, wo, wgu, wd, bias, own, part = take(7)
    tables = take(3)
    attn_sems, mlp_sems, out_sems = take(3)
    comm, extra, loaded = take(7), take(4), take(3)
    (load_sems,) = take(1)
    stage, cuts, packs = take(4 * layers), take(2 * layers), take(2 * layers)
    tile_ref, tiles_ref, stage_sems, swap_send, swap_recv, small_send, small_recv = take(7)
    lines = [take(3) for _ in packs]
    select_ref, angle_ref, top_ref = loaded
    mine, core = lax.axis_index("shard"), lax.axis_index("dp")
    stage_loads = []
    for layer in range(layers):
        for slot, weight in enumerate(weights):
            target = stage[4 * layer + slot]
            rows = target.shape[0]
            source = weight.at[layer, pl.ds(pl.multiple_of(core * rows, rows), rows)]
            number = len(stage_loads)
            stage_loads.append(pltpu.make_async_copy(source, target, stage_sems.at[number]))
    stage_loads[1].start()
    for number, load in enumerate(stage_loads):
        if number != 1:
            load.start()
    loads = start_loads(sources, loaded, load_sems)
    greet(
        ctx_peers(ctx)
        + [{"shard": lax.rem(mine + step, shards)} for step in range(1, shards)]
        + [{"dp": 1 - core}]
    )
    tile_ref[...] = jnp.zeros_like(tile_ref)
    own_width = own_gains_ref.shape[2]
    for layer in range(layers):
        own_gains = own_gains_ref[layer].astype(BF).astype(F32)
        tile_ref[2 * layer : 2 * layer + 2, :own_width] = own_gains
    small = small_gather_steps(ctx, shards, tile_ref, tiles_ref, small_send, small_recv)
    next(small)
    gathers, counts = [], []
    for number, (pack_ref, whole_ref, line) in enumerate(zip(packs, whole_refs, lines)):
        parts = halves(pack_ref.shape[0])
        if number == 0:
            count = ctx * cuts[0].shape[1]
            parts = [(count, pack_ref.shape[0] - count), (0, count)]
        gathers.append(z_gather_steps(shards, parts, number > 0, pack_ref, whole_ref, *line))
        counts.append(len(parts))
    stream = z_stream(shards - 1, gathers, counts)
    there, stored = [0], []

    def serve():
        there[0] = next(stream, there[0])

    def wait_for(number):
        while there[0] <= number:
            serve()

    def store(source, target):
        stored.append(pltpu.make_async_copy(source, target, out_sems.at[len(stored)]))
        stored[-1].start()

    def prepare():
        wait_all(loads)
        finish(gather_steps(ctx, angle_ref, angles_ref, *extra[:2]))
        build_tables(angles_ref, select_ref, tables, bias)
        store(angles_ref, common_out[0])

    def make_packs(numbers):
        return begin_packs(
            ctx,
            numbers,
            pieces,
            stage_loads,
            stage,
            cuts,
            packs,
            (swap_send, swap_recv),
            lambda: next(gathers[0]),
            serve,
        )

    swaps = make_packs(range(2))
    finish(small)
    gains_ref[...] = gain_rows(tiles_ref, own_width)
    store(gains_ref, common_out[2])
    wait_all(swaps)
    serve()
    serve()
    for layer in range(layers):
        new_ref, *kept, next_normed = kept_refs[layer]

        def load_attn(layer=layer):
            wait_for(2 * layer)
            return load_pair(ctx, [whole_refs[2 * layer]], wq, wo, attn_sems)

        def load_mlp(layer=layer):
            wait_for(2 * layer + 1)
            return load_pair(ctx, [whole_refs[2 * layer + 1]], wgu, wd, mlp_sems)

        attn_stage(
            ctx,
            serve,
            load_attn,
            prepare if layer == 0 else lambda: None,
            stream_ref,
            gains_ref[2 * layer : 2 * layer + 1],
            kept,
            new_ref,
            wq,
            wo,
            own,
            part,
            tables,
            bias,
            comm,
        )
        for source, target in zip(kept_refs[layer][:5], kept_out[layer]):
            store(source, target)
        if layer == 0:
            finish(gather_steps(ctx, top_ref, tops_ref, *extra[2:]))
            store(tops_ref, common_out[1])
            if layers > 1:
                wait_all(make_packs(range(2, 2 * layers)))
            serve()
        gain = gains_ref[2 * layer + 1 : 2 * layer + 2]
        if layer < last:
            stream_ref, gu_ref = gate_refs[layer]
            mlp_stage(
                ctx,
                serve,
                load_mlp,
                new_ref,
                gain,
                stream_ref,
                next_normed,
                gu_ref,
                wgu,
                wd,
                own,
                part,
                comm,
            )
            for source, target in zip(gate_refs[layer], gate_out[layer]):
                store(source, target)
        else:
            own[...] = norm_forward(new_ref[...], gain)
            rows = gather_steps(ctx, own, next_normed, *extra[:2])
            next(rows)
            next(rows)
            serve()
            finish(rows)
        store(next_normed, kept_out[layer][5])
    wait_for(len(packs) - 1)
    wait_all(stored)


def attn_backward_kernel(ctx, shards, count, row, ends, firsts, dh_ref, gains_ref, *refs):
    refs = list(refs)

    def take(number):
        taken = refs[:number]
        del refs[:number]
        return taken

    sources = take(10 if ends else 7)
    end_weights = take(ends)
    weights, line_sources = take(count), take(len(firsts))
    new_dh, gain_grad = take(2)
    end_gain_grad, up_ref = take(2) if ends else (None, None)
    line_outs = take(len(firsts))
    outs = take(count)
    made, (made_sems,) = take(count), take(1)
    wq, wo, bias, own, grads, mixed, dproj, part, dy, sems = take(10)
    tables, comm = take(3), take(7)
    loaded, (load_sems,) = take(len(sources)), take(1)
    wgu, wd, end_sems = take(3) if ends else (None, None, None)
    stream_ref, normed_ref, qkv_ref, att_ref, lse_ref, select_ref, angle_ref = loaded[-7:]
    loads = start_loads(sources, loaded, load_sems)
    lines = scatter_lines(ctx, shards, firsts, line_sources, line_outs, refs)

    def serve():
        for line in lines:
            next(line, None)

    serve()
    if ends:
        end_wide, end_deep = load_pair(ctx, end_weights, wgu, wd, end_sems)
    wide, deep = load_pair(ctx, weights, wq, wo, sems)
    serve()
    grad_stream = dh_ref[...].astype(F32)
    if ends:
        dgu, hidden, end_stream = loaded[:3]
        wait_all(loads[:3])
        wait_all(end_wide)
        part[...] = dot(dgu[...], wgu[...], ((1,), (1,))).astype(BF)
        scattered = scatter_steps(ctx, part, None, dy, *comm[2:])
        next(scattered)
        serve()
        wait_all(end_deep)
        up_ref[...] = dot(hidden[...], wd[...]).astype(BF)
        wait_all(loads[3:])
        build_tables(angle_ref, select_ref, tables, bias)
        next(scattered)
        serve()
        finish(scattered)
        dx, end_gain_grad[...] = norm_backward(
            dy[...], gains_ref[row + 1 : row + 2], end_stream[...].astype(F32)
        )
        new_dh[...] = grad_stream + dx
    else:
        new_dh[...] = grad_stream
    own[...] = new_dh[...].astype(BF)
    gathered = gather_steps(ctx, own, grads, *comm[:2])
    next(gathered)
    next(gathered)
    serve()
    if not ends:
        wait_all(loads)
        build_tables(angle_ref, select_ref, tables, bias)
    finish(gathered)
    serve()
    wait_all(deep)
    mixed[...] = dot(grads[...], wo[...], ((1,), (1,))).astype(BF)
    kv_heads = qkv_ref.shape[1] // (4 * HEAD_DIM)
    scale = HEAD_DIM ** (-0.5)
    dq, dk, dv = [], [0.0] * kv_heads, [0.0] * kv_heads
    for head in range(2 * kv_heads):
        group = head // 2
        query, grad = head_of(qkv_ref, head), head_of(mixed, head)
        key = head_of(qkv_ref, 2 * kv_heads + group)
        value = head_of(qkv_ref, 3 * kv_heads + group)
        scores = dot(query, key, ((1,), (1,))) * scale + bias[...]
        probs = jnp.exp(scores - lse_ref[:, head : head + 1])
        dprobs = dot(grad, value, ((1,), (1,)))
        inner = jnp.sum(probs * dprobs, axis=1, keepdims=True)
        dscores = (probs * (dprobs - inner)).astype(BF)
        dq.append(dot(dscores, key) * scale)
        dk[group] = dk[group] + dot(dscores, query, ((0,), (0,))) * scale
        dv[group] = dv[group] + dot(probs.astype(BF), grad, ((0,), (0,)))
    serve()
    dproj[...] = rope(jnp.concatenate(dq + dk + dv, axis=1), tables, back=True).astype(BF)
    wait_all(wide)
    part[...] = dot(dproj[...], wq[...], ((1,), (1,))).astype(BF)
    scattered = scatter_steps(ctx, part, None, dy, *comm[2:])
    next(scattered)
    stored = store_gate_grad(ctx, normed_ref, dproj, made, outs, made_sems)
    copies = next(stored)
    next(scattered)
    copies += next(stored)
    copies.append(store_down_grad(ctx, att_ref, grads, made, outs, made_sems))
    serve()
    finish(scattered)
    dx, gain_grad[...] = norm_backward(
        dy[...], gains_ref[row : row + 1], stream_ref[...].astype(F32)
    )
    new_dh[...] = new_dh[...] + dx
    wait_all(copies)
    for line in lines:
        finish(line)


def gate_backward(gate, up, grad_hidden):
    sig = sigmoid(gate)
    silu = gate * sig
    grad_gate = grad_hidden * up * sig * (1.0 + gate * (1.0 - sig))
    return (silu * up).astype(BF), grad_gate.astype(BF), (grad_hidden * silu).astype(BF)


def mlp_backward_kernel(ctx, shards, count, row, firsts, dh_ref, gains_ref, *refs):
    refs = list(refs)

    def take(number):
        taken = refs[:number]
        del refs[:number]
        return taken

    sources, weights, line_sources = take(5), take(count), take(len(firsts))
    new_dh, gain_grad, sum_out = take(3)
    line_outs = take(len(firsts))
    outs = take(count)
    made, (made_sems,) = take(count), take(1)
    wgu, wd, dgu, hidden, own, grads, part, dy, sems = take(9)
    scratch = take(12)
    loaded, (load_sems,) = take(5), take(1)
    normed_ref, gu_ref, stream_ref, sum_ref, base_ref = loaded
    loads = start_loads(sources, loaded, load_sems)
    lines = scatter_lines(ctx, shards, firsts, line_sources, line_outs, refs)

    def serve():
        for line in lines:
            next(line, None)

    own[...] = dh_ref[...].astype(BF)
    gathered = gather_steps(ctx, own, grads, *scratch[:2])
    summed = scatter_steps(ctx, sum_ref, base_ref, sum_out, *scratch[2:7])
    scattered = scatter_steps(ctx, part, None, dy, *scratch[7:])
    next(gathered)
    serve()
    wide, deep = load_pair(ctx, weights, wgu, wd, sems)
    next(gathered)
    serve()
    wait_all(loads)
    next(summed)
    serve()
    finish(gathered)
    serve()
    wait_all(deep)
    half = gu_ref.shape[1] // 2
    grad_hidden = dot(grads[...], wd[...], ((1,), (1,)))
    hidden[...], dgu[:, :half], dgu[:, half:] = gate_backward(
        gu_ref[:, :half], gu_ref[:, half:], grad_hidden
    )
    next(summed)
    serve()
    wait_all(wide)
    part[...] = dot(dgu[...], wgu[...], ((1,), (1,))).astype(BF)
    next(scattered)
    serve()
    finish(summed)
    stored = store_gate_grad(ctx, normed_ref, dgu, made, outs, made_sems)
    copies = next(stored)
    next(scattered)
    serve()
    copies += next(stored)
    copies.append(store_down_grad(ctx, hidden, grads, made, outs, made_sems))
    serve()
    finish(scattered)
    dx, gain_grad[...] = norm_backward(
        dy[...], gains_ref[row : row + 1], stream_ref[...].astype(F32)
    )
    new_dh[...] = dh_ref[...].astype(F32) + dx
    wait_all(copies)
    for line in lines:
        finish(line)


def mlp_last_kernel(ctx, count, *refs):
    sources, refs = refs[:2], refs[2:]
    weights, outs = refs[:count], refs[count : 2 * count]
    hidden_out, dgu_out, *refs = refs[2 * count :]
    made, (made_sems, hidden, dgu, wgu, wd, sems, *loaded) = refs[:count], refs[count:]
    *loaded, load_sems = loaded
    normed_ref, grad_ref = loaded
    loads = start_loads(sources, loaded, load_sems)
    wide, deep = load_pair(ctx, weights, wgu, wd, sems)
    wait_all(loads + wide + deep)
    half = dgu.shape[1] // 2
    tile = half // 2

    @pl.loop(0, half // tile)
    def _(step):
        start = pl.multiple_of(step * tile, tile)
        one, two = pl.ds(start, tile), pl.ds(pl.multiple_of(half + start, tile), tile)
        gate = dot(normed_ref[...], wgu[:, one])
        up = dot(normed_ref[...], wgu[:, two])
        grad_hidden = dot(grad_ref[...], wd[one, :], ((1,), (1,)))
        hidden[:, one], dgu[:, one], dgu[:, two] = gate_backward(gate, up, grad_hidden)

    copies = start_loads((hidden, dgu), (hidden_out, dgu_out), load_sems)
    for left in store_gate_grad(ctx, normed_ref, dgu, made, outs, made_sems):
        copies += left
    copies.append(store_down_grad(ctx, hidden, grad_ref, made, outs, made_sems))
    wait_all(copies)


def local_call(kernel, out_shape, scratch, flops, hbm, *args):
    bytes_moved = sum(a.size * a.dtype.itemsize for a in args)
    bytes_moved += sum(a.size * a.dtype.itemsize for a in out_shape)
    spaces = [pl.ANY if hbm[0] <= i <= hbm[1] else pltpu.VMEM for i in range(len(args))]
    return pl.pallas_call(
        kernel,
        out_shape=out_shape,
        in_specs=[pl.BlockSpec(memory_space=space) for space in spaces],
        out_specs=[pl.BlockSpec(memory_space=pl.ANY) for _ in out_shape],
        scratch_shapes=scratch,
        cost_estimate=pl.CostEstimate(flops=flops, bytes_accessed=bytes_moved, transcendentals=0),
        compiler_params=pltpu.CompilerParams(vmem_limit_bytes=VMEM_LIMIT),
    )(*args)


def weight_set(packed, width):
    ctx = lax.axis_size("ctx")
    groups, _, columns = packed.shape
    kind, rows = fold(columns, width), width // (ctx * groups)
    if kind != "cut" and rows % 16 == 0:
        return (packed,)
    return spread(packed, width)


def weight_scratch(weights, width):
    ctx = lax.axis_size("ctx")
    columns = weights[0].shape[-1]
    if len(weights) == 2:
        return [pltpu.VMEM(w.shape, BF) for w in weights], pltpu.SemaphoreType.DMA((2,))
    groups, rows, _ = weights[0].shape
    own_rows, parts = below_parts(weights[0].shape, width // groups, width)
    return [
        pltpu.VMEM((width, columns), BF),
        pltpu.VMEM((own_rows * groups, width), BF),
    ], pltpu.SemaphoreType.DMA((groups * (ctx + len(parts)),))


def comm_scratch(ctx, own, width):
    return [
        *pair_of_sems(),
        *scatter_scratch(ctx, own, width),
        *pair_of_sems(),
    ]


def kernel_id(kind, layer):
    return 16 + 8 * layer + kind


def mlp_forward_call(layer, stream, gains, weights):
    ctx = lax.axis_size("ctx")
    own, width = stream.shape
    rows, columns = ctx * own, weights[0].shape[-1]
    scratch, sems = weight_scratch(weights, width)
    return remote_call(
        functools.partial(mlp_forward_kernel, ctx, len(weights), 2 * layer + 1),
        [shape_of((own, width), F32), shape_of((rows, width)), shape_of((rows, columns), F32)],
        [
            *scratch,
            pltpu.VMEM((own, width), BF),
            pltpu.VMEM((rows, width), BF),
            sems,
            *comm_scratch(ctx, own, width),
        ],
        len(weights),
        kernel_id(0, layer),
        stream,
        gains,
        *weights,
    )


def attn_forward_call(layer, stream, gains, weights, tables, top, is_last):
    ctx = lax.axis_size("ctx")
    own, width = stream.shape
    rows, columns = ctx * own, weights[0].shape[-1]
    scratch, sems = weight_scratch(weights, width)
    is_first = top is not None
    loaded = [*tables, top] if is_first else list(tables)
    outs = remote_call(
        functools.partial(
            attn_forward_kernel, ctx, len(weights), 2 * layer, is_first, is_last
        ),
        [
            shape_of((own, width), F32),
            shape_of((rows, width)),
            shape_of((rows, columns)),
            shape_of((rows, columns // 2)),
            shape_of((rows, 128), F32),
            *([shape_of((rows, 128), F32), shape_of((rows, width))] if is_first else []),
            *([shape_of((rows, width))] if is_last else []),
        ],
        [
            *scratch,
            pltpu.VMEM((rows, rows), F32),
            pltpu.VMEM((own, width), BF),
            pltpu.VMEM((rows, width), BF),
            *[pltpu.VMEM((rows, columns), F32)] * 3,
            sems,
            *comm_scratch(ctx, own, width),
            *pair_of_sems(),
            *pair_of_sems(),
            *load_scratch(loaded),
        ],
        len(loaded) + len(weights),
        kernel_id(1, layer),
        stream,
        gains,
        *loaded,
        *weights,
    )
    return outs[0], outs[1:5], outs[5:]


def forward_call(stream, gains, tables, top, weights, pieces):
    ctx, shards, layers = lax.axis_size("ctx"), lax.axis_size("shard"), weights[0].shape[0]
    own, width = stream.shape
    rows = ctx * own
    columns, gate_columns = weights[0].shape[2] // ctx, weights[2].shape[2] // ctx
    stage, cuts, packs = [], [], []
    for _ in range(layers):
        for wide, deep in (weights[:2], weights[2:]):
            wide_rows, wide_columns = wide.shape[1] // 2, wide.shape[2] // ctx
            below = deep.shape[1] // 2 * deep.shape[2] // wide_columns
            stage += [
                pltpu.VMEM((wide_rows, wide.shape[2]), F32),
                pltpu.VMEM((deep.shape[1] // 2, deep.shape[2]), F32),
            ]
            cuts.append(pltpu.VMEM((ctx, wide_rows, wide_columns), BF))
            packs.append((ctx * wide_rows + below, wide_columns))
    wholes = [shape_of((2 * shards,) + pack) for pack in packs]
    attn_scratch, attn_sems = weight_scratch(wholes[:1], width)
    mlp_scratch, mlp_sems = weight_scratch(wholes[1:2], width)
    kept = [
        shape_of((own, width), F32),
        shape_of((rows, width)),
        shape_of((rows, columns)),
        shape_of((rows, columns // 2)),
        shape_of((rows, 128), F32),
        shape_of((rows, width)),
    ]
    gate_kept = [shape_of((own, width), F32), shape_of((rows, gate_columns), F32)]
    tile = (-(-2 * layers // 8) * 8, 128)
    common = [shape_of((rows, 128), F32), shape_of((rows, width)), shape_of((tile[0], width), F32)]
    outs = kept * layers + gate_kept * (layers - 1) + common
    loaded = [*tables, top]
    swaps = 2 * layers * (ctx - 1)
    results = remote_call(
        functools.partial(forward_kernel, ctx, shards, layers, pieces),
        outs + wholes,
        [
            *[pltpu.VMEM(out.shape, out.dtype) for out in outs],
            *attn_scratch,
            *mlp_scratch,
            pltpu.VMEM((rows, rows), F32),
            pltpu.VMEM((own, width), BF),
            pltpu.VMEM((rows, width), BF),
            *[pltpu.VMEM((rows, columns), F32)] * 3,
            attn_sems,
            mlp_sems,
            pltpu.SemaphoreType.DMA((len(outs),)),
            *comm_scratch(ctx, own, width),
            *pair_of_sems(),
            *pair_of_sems(),
            *load_scratch(loaded),
            *stage,
            *cuts,
            *[pltpu.VMEM(pack, BF) for pack in packs],
            pltpu.VMEM(tile, F32),
            pltpu.VMEM((ctx, shards) + tile, F32),
            pltpu.SemaphoreType.DMA((4 * layers,)),
            pltpu.SemaphoreType.DMA((swaps,)),
            pltpu.SemaphoreType.DMA((swaps,)),
            pltpu.SemaphoreType.DMA((ctx + shards + 1,)),
            pltpu.SemaphoreType.DMA((ctx + shards + 1,)),
            *line_sems(shards) * len(packs),
        ],
        len(loaded) + len(weights),
        kernel_id(5, 0),
        stream,
        gains,
        *loaded,
        *weights,
        hbm_out=len(outs) + len(wholes),
    )
    per_layer = [results[6 * layer : 6 * layer + 6] for layer in range(layers)]
    results = results[6 * layers :]
    gates = [results[2 * layer : 2 * layer + 2] for layer in range(layers - 1)]
    return per_layer, gates, results[2 * layers - 2 : 2 * layers + 1], results[2 * layers + 1 :]


def attn_backward_call(
    layer, grad_stream, stream, gains, kept, weights, tables, ends, end_weights, line
):
    ctx, shards = lax.axis_size("ctx"), lax.axis_size("shard")
    own, width = stream.shape
    rows, columns = ctx * own, weights[0].shape[-1]
    scratch, sems = weight_scratch(weights, width)
    line_outs, line_scratch = scatter_sums(line, shards)
    loaded = [*ends, stream, *kept, *tables]
    end_scratch = []
    if ends:
        end_scratch, end_sems = weight_scratch(end_weights, width)
        end_scratch.append(end_sems)
    firsts = [first for _, first, _ in line]
    results = remote_call(
        functools.partial(
            attn_backward_kernel,
            ctx,
            shards,
            len(weights),
            2 * layer,
            len(end_weights),
            firsts,
        ),
        [
            shape_of((own, width), F32),
            shape_of((1, width), F32),
            *([shape_of((1, width), F32), shape_of((rows, width))] if ends else []),
            *line_outs,
            *[shape_of(weight.shape) for weight in weights],
        ],
        [
            *grad_scratch(weights),
            *scratch,
            pltpu.VMEM((rows, rows), F32),
            pltpu.VMEM((own, width), BF),
            pltpu.VMEM((rows, width), BF),
            pltpu.VMEM((rows, columns // 2), BF),
            pltpu.VMEM((rows, columns), BF),
            pltpu.VMEM((rows, width), BF),
            pltpu.VMEM((own, width), F32),
            sems,
            *[pltpu.VMEM((rows, columns), F32)] * 3,
            *comm_scratch(ctx, own, width),
            *load_scratch(loaded),
            *end_scratch,
            *line_scratch,
        ],
        len(loaded) + len(end_weights) + len(weights) + len(line),
        kernel_id(2, layer),
        grad_stream,
        gains,
        *loaded,
        *end_weights,
        *weights,
        *[grads for grads, _, _ in line],
        hbm_out=len(weights),
    )
    results, outs = results[: -len(weights)], results[-len(weights) :]
    new_dh, gain_grad, *more = results
    if ends:
        return packed_grads(outs), new_dh, gain_grad[0], (more[0][0], more[1]), more[2:]
    return packed_grads(outs), new_dh, gain_grad[0], (), more


def packed_grads(outs):
    return outs[0] if len(outs) == 1 else pack_grads(*outs)


def remote_call(kernel, out_shape, scratch, hbm, collective_id, *args, hbm_out=0):
    spaces = [pltpu.VMEM] * (len(args) - hbm) + [pl.ANY] * hbm
    out_spaces = [pltpu.VMEM] * (len(out_shape) - hbm_out) + [pl.ANY] * hbm_out
    return pl.pallas_call(
        kernel,
        out_shape=out_shape,
        in_specs=[pl.BlockSpec(memory_space=space) for space in spaces],
        out_specs=[pl.BlockSpec(memory_space=space) for space in out_spaces],
        scratch_shapes=scratch,
        compiler_params=pltpu.CompilerParams(
            collective_id=collective_id, has_side_effects=True, vmem_limit_bytes=VMEM_LIMIT
        ),
    )(*args)


def load_scratch(args):
    return [
        *[pltpu.VMEM(arg.shape, arg.dtype) for arg in args],
        pltpu.SemaphoreType.DMA((len(args),)),
    ]


def pair_of_sems():
    return [pltpu.SemaphoreType.DMA((8,)), pltpu.SemaphoreType.DMA((8,))]


def mlp_backward_call(
    layer, grad_stream, stream, gains, normed, gate_up, weights, summed, base, line
):
    ctx = lax.axis_size("ctx")
    rows, width = normed.shape
    own = base.shape[0]
    columns = weights[0].shape[-1]
    scratch, sems = weight_scratch(weights, width)
    shards = lax.axis_size("shard")
    line_outs, line_scratch = scatter_sums(line, shards)
    firsts = [first for _, first, _ in line]
    loaded = [normed, gate_up, stream, summed, base]
    results = remote_call(
        functools.partial(
            mlp_backward_kernel, ctx, shards, len(weights), 2 * layer + 1, firsts
        ),
        [
            shape_of((own, width), F32),
            shape_of((1, width), F32),
            shape_of((own, width)),
            *line_outs,
            *[shape_of(weight.shape) for weight in weights],
        ],
        [
            *grad_scratch(weights),
            *scratch,
            pltpu.VMEM((rows, columns), BF),
            pltpu.VMEM((rows, columns // 2), BF),
            pltpu.VMEM((own, width), BF),
            pltpu.VMEM((rows, width), BF),
            pltpu.VMEM((rows, width), BF),
            pltpu.VMEM((own, width), F32),
            sems,
            *pair_of_sems(),
            *scatter_scratch(ctx, own, width),
            *pair_of_sems(),
            *scatter_scratch(ctx, own, width),
            *pair_of_sems(),
            *load_scratch(loaded),
            *line_scratch,
        ],
        len(loaded) + len(weights) + len(line),
        kernel_id(3, layer),
        grad_stream,
        gains,
        *loaded,
        *weights,
        *[grads for grads, _, _ in line],
        hbm_out=len(weights),
    )
    (new_dh, gain_grad, total, *sums), outs = results[: -len(weights)], results[-len(weights) :]
    return packed_grads(outs), new_dh, gain_grad[0], total, sums


def mlp_last_call(normed, weights, grad_mlp):
    rows, width = normed.shape
    columns = weights[0].shape[-1]
    scratch, sems = weight_scratch(weights, width)
    *outs, hidden, grad_gate_up = local_call(
        functools.partial(mlp_last_kernel, lax.axis_size("ctx"), len(weights)),
        [
            *[shape_of(weight.shape) for weight in weights],
            shape_of((rows, columns // 2)),
            shape_of((rows, columns)),
        ],
        [
            *grad_scratch(weights),
            pltpu.VMEM((rows, columns // 2), BF),
            pltpu.VMEM((rows, columns), BF),
            *scratch,
            sems,
            *load_scratch((normed, grad_mlp)),
        ],
        6 * rows * width * columns,
        (0, 1 + len(weights)),
        normed,
        grad_mlp,
        *weights,
    )
    return packed_grads(outs), hidden, grad_gate_up


def adam_kernel(rate, decay, kept, pieces, w_ref, m_ref, v_ref, g_ref, *refs):
    new_w, new_m, new_v = refs[kept:]
    if w_ref.shape[-1] == g_ref.shape[-1]:
        grad = g_ref[...].astype(F32).reshape(w_ref.shape)
    else:
        grad = from_members(g_ref[...].astype(F32), pieces)[None]
    new_w[...], new_m[...], new_v[...] = adam_step(
        w_ref[...], m_ref[...], v_ref[...], grad, rate, decay
    )


def adam_layer(layer, slot, weight, moment, square, grad, done, pieces):
    _, rows, columns = weight.shape
    if len(pieces) == 3:
        members, _, width = grad.shape
        parts = 2 if rows % 16 == 0 else 1
        grid = (1, parts)
        grad_spec = pl.BlockSpec((members, rows // parts, width), lambda i, j: (0, j, 0))
        spec = pl.BlockSpec((1, rows // parts, columns), lambda i, j: (layer, j, 0))
    elif len(pieces) == 2:
        members, _, both = grad.shape
        grid, width = (2, members), both // 2
        grad_spec = pl.BlockSpec((1, rows, width), lambda i, j: (j, 0, i))
        spec = pl.BlockSpec((1, rows, width), lambda i, j: (layer, 0, i * members + j))
    else:
        grid, width = (1, 3), columns // 3
        grad_spec = pl.BlockSpec((rows, width), lambda i, j: (0, j))
        spec = pl.BlockSpec((1, rows, width), lambda i, j: (layer, 0, j))
    kept = [] if done is None else list(done)
    size = rows * columns
    return pl.pallas_call(
        functools.partial(adam_kernel, RATES[slot], DECAYS[slot], len(kept), pieces),
        grid=grid,
        out_shape=[shape_of(weight.shape, F32)] * 3,
        in_specs=[spec, spec, spec, grad_spec] + [pl.BlockSpec(memory_space=pl.ANY)] * len(kept),
        out_specs=[spec] * 3,
        input_output_aliases={4 + i: i for i in range(len(kept))},
        cost_estimate=pl.CostEstimate(
            flops=20 * size, bytes_accessed=26 * size, transcendentals=size
        ),
        compiler_params=pltpu.CompilerParams(vmem_limit_bytes=SMALL_LIMIT),
    )(weight, moment, square, grad, *kept)


def in_order(first, then):
    return lax.optimization_barrier((first, then))


def half_rows(shard):
    half = shard.shape[0] // 2
    return lax.dynamic_slice_in_dim(shard, lax.axis_index("dp") * half, half, axis=0)


def member_parts(shard, pieces, ctx):
    parts = []
    for member in range(ctx):
        cut, start = [], 0
        for width in pieces:
            own = width // ctx
            cut.append(shard[:, start + member * own : start + (member + 1) * own])
            start += width
        parts.append(jnp.concatenate(cut, axis=1))
    return parts


def by_member(shard, pieces):
    return jnp.stack(member_parts(shard, pieces, lax.axis_size("ctx")))


def from_members(parts, pieces):
    ctx = parts.shape[0]
    out, start = [], 0
    for width in pieces:
        out += [parts[i, :, start : start + width // ctx] for i in range(ctx)]
        start += width // ctx
    return jnp.concatenate(out, axis=1)


def fold(columns, width):
    if width % columns == 0:
        return "even"
    return "bent" if columns > width and width % (columns - width) == 0 else "cut"


def pack(wide, rows_part):
    columns, (m, width) = wide.shape[1], rows_part.shape
    kind = fold(columns, width)
    if kind == "bent":
        rest = columns - width
        whole = m * width // columns
        right = [rows_part[whole:, i * rest : (i + 1) * rest] for i in range(width // rest)]
        below = jnp.concatenate([rows_part[:whole], jnp.concatenate(right, axis=0)], axis=1)
        return jnp.concatenate([wide, below], axis=0)
    unit = math.gcd(columns, width)
    below = jnp.concatenate(jnp.split(rows_part, width // unit, axis=1), axis=0)
    below = jnp.concatenate(jnp.split(below, columns // unit, axis=0), axis=1)
    return jnp.concatenate([wide, below], axis=0)


def unpack(packed, count, width):
    columns = packed.shape[-1]
    wide, below = packed[..., :count, :], packed[..., count:, :]
    kind = fold(columns, width)
    if kind == "bent":
        rest = columns - width
        right = jnp.split(below[..., width:], width // rest, axis=-2)
        return wide, jnp.concatenate(
            [below[..., :width], jnp.concatenate(right, axis=-1)], axis=-2
        )
    unit = math.gcd(columns, width)
    below = jnp.concatenate(jnp.split(below, columns // unit, axis=-1), axis=-2)
    return wide, jnp.concatenate(jnp.split(below, width // unit, axis=-2), axis=-1)


def pack_share(member_parts, rows_part):
    ctx, rows, columns = member_parts.shape
    return pack(member_parts.reshape(ctx * rows, columns), rows_part)


def spread(whole, width):
    ctx = lax.axis_size("ctx")
    groups, _, columns = whole.shape
    rows = width // (ctx * groups)
    wide, rows_whole = unpack(whole, ctx * rows, width)
    wide = jnp.transpose(wide.reshape(groups, ctx, rows, columns), (1, 0, 2, 3))
    return wide.reshape(-1, columns), rows_whole.reshape(-1, width)


def pack_grads(wide, rows_part):
    ctx, shards = lax.axis_size("ctx"), lax.axis_size("shard")
    columns, width = wide.shape[1], rows_part.shape[1]
    groups = shards * 2
    rows = wide.shape[0] // (ctx * groups)
    wide = jnp.transpose(wide.astype(BF).reshape(ctx, groups, rows, columns), (1, 0, 2, 3))
    wide = wide.reshape(groups, ctx * rows, columns)
    return jax.vmap(pack)(wide, rows_part.astype(BF).reshape(groups, -1, width))


def reduce_grads(packed):
    return lax.psum_scatter(
        packed.reshape(-1, packed.shape[-1]), ("shard", "dp"), scatter_dimension=0, tiled=True
    )


def share_grads(mine, width, collective_id):
    ctx, groups = lax.axis_size("ctx"), lax.axis_size("shard") * 2
    columns = mine.shape[1]
    rows = width // (ctx * groups)
    deep = (mine.shape[0] - ctx * rows) * columns // width
    sums = (mine,)
    if fold(columns, width) == "cut" or rows % 16:
        wide, rows_part = unpack(mine, ctx * rows, width)
        sums = (wide.reshape(ctx, rows, columns), rows_part)
    wide, rows_part = share_plane(sums, ((rows, columns), (deep, width)), collective_id)
    return wide.reshape(ctx, 2 * rows, columns), rows_part.reshape(-1, width)


def rope_select(ctx):
    half_dim = HEAD_DIM // 2
    columns = (HEADS + 2 * KV_HEADS) * HEAD_DIM // ctx
    turned = (HEADS + KV_HEADS) * HEAD_DIM // ctx
    select = np.zeros((3, 128, columns), np.float32)
    for column in range(columns):
        place = column % HEAD_DIM
        if column >= turned:
            select[0, HEAD_DIM + 1, column] = 1.0
        elif place < half_dim:
            select[0, place, column] = 1.0
            select[1, half_dim + place, column] = -1.0
        else:
            select[0, place - half_dim, column] = 1.0
            select[2, place, column] = 1.0
    return np.concatenate(list(select), axis=1)


def body(
    tokens,
    cotangent,
    positions,
    w_qkv,
    w_out,
    w_gate_up,
    w_down,
    norm_gains,
    first_qkv,
    first_out,
    first_gate_up,
    first_down,
    first_gains,
    second_qkv,
    second_out,
    second_gate_up,
    second_down,
    second_gains,
):
    ctx, shards = lax.axis_size("ctx"), lax.axis_size("shard")
    layer_count, own_width, width = w_qkv.shape[0], norm_gains.shape[2], tokens.shape[2]
    width_q, width_kv = HEADS * HEAD_DIM, KV_HEADS * HEAD_DIM
    qkv_pieces, gate_pieces = (width_q, width_kv, width_kv), (FF, FF)
    rows = tokens.shape[1]
    last = layer_count - 1

    lined = shards == 4 and width // (ctx * shards * 2) % 16 == 0
    attn_sets, mlp_sets = [None] * layer_count, [None] * layer_count
    if not lined:
        tile = norm_gains.astype(BF).astype(F32).reshape(2 * layer_count, own_width)
        tile = jnp.pad(tile, ((0, -2 * layer_count % 8), (0, -own_width % 128)))
        gains = jnp.transpose(small_gather(tile)[..., :own_width], (2, 0, 1, 3))
        gains = gains.reshape(-1, width)
        for layer in range(layer_count):
            parts = by_member(half_rows(w_qkv[layer]).astype(BF), qkv_pieces)
            packed = pack_share(swap_ctx(parts, 2), half_rows(w_out[layer]).astype(BF))
            packed = lax.all_gather(packed, ("shard", "dp"), axis=0)
            attn_sets[layer] = weight_set(packed, width)
            parts = by_member(half_rows(w_gate_up[layer]).astype(BF), gate_pieces)
            packed = pack_share(swap_ctx(parts, 3), half_rows(w_down[layer]).astype(BF))
            packed = lax.all_gather(packed, ("shard", "dp"), axis=0)
            mlp_sets[layer] = weight_set(packed, width)

    angles = rope_angles(positions[0])
    position = positions[0].astype(F32)[:, None]
    angles = jnp.concatenate(
        [jnp.cos(angles), jnp.sin(angles), position, jnp.ones_like(position)], axis=1
    )
    angles = jnp.pad(angles, ((0, 0), (0, 128 - angles.shape[1])))
    select = jnp.asarray(rope_select(ctx))

    stream, grad_stream = tokens[0], cotangent[0]
    saved = []
    if lined:
        per_layer, gates, (angles, grad_top, gains), wholes = forward_call(
            stream,
            norm_gains,
            (select, angles),
            cotangent[0],
            (w_qkv, w_out, w_gate_up, w_down),
            (qkv_pieces, gate_pieces),
        )
        for layer in range(layer_count):
            middle, *kept, normed_two = per_layer[layer]
            saved.append([stream, middle, kept, normed_two])
            attn_sets[layer], mlp_sets[layer] = (wholes[2 * layer],), (wholes[2 * layer + 1],)
            if layer < last:
                stream, gate_up = gates[layer]
                saved[-1].append(gate_up)
    else:
        for layer in range(layer_count):
            middle, kept, more = attn_forward_call(
                layer,
                stream,
                gains,
                attn_sets[layer],
                (select, angles),
                cotangent[0] if layer == 0 else None,
                layer == last,
            )
            saved.append([stream, middle, kept])
            if layer == 0:
                angles, grad_top = more[:2]
            if layer == last:
                saved[-1].append(more[-1])
            else:
                stream, *gate_kept = mlp_forward_call(layer, middle, gains, mlp_sets[layer])
                saved[-1] += gate_kept
    tables = (select, angles)

    params = (w_qkv, w_out, w_gate_up, w_down)
    firsts = (first_qkv, first_out, first_gate_up, first_down)
    seconds = (second_qkv, second_out, second_gate_up, second_down)
    updated = [None] * 4

    def step(layer, slots, grads, pieces):
        for slot, grad, cut in zip(slots, grads, (pieces, ())):
            updated[slot] = adam_layer(
                layer, slot, params[slot], firsts[slot], seconds[slot], grad, updated[slot], cut
            )

    def step_mlp(layer, mine):
        step(layer, (2, 3), share_grads(mine, width, 4), gate_pieces)

    def step_attn(layer, mine):
        step(layer, (0, 1), share_grads(mine, width, 5), qkv_pieces)

    def sum_gains(gain_grads):
        gain_tiles = jnp.stack(gain_grads).reshape(2 * layer_count, ctx, shards, own_width)
        gain_tiles = jnp.transpose(gain_tiles, (2, 1, 0, 3))
        gain_tiles = jnp.pad(
            gain_tiles, ((0, 0), (0, 0), (0, -2 * layer_count % 8), (0, -own_width % 128))
        )
        return small_reduce(gain_tiles)[: 2 * layer_count, :own_width].reshape(norm_gains.shape)

    attn_mine, mlp_mine = [None] * layer_count, [None] * layer_count
    gain_grads = [None] * layer_count
    for layer in reversed(range(layer_count)):
        before, middle, kept, normed_two = saved[layer][:4]
        ends = []
        if layer == last:
            packed, hidden, grad_gate_up = mlp_last_call(normed_two, mlp_sets[layer], grad_top)
            ends = [grad_gate_up, hidden, middle]
        else:
            line = []
            if lined:
                line = [
                    (mlp_mine[layer + 1], cut, mlp_mine[layer + 1].shape[1] - cut),
                    (attn_mine[layer + 1], 0, attn_mine[layer + 1].shape[1]),
                ]
            packed, grad_stream, grad_g2, total, sums = mlp_backward_call(
                layer,
                grad_stream,
                middle,
                gains,
                normed_two,
                saved[layer][4],
                mlp_sets[layer],
                up_part,
                saved[last][1],
                line,
            )
            if lined:
                mlp_mine[layer + 1] = jnp.concatenate([head_sums[0], sums[0]], axis=0)
                attn_mine[layer + 1] = sums[1]
            if layer == last - 1:
                output = total
        line = []
        if lined and layer > 0:
            mlp_mine[layer] = packed
            cut = packed.shape[1] * 8 // 9 // 16 * 16
            line = [(packed, 0, cut)]
        else:
            mlp_mine[layer] = reduce_grads(packed)
        if layer < last and not lined:
            mlp_mine[layer + 1], grad_stream = in_order(mlp_mine[layer + 1], grad_stream)
        packed, grad_stream, grad_g1, more, head_sums = attn_backward_call(
            layer,
            grad_stream,
            before,
            gains,
            kept,
            attn_sets[layer],
            tables,
            ends,
            mlp_sets[layer] if ends else (),
            line,
        )
        if ends:
            grad_g2, up_part = more
        gain_grads[layer] = jnp.stack([grad_g1, grad_g2])
        if layer == 0:
            gain_grad = sum_gains(gain_grads)
        if layer < last:
            packed, mine = in_order(packed, (mlp_mine[layer + 1], attn_mine[layer + 1]))
            step_mlp(layer + 1, mine[0])
            step_attn(layer + 1, mine[1])
            (updated, gain_grad), (mlp_mine[layer], packed) = in_order(
                (updated, gain_grad), (mlp_mine[layer], packed)
            )
        attn_mine[layer] = packed if lined and layer > 0 else reduce_grads(packed)
    step_mlp(0, mlp_mine[0])
    updated, mine = in_order(updated, attn_mine[0])
    step_attn(0, mine)

    updated = list(updated)
    updated.append(
        adam_step(norm_gains, first_gains, second_gains, gain_grad, RATES[4], DECAYS[4])
    )
    return (
        output[None],
        grad_stream[None],
        *[updated[slot][0] for slot in range(5)],
        *[updated[slot][1] for slot in range(5)],
        *[updated[slot][2] for slot in range(5)],
    )


def solution(mesh):
    rows = P(("dp", "shard"), "ctx", None)
    weight = P(None, ("ctx", "shard"), None)
    gain = P(None, None, ("ctx", "shard"))
    group = (weight, weight, weight, weight, gain)
    return jax.shard_map(
        body,
        mesh=mesh,
        in_specs=(rows, rows, P(("dp", "shard"), "ctx"), *group, *group, *group),
        out_specs=(rows, rows, *group, *group, *group),
        check_vma=False,
    )
```
